32 devices in a mesh: batch: 8 (over z, x), task: 4 (over y, core).
Axes of the slice: x: 2, y: 2, z: 4, core: 2. Of those that a mesh axis runs over, the one named last changes fastest.
Arguments:
- images: bfloat16 [16, 512, 4096], P('batch', 'task'), may hold values from -6 to 6
- conv1_weight: bfloat16 [9, 512, 512], P(None, 'task'), may hold values from -0.09375 to 0.09375
- norm1_gain: float32 [512], P('task'), may hold values from 0.5 to 1.5
- norm1_bias: float32 [512], P('task'), may hold values from -3 to 3
- conv2_weight: bfloat16 [9, 512, 512], P(None, 'task'), may hold values from -0.09375 to 0.09375
- norm2_gain: float32 [512], P('task'), may hold values from 0.5 to 1.5
- norm2_bias: float32 [512], P('task'), may hold values from -3 to 3
- head_weight: bfloat16 [512, 40], P(None, 'task'), may hold values from -0.53033009 to 0.53033009, as said below
- head_bias: float32 [40], P('task'), may hold values from -3 to 3
- labels: int32 [16, 40], P('batch', 'task'), may hold values from 0 to 1
- image_counts: int32 [8], replicated, may hold values from 1 to 2, as said below
- average_weights: float32 [40], replicated, may hold values from 0.2 to 1
Outputs:
- pooled: float32 [16, 512], P('batch', 'task')
- input_grad: float32 [16, 512, 4096], P('batch', 'task')
- conv1_grad: float32 [9, 512, 512], P(None, 'task')
- norm1_gain_grad: float32 [512], P('task')
- norm1_bias_grad: float32 [512], P('task')
- conv2_grad: float32 [9, 512, 512], P(None, 'task')
- norm2_gain_grad: float32 [512], P('task')
- norm2_bias_grad: float32 [512], P('task')
- head_weight_grad: float32 [512, 40], P(None, 'task')
- head_bias_grad: float32 [40], P('task')
- task_weights: float32 [40], replicated
- average_next: float32 [40], replicated
The draws below stay inside these ranges and needn't reach their ends.
Inputs may be any that keep to these rules, and one draw needn't show every extreme that they name: `head_weight`: head columns of differing norms. `image_counts`: real images are the first slots of each batch index; some batch index is full in every draw.
All inputs are finite; a program needn't handle non-finite values.
Results may differ from the reference program's by a relative error of at most 0.0036.
Values may be sent and summed in bfloat16 or wider, within the bound.
No kernel may reach another device: no remote copies, remote signals or barrier semaphores. Data moves between devices by JAX's collectives and lax.ppermute only.
A program may use at most 256 MiB of HBM per device.

```python
import math
import jax
import jax.numpy as jnp
from jax import lax

C = 512
TASKS = 40
SIDE = 64
IMG_DEV = 2
FW_STEPS = 20
IMAGES = 16
N_BATCH = 8


def draw_images(key, part):
    key = jax.random.fold_in(key, 11)
    first_key, second_key = jax.random.split(key)
    offsets = jax.random.normal(second_key, (IMAGES, C, 1), jnp.float32)
    noise = jax.random.normal(first_key, (IMAGES, C, SIDE * SIDE), jnp.float32)
    return jnp.clip(0.8 * noise + 0.6 * offsets, -6.0, 6.0).astype(jnp.bfloat16)


def draw_head_weight(key, part):
    key = jax.random.fold_in(key, 23)
    first_key, second_key = jax.random.split(key)
    column_scales = jnp.exp(jax.random.uniform(second_key, (1, TASKS), jnp.float32, -0.7, 0.7))
    base_values = jnp.clip(jax.random.normal(first_key, (C, TASKS), jnp.float32), -6.0, 6.0)
    return (base_values * column_scales * C ** (-0.5)).astype(jnp.bfloat16)


def draw_image_counts(key, part):
    key = jax.random.fold_in(key, 37)
    first_key, second_key = jax.random.split(key)
    drawn_counts = jax.random.randint(first_key, (N_BATCH,), 1, IMG_DEV + 1)
    fullest = jax.random.randint(second_key, (), 0, N_BATCH)
    return jnp.where(jnp.arange(N_BATCH) == fullest, IMG_DEV, drawn_counts).astype(jnp.int32)


def place_ends(values, own_key, least, high):
    longest = values.shape.index(max(values.shape))
    spots = []
    for shift in (0, 1):
        where = [jax.random.randint(jax.random.fold_in(own_key, axis), (), 0, length) for axis, length in enumerate(values.shape)]
        where[longest] = (where[longest] + shift) % values.shape[longest]
        spots.append(tuple(where))
    return values.at[spots[0]].set(least).at[spots[1]].set(high)


def shard_levels(key, shape, shards, least, high):
    def one(axis_at, shards_of):
        steps = jax.random.uniform(jax.random.fold_in(jax.random.fold_in(key, 6), axis_at), (shards_of,), jnp.float32, least / len(shards), high / len(shards))
        return jnp.repeat(jnp.exp(steps), shape[axis_at] // shards_of).reshape((-1,) + (1,) * (len(shape) - axis_at - 1))

    factor_of = one(*shards[0])
    for cut in shards[1:]:
        factor_of = factor_of * one(*cut)
    return factor_of


def normal_values(key, shape, width, bound, cuts=(), kind=jnp.bfloat16):
    values = jax.random.normal(key, shape, jnp.float32) * width
    if len(cuts) > 0:
        values = shard_levels(key, shape, cuts, -0.22, 0.18) * values
    return jnp.clip(values, min=-bound, max=bound).astype(kind)


def setup_inputs(seed: int = 0) -> dict:
    keys = jax.random.split(jax.random.key(seed), 13)
    images = draw_images(jax.random.fold_in(keys[12], 71), 0)
    conv1_weight = normal_values(keys[1], (9, C, C), (9 * C) ** -0.5, 0.09375, ((1, 4),))
    norm1_gain = jnp.clip(1.0 + 0.1 * jax.random.normal(keys[2], (C,), jnp.float32), 0.5, 1.5)
    norm1_bias = normal_values(keys[3], (C,), 0.5, 3.0, ((0, 4),), jnp.float32)
    conv2_weight = normal_values(keys[4], (9, C, C), (9 * C) ** -0.5, 0.09375, ((1, 4),))
    norm2_gain = jnp.clip(1.0 + 0.1 * jax.random.normal(keys[5], (C,), jnp.float32), 0.5, 1.5)
    norm2_bias = normal_values(keys[6], (C,), 0.5, 3.0, ((0, 4),), jnp.float32)
    head_weight = draw_head_weight(jax.random.fold_in(keys[12], 71), 0)
    head_bias = normal_values(keys[8], (TASKS,), 0.5, 3.0, ((0, 4),), jnp.float32)
    labels = place_ends(jax.random.randint(keys[9], (IMAGES, TASKS), 0, 2), jax.random.fold_in(keys[9], 1), 0, 1).astype(jnp.int32)
    image_counts = draw_image_counts(jax.random.fold_in(keys[12], 71), 0)
    average_weights = jnp.clip(jnp.exp(jax.random.uniform(keys[11], (TASKS,), jnp.float32, math.log(0.2), math.log(1.0))), 0.2, 1.0)
    return dict(images=images, conv1_weight=conv1_weight, norm1_gain=norm1_gain, norm1_bias=norm1_bias, conv2_weight=conv2_weight, norm2_gain=norm2_gain, norm2_bias=norm2_bias, head_weight=head_weight, head_bias=head_bias, labels=labels, image_counts=image_counts, average_weights=average_weights)


eps = 1e-05
loss_scale = 4096.0
highest = lax.Precision.HIGHEST

@jax.custom_vjp
def low(v):
    return lax.optimization_barrier(v.astype(jnp.bfloat16)).astype(jnp.float32)

@jax.custom_vjp
def low_back(v):
    return v

def low_keep(v):
    return (low(v), None)

def low_pass(kept, grad):
    return (grad,)

def back_keep(v):
    return (v, None)

def back_low(kept, grad):
    return (low(grad),)
low.defvjp(low_keep, low_pass)
low_back.defvjp(back_keep, back_low)

def edge_masks(image_side):
    column = jnp.arange(image_side * image_side, dtype=jnp.int32) % image_side
    return [((column + shift_by >= 0) & (column + shift_by < image_side)).astype(jnp.float32) for shift_by in (-1, 0, 1)]

def move(values, offset, image_side):
    margin = image_side + 1
    pad_widths = [(0, 0)] * (values.ndim - 1) + [(margin, margin)]
    padded = jnp.pad(values, pad_widths)
    return lax.slice_in_dim(padded, margin + offset, margin + offset + image_side * image_side, axis=values.ndim - 1)

def tap_offset(kernel_tap, image_side):
    return (kernel_tap // 3 - 1) * image_side + (kernel_tap % 3 - 1)

def convolve(activity, weight):
    masks_list = edge_masks(SIDE)
    result = jnp.zeros(activity.shape[:1] + weight.shape[1:2] + activity.shape[2:], activity.dtype)
    for kernel_tap in range(9):
        shifted = move(activity, tap_offset(kernel_tap, SIDE), SIDE) * masks_list[kernel_tap % 3]
        result = result + jnp.einsum('oc,ncp->nop', weight[kernel_tap], shifted, precision=highest)
    return result
checked_convolve = jax.checkpoint(convolve)

def frank_wolfe(gram_matrix, average_weights):
    task_count = gram_matrix.shape[0]
    normalized = gram_matrix / (jnp.trace(gram_matrix) / task_count)
    start_weights = average_weights / jnp.sum(average_weights)

    def advance(loop_index, current):
        slope_values = jnp.dot(normalized, current, precision=highest)
        target = jax.nn.softmax(-task_count * slope_values)
        step_rate = 1.0 / (loop_index + 4.0)
        return (1.0 - step_rate) * current + step_rate * target
    final_weights = lax.fori_loop(0, FW_STEPS, advance, start_weights)
    return (final_weights, 0.9 * start_weights + 0.1 * final_weights)

def reference(images, conv1_weight, norm1_gain, norm1_bias, conv2_weight, norm2_gain, norm2_bias, head_weight, head_bias, labels, image_counts, average_weights):
    slot_index = jnp.arange(IMAGES, dtype=jnp.int32)
    owner_count = image_counts[(slot_index // IMG_DEV).astype(jnp.int32)]
    valid_rows = (slot_index % IMG_DEV < owner_count).astype(jnp.float32)
    image_total = jnp.sum(image_counts).astype(jnp.float32)
    pixel_total = image_total * (SIDE * SIDE)
    row_weights = valid_rows[:, None, None]

    def normalize(conv_out, norm_gain, norm_bias):
        mean_value = lax.optimization_barrier(jnp.sum(conv_out * row_weights, axis=(0, 2))) / pixel_total
        centered = conv_out - mean_value[None, :, None]
        spread = lax.optimization_barrier(jnp.sum(centered * centered * row_weights, axis=(0, 2))) / pixel_total
        return centered * lax.rsqrt(spread + eps)[None, :, None] * norm_gain[None, :, None] + norm_bias[None, :, None]

    def block(inputs, first_weight, first_gain, first_bias, second_weight, second_gain, second_bias):
        first_out = low_back(checked_convolve(inputs, first_weight))
        activity = low(jax.nn.silu(normalize(first_out, first_gain, first_bias)))
        second_out = low_back(checked_convolve(activity, second_weight))
        summed = normalize(second_out, second_gain, second_bias) + inputs
        return lax.optimization_barrier(jnp.mean(jax.nn.silu(summed), axis=2)) * valid_rows[:, None]
    targets = labels.astype(jnp.float32)

    def task_losses(pooled_in, head_in, bias_in):
        logits = jnp.dot(pooled_in, head_in, precision=highest) + bias_in[None, :]
        terms = jax.nn.softplus(logits) - targets * logits
        return lax.optimization_barrier(jnp.sum(terms * valid_rows[:, None], axis=0)) / image_total
    head_float = head_weight.astype(jnp.float32)
    pooled, block_back = jax.vjp(block, images.astype(jnp.float32), conv1_weight.astype(jnp.float32), norm1_gain, norm1_bias, conv2_weight.astype(jnp.float32), norm2_gain, norm2_bias)
    losses, head_back = jax.vjp(task_losses, pooled, head_float, head_bias)
    unit_rows = jnp.eye(TASKS, dtype=losses.dtype)
    task_grads = jax.vmap(lambda unit_vector: head_back(unit_vector)[0])(unit_rows)
    gram_matrix = jnp.einsum('tnc,snc->ts', task_grads, task_grads, precision=highest)
    task_weights, average_next = frank_wolfe(gram_matrix, average_weights)
    pooled_grad, head_weight_grad, head_bias_grad = head_back(loss_scale * TASKS * task_weights)
    grads = block_back(pooled_grad)
    return (pooled, grads[0], grads[1], grads[2], grads[3], grads[4], grads[5], grads[6], head_weight_grad, head_bias_grad, task_weights, average_next)
```

```python
import functools

import jax
import jax.numpy as jnp
from jax import lax
from jax.experimental import pallas as pl
from jax.experimental.pallas import tpu as pltpu
from jax.sharding import PartitionSpec as P

SIDE = 64
FW_STEPS = 20
LANES = 128
ROWS = 8

eps = 1e-05
loss_scale = 4096.0
highest = lax.Precision.HIGHEST
f32 = jnp.float32
bf16 = jnp.bfloat16


def params(mib, **more):
    return pltpu.CompilerParams(vmem_limit_bytes=mib << 20, **more)


def cost(flops, moved):
    return pl.CostEstimate(flops=flops, bytes_accessed=moved, transcendentals=0)


VM = pl.BlockSpec(memory_space=pltpu.VMEM)
SM = pl.BlockSpec(memory_space=pltpu.SMEM)


def sigmoid(v):
    return 1.0 / (1.0 + jnp.exp(-v))


def silu_slope(v):
    s = sigmoid(v)
    return s * (1.0 + v * (1.0 - s))


def half(h):
    return slice(h * LANES, (h + 1) * LANES)


def fill_shifted(dst, src, col0, rows):
    width = src.shape[1]
    cols = slice(col0, col0 + width)
    block = 512
    zero = jnp.zeros((3, SIDE, width), bf16)
    dst[:, 0:SIDE, cols] = zero
    dst[:, SIDE + rows : SIDE + rows + SIDE, cols] = zero

    def step(i, carry):
        at = pl.multiple_of(i * block, block)
        low = src[pl.ds(at, block), :]
        to = pl.ds(pl.multiple_of(at + SIDE, SIDE), block)
        dst[1, to, cols] = low
        value = low.astype(f32)
        column = lax.broadcasted_iota(jnp.int32, (block, width), 0) & (SIDE - 1)
        dst[0, to, cols] = jnp.where(column == 0, 0.0, pltpu.roll(value, 1, 0)).astype(bf16)
        dst[2, to, cols] = jnp.where(column == SIDE - 1, 0.0, pltpu.roll(value, block - 1, 0)).astype(bf16)
        return carry

    lax.fori_loop(0, rows // block, step, 0)


def send_rows(out, rows):
    n = out.shape[0]
    out[...] = jnp.zeros(out.shape, f32)
    for at, value in rows:
        out[:, at : at + 1, :] = jnp.broadcast_to(value[None], (n, 1, LANES))


def weighted(got, weight, row):
    return jnp.sum(got[:, row, :] * weight, axis=0, keepdims=True)


def norm_coefs(got, weight_ref, h, rows):
    weight = weight_ref[...]
    count = jnp.sum(weight, axis=0, keepdims=True)
    means = got[:, h, :]
    mean = jnp.sum(means * weight, axis=0, keepdims=True) / count
    away = means - mean
    squares = jnp.sum((got[:, 2 + h, :] + rows * (away * away)) * weight, axis=0, keepdims=True)
    return mean, lax.rsqrt(squares / (count * rows) + eps)


def conv_kernel(n_parts, *refs):
    xs, w, out, stats, scratch = refs[:n_parts], *refs[n_parts:]
    rows, width = out.shape
    chunk = 1024
    for i in range(n_parts):
        fill_shifted(scratch, xs[i], i * width, rows)

    def step(j, total):
        at = pl.multiple_of(j * chunk, chunk)
        acc = None
        for k in range(9):
            dy, dx = k // 3 - 1, k % 3 - 1
            lhs = scratch[dx + 1, pl.ds(pl.multiple_of(at + SIDE * (dy + 1), SIDE), chunk), :]
            term = lax.dot_general(lhs, w[k], (((1,), (1,)), ((), ())), preferred_element_type=f32)
            acc = term if acc is None else acc + term
        out[pl.ds(at, chunk), :] = acc
        return total + jnp.sum(acc, axis=0, keepdims=True)

    total = lax.fori_loop(0, rows // chunk, step, jnp.zeros((1, width), f32))
    mean = total / rows

    def spread(j, acc):
        away = out[pl.ds(pl.multiple_of(j * chunk, chunk), chunk), :] - mean
        return acc + jnp.sum(away * away, axis=0, keepdims=True)

    squares = lax.fori_loop(0, rows // chunk, spread, jnp.zeros((1, width), f32))
    send_rows(
        stats,
        [(h, mean[:, half(h)]) for h in range(width // LANES)]
        + [(2 + h, squares[:, half(h)]) for h in range(width // LANES)],
    )


def conv_stats(x_parts, w, n_devices):
    rows, width = x_parts[0].shape
    n = len(x_parts)
    return pl.pallas_call(
        functools.partial(conv_kernel, n),
        in_specs=[VM] * (n + 1),
        out_specs=(VM, VM),
        out_shape=(
            jax.ShapeDtypeStruct((rows, width), f32),
            jax.ShapeDtypeStruct((n_devices, ROWS, LANES), f32),
        ),
        scratch_shapes=[pltpu.VMEM((3, rows + 2 * SIDE, n * width), bf16)],
        compiler_params=params(40),
        cost_estimate=cost(2 * 9 * rows * width * width * n, 16 << 20),
        name="conv_stats",
    )(*x_parts, w)


def act_kernel(c, got, weight, vecs, out, coefs):
    rows = loss_scale
    for h in range(c.shape[1] // LANES):
        mean, scale = norm_coefs(got, weight, h, rows)
        coefs[h : h + 1, :] = mean
        coefs[2 + h : 3 + h, :] = scale
        normed = (c[:, half(h)] - mean) * scale * vecs[h : h + 1, :] + vecs[2 + h : 3 + h, :]
        out[:, half(h)] = (normed * sigmoid(normed)).astype(bf16)


def blocked(block, width):
    return pl.BlockSpec((block, width), lambda i: (i, 0))


def whole(shape):
    return pl.BlockSpec(shape, lambda i: (0,) * len(shape))


def activate(c, got, weight, vecs):
    rows, width = c.shape
    block = 512
    return pl.pallas_call(
        act_kernel,
        grid=(rows // block,),
        in_specs=[blocked(block, width), whole(got.shape), whole(weight.shape), whole(vecs.shape)],
        out_specs=(blocked(block, width), whole((ROWS, LANES))),
        out_shape=(
            jax.ShapeDtypeStruct((rows, width), bf16),
            jax.ShapeDtypeStruct((ROWS, LANES), f32),
        ),
        compiler_params=params(16),
        cost_estimate=cost(20 * rows * width, 6 * rows * width),
        name="activate",
    )(c, got, weight, vecs)


def pool_kernel(meta, c, x, got, weight, vecs, labels, out, coefs, sums):
    step, last = pl.program_id(0), pl.num_programs(0) - 1
    halves = c.shape[1] // LANES

    @pl.when(step == 0)
    def _():
        sums[...] = jnp.zeros_like(sums)

    for h in range(halves):
        mean, scale = norm_coefs(got, weight, h, loss_scale)
        coefs[h : h + 1, :] = mean
        coefs[2 + h : 3 + h, :] = scale
        hat = (c[:, half(h)] - mean) * scale
        v = hat * vecs[4 + h : 5 + h, :] + vecs[6 + h : 7 + h, :] + x[:, half(h)].astype(f32)
        s = sigmoid(v)
        slope = s * (1.0 + v * (1.0 - s))
        sums[h : h + 1, :] += jnp.sum(v * s, axis=0, keepdims=True)
        sums[2 + h : 3 + h, :] += jnp.sum(slope * hat, axis=0, keepdims=True)
        sums[4 + h : 5 + h, :] += jnp.sum(slope, axis=0, keepdims=True)

    @pl.when(step == last)
    def _():
        valid = meta[3].astype(f32)
        rows = []
        for h in range(halves):
            rows.append((h, sums[h : h + 1, :] * (valid / loss_scale)))
            rows.append((2 + h, sums[2 + h : 3 + h, :]))
            rows.append((4 + h, sums[4 + h : 5 + h, :]))
        rows.append((6, labels[0:1, :]))
        rows.append((7, labels[1:2, :]))
        send_rows(out, rows)


def pool(meta, c, x, got, weight, vecs, labels):
    rows, width = c.shape
    block = 512
    return pl.pallas_call(
        pool_kernel,
        grid=(rows // block,),
        in_specs=[
            SM,
            blocked(block, width),
            blocked(block, width),
            whole(got.shape),
            whole(weight.shape),
            whole(vecs.shape),
            whole(labels.shape),
        ],
        out_specs=(whole(got.shape), whole((ROWS, LANES))),
        out_shape=(
            jax.ShapeDtypeStruct(got.shape, f32),
            jax.ShapeDtypeStruct((ROWS, LANES), f32),
        ),
        scratch_shapes=[pltpu.VMEM((ROWS, LANES), f32)],
        compiler_params=params(16),
        cost_estimate=cost(30 * rows * width, 6 * rows * width),
        name="pool",
    )(meta, c, x, got, weight, vecs, labels)


def head_kernel(n_parts, meta, got, ht, bias, valid, avg_row, avg_col, coefs, tw, an, hwg, hbg, pooled_own, pooled, slopes, shifts, labels, grads, mine_all, pooled_part):
    tasks, channels = ht.shape
    images = valid.shape[0]
    n_task = 2 * n_parts
    width = channels // n_parts
    halves = width // LANES
    r = meta[2]
    for n in range(images):
        base = (n // 2) * n_task + (n % 2) * n_parts
        for part in range(n_parts):
            for h in range(halves):
                lo = part * width + h * LANES
                pooled[n : n + 1, lo : lo + LANES] = got[base + part, h : h + 1, :]
        for h in range(halves):
            slopes[n : n + 1, half(h)] = got[base + r, 2 + h : 3 + h, :]
            shifts[n : n + 1, half(h)] = got[base + r, 4 + h : 5 + h, :]
        row = 6 + n % 2
        lab = got[(n // 2) * n_task, row : row + 1, :]
        for t in range(1, n_task):
            lab = lab + got[(n // 2) * n_task + t, row : row + 1, :]
        labels[n : n + 1, :] = lab
    pooled_all = pooled[...]
    table = ht[...]
    both_last = (((1,), (1,)), ((), ()))
    both_first = (((0,), (0,)), ((), ()))
    logits = lax.dot_general(pooled_all, table, both_last, precision=highest, preferred_element_type=f32) + bias[...]
    count = jnp.sum(valid[...], axis=0, keepdims=True)
    errors = valid[...] * (sigmoid(logits) - labels[:, 0:tasks]) / count
    gram = lax.dot_general(errors, errors, both_first, precision=highest, preferred_element_type=f32) * lax.dot_general(
        table, table, both_last, precision=highest, preferred_element_type=f32
    )
    row_id = lax.broadcasted_iota(jnp.int32, (tasks, tasks), 0)
    col_id = lax.broadcasted_iota(jnp.int32, (tasks, tasks), 1)
    trace = jnp.sum(jnp.sum(jnp.where(row_id == col_id, gram, 0.0), axis=1, keepdims=True), axis=0, keepdims=True)
    normalized = gram / (trace / tasks)
    start_row = avg_row[...] / jnp.sum(avg_row[...], axis=1, keepdims=True)
    start_col = avg_col[...] / jnp.sum(avg_col[...], axis=0, keepdims=True)
    w_row, w_col = start_row, start_col
    for j in range(FW_STEPS):
        rate = 1.0 / (j + 4.0)
        z_col = -tasks * jnp.sum(normalized * w_row, axis=1, keepdims=True)
        z_row = -tasks * jnp.sum(normalized * w_col, axis=0, keepdims=True)
        e_col = jnp.exp(z_col - jnp.max(z_col, axis=0, keepdims=True))
        e_row = jnp.exp(z_row - jnp.max(z_row, axis=1, keepdims=True))
        w_col = (1.0 - rate) * w_col + rate * (e_col / jnp.sum(e_col, axis=0, keepdims=True))
        w_row = (1.0 - rate) * w_row + rate * (e_row / jnp.sum(e_row, axis=1, keepdims=True))
    tw[...] = w_row
    an[...] = 0.9 * start_row + 0.1 * w_row
    logit_grads = errors * ((loss_scale * tasks) * w_row)
    hbg[...] = jnp.sum(logit_grads, axis=0, keepdims=True)
    hwg[...] = lax.dot_general(logit_grads, pooled_all, both_first, precision=highest, preferred_element_type=f32)
    grads[...] = jnp.dot(logit_grads, table, precision=highest, preferred_element_type=f32) / loss_scale
    own = pl.ds(pl.multiple_of(r * width, LANES), width)
    q = grads[:, own]
    mine_all[...] = q
    pooled_part[...] = pooled[:, own]
    gain = jnp.sum(q * slopes[...], axis=0, keepdims=True)
    shift = jnp.sum(q * shifts[...], axis=0, keepdims=True)
    mine = mine_all[pl.ds(2 * meta[0] + meta[1], 1), :]
    coefs[...] = jnp.zeros(coefs.shape, f32)
    for h in range(halves):
        coefs[h : h + 1, :] = gain[:, half(h)]
        coefs[2 + h : 3 + h, :] = shift[:, half(h)]
        coefs[4 + h : 5 + h, :] = mine[:, half(h)]
    for i in range(2):
        pooled_own[i : i + 1, :] = pooled_part[pl.ds(2 * meta[0] + i, 1), :]


def head(meta, got, ht, bias, valid, avg_row, avg_col, n_parts):
    tasks, channels = ht.shape
    images = valid.shape[0]
    width = channels // n_parts
    shapes = [(ROWS, LANES), (1, tasks), (1, tasks), (tasks, channels), (1, tasks), (2, width)]
    return pl.pallas_call(
        functools.partial(head_kernel, n_parts),
        in_specs=[SM] + [VM] * 6,
        out_specs=tuple(VM for _ in shapes),
        out_shape=tuple(jax.ShapeDtypeStruct(s, f32) for s in shapes),
        scratch_shapes=[
            pltpu.VMEM((images, channels), f32),
            pltpu.VMEM((images, width), f32),
            pltpu.VMEM((images, width), f32),
            pltpu.VMEM((images, LANES), f32),
            pltpu.VMEM((images, channels), f32),
            pltpu.VMEM((images, width), f32),
            pltpu.VMEM((images, width), f32),
        ],
        compiler_params=params(16),
        cost_estimate=cost(1 << 20, 1 << 20),
        name="head",
    )(meta, got, ht, bias, valid, avg_row, avg_col)


def grad_two_kernel(meta, c, x, coefs, vecs, heads, pixels, low, summed):
    valid = meta[3].astype(f32)
    for h in range(c.shape[1] // LANES):
        mean, scale = coefs[h : h + 1, :], coefs[2 + h : 3 + h, :]
        gain = vecs[4 + h : 5 + h, :]
        hat = (c[:, half(h)] - mean) * scale
        v = hat * gain + vecs[6 + h : 7 + h, :] + x[:, half(h)].astype(f32)
        dn = (valid * heads[4 + h : 5 + h, :]) * silu_slope(v)
        summed[:, half(h)] = dn
        away = (heads[2 + h : 3 + h, :] + hat * heads[h : h + 1, :]) / pixels[0]
        low[:, half(h)] = ((valid * gain * scale) * (dn - away)).astype(bf16)


def grad_two(meta, c, x, coefs, vecs, heads, pixels):
    rows, width = c.shape
    block = 512
    return pl.pallas_call(
        grad_two_kernel,
        grid=(rows // block,),
        in_specs=[
            SM,
            blocked(block, width),
            blocked(block, width),
            whole(coefs.shape),
            whole(vecs.shape),
            whole(heads.shape),
            SM,
        ],
        out_specs=(blocked(block, width), blocked(block, width)),
        out_shape=(
            jax.ShapeDtypeStruct((rows, width), bf16),
            jax.ShapeDtypeStruct((rows, width), f32),
        ),
        compiler_params=params(16),
        cost_estimate=cost(30 * rows * width, 12 * rows * width),
        name="grad_two",
    )(meta, c, x, coefs, vecs, heads, pixels)


def grad_one_kernel(meta, c, dn, got, weight, coefs, vecs, pixels, low, sums):
    valid = meta[3].astype(f32)
    for h in range(c.shape[1] // LANES):
        gain_grad = weighted(got, weight[...], h)
        bias_grad = weighted(got, weight[...], 2 + h)
        sums[h : h + 1, :] = gain_grad
        sums[2 + h : 3 + h, :] = bias_grad
        mean, scale = coefs[h : h + 1, :], coefs[2 + h : 3 + h, :]
        hat = (c[:, half(h)] - mean) * scale
        away = (bias_grad + hat * gain_grad) / pixels[0]
        low[:, half(h)] = ((valid * vecs[h : h + 1, :] * scale) * (dn[:, half(h)] - away)).astype(bf16)


def grad_one(meta, c, dn, got, weight, coefs, vecs, pixels):
    rows, width = c.shape
    block = 512
    return pl.pallas_call(
        grad_one_kernel,
        grid=(rows // block,),
        in_specs=[
            SM,
            blocked(block, width),
            blocked(block, width),
            whole(got.shape),
            whole(weight.shape),
            whole(coefs.shape),
            whole(vecs.shape),
            SM,
        ],
        out_specs=(blocked(block, width), whole((ROWS, LANES))),
        out_shape=(
            jax.ShapeDtypeStruct((rows, width), bf16),
            jax.ShapeDtypeStruct((ROWS, LANES), f32),
        ),
        compiler_params=params(16),
        cost_estimate=cost(10 * rows * width, 10 * rows * width),
        name="grad_one",
    )(meta, c, dn, got, weight, coefs, vecs, pixels)


def back_products(scratch, w, at, chunk):
    acc = None
    for k in range(9):
        dy, dx = k // 3 - 1, k % 3 - 1
        lhs = scratch[1 - dx, pl.ds(pl.multiple_of(at + SIDE * (1 - dy), SIDE), chunk), :]
        term = jnp.dot(lhs, w[k], preferred_element_type=f32)
        acc = term if acc is None else acc + term
    return acc


def back_two_kernel(n_parts, *refs):
    meta, gs = refs[0], refs[1 : 1 + n_parts]
    w, c, coefs, vecs, out, stats, scratch = refs[1 + n_parts :]
    rows, width = out.shape
    halves = width // LANES
    chunk = 1024
    for i in range(n_parts):
        fill_shifted(scratch, gs[i], i * width, rows)

    def step(j, carry):
        at = pl.multiple_of(j * chunk, chunk)
        acc = back_products(scratch, w, at, chunk)
        sums = []
        for h in range(halves):
            hat = (c[pl.ds(at, chunk), half(h)] - coefs[h : h + 1, :]) * coefs[2 + h : 3 + h, :]
            dn = acc[:, half(h)] * silu_slope(hat * vecs[h : h + 1, :] + vecs[2 + h : 3 + h, :])
            out[pl.ds(at, chunk), half(h)] = dn
            sums.append(carry[2 * h] + jnp.sum(dn * hat, axis=0, keepdims=True))
            sums.append(carry[2 * h + 1] + jnp.sum(dn, axis=0, keepdims=True))
        return tuple(sums)

    zero = jnp.zeros((1, LANES), f32)
    sums = lax.fori_loop(0, rows // chunk, step, (zero,) * (2 * halves))
    send_rows(stats, [(2 * i + h, sums[2 * h + i]) for h in range(halves) for i in range(2)])


def back_two(meta, g_parts, w, c, coefs, vecs, n_devices):
    rows, width = c.shape
    n = len(g_parts)
    return pl.pallas_call(
        functools.partial(back_two_kernel, n),
        in_specs=[SM] + [VM] * (n + 4),
        out_specs=(VM, VM),
        out_shape=(
            jax.ShapeDtypeStruct((rows, width), f32),
            jax.ShapeDtypeStruct((n_devices, ROWS, LANES), f32),
        ),
        scratch_shapes=[pltpu.VMEM((3, rows + 2 * SIDE, n * width), bf16)],
        compiler_params=params(44),
        cost_estimate=cost(2 * 9 * rows * width * width * n, 16 << 20),
        name="back_two",
    )(meta, *g_parts, w, c, coefs, vecs)


def back_one_kernel(n_parts, *refs):
    meta, gs = refs[0], refs[1 : 1 + n_parts]
    w, summed, keep, send, scratch = refs[1 + n_parts :]
    rows, width = summed.shape
    cs = width // 2
    chunk = 1024
    first = meta[1] == 0
    for i in range(n_parts):
        fill_shifted(scratch, gs[i], i * width, rows)

    def step(j, carry):
        at = pl.multiple_of(j * chunk, chunk)
        acc = back_products(scratch, w, at, chunk) + summed[pl.ds(at, chunk), :]
        a, b = acc[:, :cs], acc[:, cs:]
        keep[:, pl.ds(at, chunk)] = jnp.where(first, a, b).T
        send[:, pl.ds(at, chunk)] = jnp.where(first, b, a).T.astype(bf16)
        return carry

    lax.fori_loop(0, rows // chunk, step, 0)


def back_one(meta, g_parts, w, summed):
    rows, width = summed.shape
    n = len(g_parts)
    return pl.pallas_call(
        functools.partial(back_one_kernel, n),
        in_specs=[SM] + [VM] * (n + 2),
        out_specs=(VM, VM),
        out_shape=(
            jax.ShapeDtypeStruct((width // 2, rows), f32),
            jax.ShapeDtypeStruct((width // 2, rows), bf16),
        ),
        scratch_shapes=[pltpu.VMEM((3, rows + 2 * SIDE, n * width), bf16)],
        compiler_params=params(40),
        cost_estimate=cost(2 * 9 * rows * width * width * n, 16 << 20),
        name="back_one",
    )(meta, *g_parts, w, summed)


def weight_kernel(n_parts, *refs):
    meta, g, xs = refs[0], refs[1], refs[2 : 2 + n_parts]
    keep, send, scratch = refs[2 + n_parts :]
    rows, width = g.shape
    cs = width // 2
    first = meta[1] == 0
    fill_shifted(scratch, g, 0, rows)
    for k in range(9):
        dy, dx = k // 3 - 1, k % 3 - 1
        lo = SIDE * (1 - dy)
        lhs = scratch[1 - dx, lo : lo + rows, :]
        for i in range(n_parts):
            term = lax.dot_general(lhs, xs[i][...], (((0,), (0,)), ((), ())), preferred_element_type=f32)
            a, b = term[:cs], term[cs:]
            cols = slice(i * width, (i + 1) * width)
            keep[k, :, cols] = jnp.where(first, a, b)
            send[k, :, cols] = jnp.where(first, b, a).astype(bf16)


def weight_grad(meta, g, x_parts):
    rows, width = g.shape
    n = len(x_parts)
    shape = (9, width // 2, n * width)
    return pl.pallas_call(
        functools.partial(weight_kernel, n),
        in_specs=[SM] + [VM] * (n + 1),
        out_specs=(VM, VM),
        out_shape=(jax.ShapeDtypeStruct(shape, f32), jax.ShapeDtypeStruct(shape, bf16)),
        scratch_shapes=[pltpu.VMEM((3, rows + 2 * SIDE, width), bf16)],
        compiler_params=params(32),
        cost_estimate=cost(2 * 9 * rows * width * width * n, 16 << 20),
        name="weight_grad",
    )(meta, g, *x_parts)


def swap(values, axis, by):
    n = lax.axis_size(axis)
    return lax.ppermute(values, axis, [(i, i ^ by) for i in range(n)])


def xor_order(values, axis, r, n):
    bit = 1
    while bit < n:
        shape = values.shape
        split = values.reshape(shape[:axis] + (n // (2 * bit), 2, bit) + shape[axis + 1 :])
        values = jnp.where((r & bit) != 0, jnp.flip(split, axis + 1), split).reshape(shape)
        bit *= 2
    return values


def ordered(first, own, other, axis):
    return jnp.concatenate([jnp.where(first, own, other), jnp.where(first, other, own)], axis=axis)


def on_device(
    images,
    conv1_weight,
    norm1_gain,
    norm1_bias,
    conv2_weight,
    norm2_gain,
    norm2_bias,
    head_weight,
    head_bias,
    labels,
    image_counts,
    average_weights,
):
    n_task, n_batch = lax.axis_size("task"), lax.axis_size("batch")
    t, b = lax.axis_index("task"), lax.axis_index("batch")
    slots, cs, pixels = images.shape
    n_parts = n_task // slots
    g, r = t // n_parts, t % n_parts
    first = g == 0
    width = slots * cs
    channels = n_task * cs
    n_devices = n_task * n_batch
    tasks_here = head_weight.shape[1]
    tasks = tasks_here * n_task

    valid_images = (jnp.arange(slots)[None, :] < image_counts[:, None]).astype(f32)
    image_total = jnp.sum(image_counts).astype(f32)
    pixel_total = (image_total * pixels).reshape(1)
    own_valid = (g < lax.dynamic_index_in_dim(image_counts, b, keepdims=False)).astype(jnp.int32)
    meta = jnp.stack([b, g, r, own_valid]).astype(jnp.int32)
    same = (jnp.arange(n_parts) == r).astype(f32)
    weight = (valid_images[:, :, None] * same[None, None, :]).reshape(n_devices, 1)
    weight = jnp.broadcast_to(weight, (n_devices, LANES))

    def part_weights(w):
        full = ordered(first, w, swap(w, "task", n_parts), 1)
        full = full.reshape(9, width, slots, n_parts, cs).swapaxes(2, 3)
        return xor_order(full, 2, r, n_parts).reshape(9, width, channels)

    def back_weights(w):
        blocks = [w[:, :, i * width : (i + 1) * width] for i in range(n_parts)]
        return jnp.concatenate([blocks[0]] + [swap(blocks[i], "task", i) for i in range(1, n_parts)], axis=1)

    def all_parts(v):
        return [v] + [swap(v, "task", i) for i in range(1, n_parts)]

    w1 = part_weights(conv1_weight)
    pixel_major = jnp.swapaxes(images, 1, 2)
    own_image = jnp.where(first, pixel_major[0], pixel_major[1])
    other_image = jnp.where(first, pixel_major[1], pixel_major[0])
    x_own = ordered(first, own_image, swap(other_image, "task", n_parts), 1)
    x_parts = all_parts(x_own)
    w2 = part_weights(conv2_weight)

    lines = jnp.concatenate([norm1_gain, norm1_bias, norm2_gain, norm2_bias, head_bias])
    lines = jnp.pad(lines, (0, -lines.shape[0] % channels)).reshape(-1, channels)
    mine = jnp.concatenate([head_weight.T.astype(f32), lines])
    mine = jnp.pad(mine, ((0, -mine.shape[0] % ROWS), (0, 0)))
    gathered = lax.all_gather(mine, "task", axis=0)
    table = gathered[:, :tasks_here].reshape(tasks, slots, n_parts, cs)
    table = table.swapaxes(1, 2).reshape(tasks, channels)
    flat = gathered[:, tasks_here : tasks_here + lines.shape[0]].reshape(n_task, -1)
    bias_row = flat[:, 4 * cs : 4 * cs + tasks_here].reshape(1, tasks)
    vecs = flat[:, : 4 * cs].reshape(slots, n_parts, 4, cs)
    vecs = lax.dynamic_index_in_dim(vecs, r, axis=1, keepdims=False).swapaxes(0, 1).reshape(4, width)
    vecs = jnp.pad(vecs, ((0, 0), (0, 2 * LANES - width))).reshape(ROWS, LANES)
    label_rows = lax.dynamic_update_slice(
        jnp.zeros((slots, LANES), f32), labels.astype(f32), (0, t * tasks_here)
    )

    def exchange(rows):
        flat_rows = rows.reshape(n_devices * ROWS, LANES)
        return lax.all_to_all(flat_rows, ("batch", "task"), 0, 0, tiled=True).reshape(rows.shape)

    c1, stats = conv_stats(x_parts, w1, n_devices)
    a_own, coefs1 = activate(c1, exchange(stats), weight, vecs)
    a_parts = all_parts(a_own)
    c2, stats = conv_stats(a_parts, w2, n_devices)
    stats2 = exchange(stats)
    sums, coefs2 = pool(meta, c2, x_own, stats2, weight, vecs, label_rows)
    heads, task_weights, average_next, head_grad, bias_grad, pooled_rows = head(
        meta,
        exchange(sums),
        table,
        bias_row,
        valid_images.reshape(-1, 1),
        average_weights.reshape(1, -1),
        average_weights.reshape(-1, 1),
        n_parts,
    )

    def settle(keep, send):
        total = lax.psum(keep + swap(send, "task", n_parts).astype(f32), "batch")
        total = xor_order(total.reshape(9, cs, n_parts, slots, cs), 2, r, n_parts)
        return total.swapaxes(2, 3).reshape(9, cs, channels)

    low2, summed = grad_two(meta, c2, x_own, coefs2, vecs, heads, pixel_total)
    low2_parts = all_parts(low2)
    conv2_grad = settle(*weight_grad(meta, low2, a_parts))
    dn1, stats = back_two(meta, low2_parts, back_weights(w2), c1, coefs1, vecs, n_devices)
    low1, sums1 = grad_one(meta, c1, dn1, exchange(stats), weight, coefs1, vecs, pixel_total)
    low1_parts = all_parts(low1)
    conv1_grad = settle(*weight_grad(meta, low1, x_parts))
    keep, send = back_one(meta, low1_parts, back_weights(w1), summed)
    got = swap(send, "task", n_parts).astype(f32)
    input_grad = jnp.stack([jnp.where(first, keep, got), jnp.where(first, got, keep)])

    def own_slice(rows, at):
        line = rows[at : at + 2].reshape(-1)
        return lax.dynamic_slice_in_dim(line, g * cs, cs)

    head_weight_grad = lax.dynamic_slice_in_dim(head_grad, t * tasks_here, tasks_here, axis=0)
    head_weight_grad = head_weight_grad.reshape(tasks_here, n_parts, slots, cs).swapaxes(1, 2)
    head_weight_grad = head_weight_grad.reshape(tasks_here, channels).T
    head_bias_grad = lax.dynamic_slice_in_dim(bias_grad[0], t * tasks_here, tasks_here)
    pooled = lax.dynamic_slice_in_dim(pooled_rows, g * cs, cs, axis=1)
    return (
        pooled,
        input_grad,
        conv1_grad,
        own_slice(sums1, 0),
        own_slice(sums1, 2),
        conv2_grad,
        own_slice(heads, 0),
        own_slice(heads, 2),
        head_weight_grad,
        head_bias_grad,
        task_weights[0],
        average_next[0],
    )


def solution(mesh):
    in_specs = (
        P("batch", "task", None),
        P(None, "task", None),
        P("task"),
        P("task"),
        P(None, "task", None),
        P("task"),
        P("task"),
        P(None, "task"),
        P("task"),
        P("batch", "task"),
        P(),
        P(),
    )
    out_specs = (
        P("batch", "task"),
        P("batch", "task", None),
        P(None, "task", None),
        P("task"),
        P("task"),
        P(None, "task", None),
        P("task"),
        P("task"),
        P(None, "task"),
        P("task"),
        P(),
        P(),
    )
    return jax.shard_map(
        on_device, mesh=mesh, in_specs=in_specs, out_specs=out_specs, check_vma=False
    )
```

```python
import functools

import jax
import jax.numpy as jnp
from jax import lax
from jax.experimental import pallas as pl
from jax.experimental.pallas import tpu as pltpu
from jax.sharding import PartitionSpec as P

SIDE = 64
FW_STEPS = 20
LANES = 128
ROWS = 8

eps = 1e-05
loss_scale = 4096.0
highest = lax.Precision.HIGHEST
f32 = jnp.float32
bf16 = jnp.bfloat16


def params(mib, **more):
    return pltpu.CompilerParams(vmem_limit_bytes=mib << 20, **more)


def cost(flops, moved):
    return pl.CostEstimate(flops=flops, bytes_accessed=moved, transcendentals=0)


VM = pl.BlockSpec(memory_space=pltpu.VMEM)
SM = pl.BlockSpec(memory_space=pltpu.SMEM)


def sigmoid(v):
    return 1.0 / (1.0 + jnp.exp(-v))


def silu_slope(v):
    s = sigmoid(v)
    return s * (1.0 + v * (1.0 - s))


def half(h):
    return slice(h * LANES, (h + 1) * LANES)


def fill_shifted(dst, load, col0, width, rows):
    cols = slice(col0, col0 + width)
    block = 512
    zero = jnp.zeros((3, SIDE, width), bf16)
    dst[:, 0:SIDE, cols] = zero
    dst[:, SIDE + rows : SIDE + rows + SIDE, cols] = zero

    def step(i, carry):
        at = pl.multiple_of(i * block, block)
        low = load(at, block)
        to = pl.ds(pl.multiple_of(at + SIDE, SIDE), block)
        dst[1, to, cols] = low
        value = low.astype(f32)
        column = lax.broadcasted_iota(jnp.int32, (block, width), 0) & (SIDE - 1)
        dst[0, to, cols] = jnp.where(column == 0, 0.0, pltpu.roll(value, 1, 0)).astype(bf16)
        dst[2, to, cols] = jnp.where(column == SIDE - 1, 0.0, pltpu.roll(value, block - 1, 0)).astype(bf16)
        return carry

    lax.fori_loop(0, rows // block, step, 0)


def fill_part(dst, part, first, col0, rows):
    if len(part) == 1:
        v = part[0]
        fill_shifted(dst, lambda at, n: v[pl.ds(at, n), :], col0, v.shape[1], rows)
        return
    own, other = part
    width = own.shape[1]

    def pick(one, two):
        return lambda at, n: jnp.where(first, one[pl.ds(at, n), :], two[pl.ds(at, n), :])

    fill_shifted(dst, pick(own, other), col0, width, rows)
    fill_shifted(dst, pick(other, own), col0 + width, width, rows)


def load_slice(ref, k, s, width):
    if width % LANES == 0:
        return ref[k, :, pl.ds(pl.multiple_of(s * width, LANES), width)]
    per = LANES // width
    both = ref[k, :, pl.ds(pl.multiple_of(s // per * LANES, LANES), LANES)]
    out = both[:, 0:width]
    for i in range(1, per):
        out = jnp.where(s % per == i, both[:, i * width : (i + 1) * width], out)
    return out


def weight_rows(meta, cs):
    g, x = meta[1], meta[4]
    hs = cs // 2
    return [
        pl.ds(pl.multiple_of(g * cs, cs), cs),
        pl.ds(pl.multiple_of((1 - g) * cs + x * hs, hs), hs),
        pl.ds(pl.multiple_of((1 - g) * cs + (1 - x) * hs, hs), hs),
    ]


def send_rows(out, rows, base=None):
    n = out.shape[0]
    start = jnp.zeros((ROWS, LANES), f32) if base is None else base
    out[...] = jnp.broadcast_to(start[None], out.shape)
    for at, value in rows:
        out[:, at : at + 1, :] = jnp.broadcast_to(value[None], (n, 1, LANES))


def weighted(got, weight, row):
    return jnp.sum(got[:, row, :] * weight, axis=0, keepdims=True)


def norm_coefs(got, weight_ref, h, rows):
    weight = weight_ref[...]
    count = jnp.sum(weight, axis=0, keepdims=True)
    means = got[:, h, :]
    mean = jnp.sum(means * weight, axis=0, keepdims=True) / count
    away = means - mean
    squares = jnp.sum((got[:, 2 + h, :] + rows * (away * away)) * weight, axis=0, keepdims=True)
    return mean, lax.rsqrt(squares / (count * rows) + eps)


def conv_kernel(n_parts, per_part, meta, extra, *refs):
    pieces, refs = refs[:3], refs[3:]
    xs, (out, stats, scratch, w) = refs[: n_parts * per_part], refs[n_parts * per_part :]
    rows, width = out.shape
    cs = width // 2
    chunk = 1024
    r = meta[2]
    for i in range(n_parts):
        fill_part(scratch, xs[i * per_part : (i + 1) * per_part], meta[1] == 0, i * width, rows)

    def place(k, carry):
        for piece, to in zip(pieces, weight_rows(meta, cs)):
            for i in range(n_parts):
                for s in range(2):
                    lo = i * width + s * cs
                    w[k, to, lo : lo + cs] = load_slice(piece, k, s * n_parts + (r ^ i), cs)
        return carry

    lax.fori_loop(0, 9, place, 0)

    def step(j, carry):
        mean, squares = carry
        at = pl.multiple_of(j * chunk, chunk)
        acc = None
        for k in range(9):
            dy, dx = k // 3 - 1, k % 3 - 1
            lhs = scratch[dx + 1, pl.ds(pl.multiple_of(at + SIDE * (dy + 1), SIDE), chunk), :]
            term = lax.dot_general(lhs, w[k], (((1,), (1,)), ((), ())), preferred_element_type=f32)
            acc = term if acc is None else acc + term
        out[pl.ds(at, chunk), :] = acc
        here = jnp.sum(acc, axis=0, keepdims=True) / chunk
        away = out[pl.ds(at, chunk), :] - here
        spread = jnp.sum(away * away, axis=0, keepdims=True)
        before = jnp.asarray(j, f32)
        gap = here - mean
        share = before / (before + 1.0)
        return mean + gap / (before + 1.0), squares + spread + gap * gap * (share * chunk)

    zero = jnp.zeros((1, width), f32)
    mean, squares = lax.fori_loop(0, rows // chunk, step, (zero, zero))
    send_rows(
        stats,
        [(h, mean[:, half(h)]) for h in range(width // LANES)]
        + [(2 + h, squares[:, half(h)]) for h in range(width // LANES)],
        extra[...],
    )


def conv_stats(meta, extra, pieces, parts, n_devices):
    cs = pieces[0].shape[1]
    rows, width, channels = parts[0][0].shape[0], 2 * cs, pieces[0].shape[2]
    n, per_part = len(parts), len(parts[0])
    return pl.pallas_call(
        functools.partial(conv_kernel, n, per_part),
        in_specs=[SM] + [VM] * (4 + n * per_part),
        out_specs=(VM, VM),
        out_shape=(
            jax.ShapeDtypeStruct((rows, width), f32),
            jax.ShapeDtypeStruct((n_devices, ROWS, LANES), f32),
        ),
        scratch_shapes=[
            pltpu.VMEM((3, rows + 2 * SIDE, channels), bf16),
            pltpu.VMEM((9, width, channels), bf16),
        ],
        compiler_params=params(60),
        cost_estimate=cost(2 * 9 * rows * width * channels, 16 << 20),
        name="conv_stats",
    )(meta, extra, *pieces, *[v for part in parts for v in part])


def act_kernel(n_parts, meta, c, got, weight, out, coefs):
    halves = c.shape[1] // LANES
    cs = c.shape[1] // 2

    @pl.when(pl.program_id(0) == 0)
    def _():
        coefs[...] = jnp.zeros(coefs.shape, f32)
        for h in range(halves):
            mean, scale = norm_coefs(got, weight, h, loss_scale)
            coefs[h : h + 1, :] = mean
            coefs[2 + h : 3 + h, :] = scale
        for v in range(4):
            for g in range(2):
                row = got[g * n_parts + meta[2], 4 + v : 5 + v, 0:cs]
                lo = g * cs
                coefs[4 + 2 * v + lo // LANES : 5 + 2 * v + lo // LANES, lo % LANES : lo % LANES + cs] = row

    for h in range(halves):
        normed = (c[:, half(h)] - coefs[h : h + 1, :]) * coefs[2 + h : 3 + h, :]
        normed = normed * coefs[4 + h : 5 + h, :] + coefs[6 + h : 7 + h, :]
        out[:, half(h)] = (normed * sigmoid(normed)).astype(bf16)


def blocked(block, width):
    return pl.BlockSpec((block, width), lambda i: (i, 0))


def whole(shape):
    return pl.BlockSpec(shape, lambda i: (0,) * len(shape))


def activate(meta, c, got, weight, n_parts):
    rows, width = c.shape
    block = 1024
    return pl.pallas_call(
        functools.partial(act_kernel, n_parts),
        grid=(rows // block,),
        in_specs=[SM, blocked(block, width), whole(got.shape), whole(weight.shape)],
        out_specs=(blocked(block, width), whole((2 * ROWS, LANES))),
        out_shape=(
            jax.ShapeDtypeStruct((rows, width), bf16),
            jax.ShapeDtypeStruct((2 * ROWS, LANES), f32),
        ),
        compiler_params=params(60),
        cost_estimate=cost(20 * rows * width, 6 * rows * width),
        name="activate",
    )(meta, c, got, weight)


def turn_kernel(meta, images, own, other):
    g = meta[1]
    own[...] = images[g].T
    other[...] = images[1 - g].T


def turn(meta, images):
    slots, cs, rows = images.shape
    block = 1024
    return pl.pallas_call(
        turn_kernel,
        grid=(rows // block,),
        in_specs=[SM, pl.BlockSpec((slots, cs, block), lambda i: (0, 0, i))],
        out_specs=(blocked(block, cs), blocked(block, cs)),
        out_shape=(jax.ShapeDtypeStruct((rows, cs), bf16),) * 2,
        compiler_params=params(60),
        cost_estimate=cost(1 << 20, 8 * rows * cs),
        name="turn",
    )(meta, images)


def join_kernel(meta, keep, got, out):
    g = meta[1]
    out[g] = keep[...]
    out[1 - g] = got[...].astype(f32)


def join(meta, keep, got):
    cs, rows = keep.shape
    block = 1024
    piece = pl.BlockSpec((cs, block), lambda i: (0, i))
    return pl.pallas_call(
        join_kernel,
        grid=(rows // block,),
        in_specs=[SM, piece, piece],
        out_specs=pl.BlockSpec((2, cs, block), lambda i: (0, 0, i)),
        out_shape=jax.ShapeDtypeStruct((2, cs, rows), f32),
        compiler_params=params(60),
        cost_estimate=cost(1 << 20, 14 * rows * cs),
        name="join",
    )(meta, keep, got)


def picked(first, own, other, h, cs):
    if cs == LANES:
        return jnp.where(first, *((own[...], other[...]) if h == 0 else (other[...], own[...])))
    one, two = own[...], other[...]
    return jnp.concatenate([jnp.where(first, one, two), jnp.where(first, two, one)], axis=1)


def pool_kernel(meta, c, own, other, got, weight, coefs1, labels, out, coefs, sums):
    step, last = pl.program_id(0), pl.num_programs(0) - 1
    halves = c.shape[1] // LANES
    first = meta[1] == 0

    @pl.when(step == 0)
    def _():
        sums[...] = jnp.zeros_like(sums)
        coefs[...] = jnp.zeros(coefs.shape, f32)
        for h in range(halves):
            mean, scale = norm_coefs(got, weight, h, loss_scale)
            coefs[h : h + 1, :] = mean
            coefs[2 + h : 3 + h, :] = scale

    for h in range(halves):
        hat = (c[:, half(h)] - coefs[h : h + 1, :]) * coefs[2 + h : 3 + h, :]
        x = picked(first, own, other, h, c.shape[1] // 2).astype(f32)
        v = hat * coefs1[8 + h : 9 + h, :] + coefs1[10 + h : 11 + h, :] + x
        s = sigmoid(v)
        slope = s * (1.0 + v * (1.0 - s))
        sums[h : h + 1, :] += jnp.sum(v * s, axis=0, keepdims=True)
        sums[2 + h : 3 + h, :] += jnp.sum(slope * hat, axis=0, keepdims=True)
        sums[4 + h : 5 + h, :] += jnp.sum(slope, axis=0, keepdims=True)

    @pl.when(step == last)
    def _():
        valid = meta[3].astype(f32)
        rows = []
        for h in range(halves):
            rows.append((h, sums[h : h + 1, :] * (valid / loss_scale)))
            rows.append((2 + h, sums[2 + h : 3 + h, :]))
            rows.append((4 + h, sums[4 + h : 5 + h, :]))
        rows.append((6, labels[0:1, :]))
        rows.append((7, labels[1:2, :]))
        send_rows(out, rows)


def pool(meta, c, own, other, got, weight, coefs1, labels):
    rows, width = c.shape
    block = 1024
    return pl.pallas_call(
        pool_kernel,
        grid=(rows // block,),
        in_specs=[
            SM,
            blocked(block, width),
            blocked(block, width // 2),
            blocked(block, width // 2),
            whole(got.shape),
            whole(weight.shape),
            whole(coefs1.shape),
            whole(labels.shape),
        ],
        out_specs=(whole(got.shape), whole((ROWS, LANES))),
        out_shape=(
            jax.ShapeDtypeStruct(got.shape, f32),
            jax.ShapeDtypeStruct((ROWS, LANES), f32),
        ),
        scratch_shapes=[pltpu.VMEM((ROWS, LANES), f32)],
        compiler_params=params(60),
        cost_estimate=cost(30 * rows * width, 6 * rows * width),
        name="pool",
    )(meta, c, own, other, got, weight, coefs1, labels)


def head_kernel(n_parts, meta, got, ht, bias, valid, avg_row, avg_col, coefs, tw, an, hwg, hbg, pooled_own, pooled, slopes, shifts, labels, grads, mine_all, pooled_part):
    tasks, channels = ht.shape
    images = valid.shape[0]
    n_task = 2 * n_parts
    width = channels // n_parts
    halves = width // LANES
    r = meta[2]
    for n in range(images):
        base = (n // 2) * n_task + (n % 2) * n_parts
        for part in range(n_parts):
            for h in range(halves):
                lo = part * width + h * LANES
                pooled[n : n + 1, lo : lo + LANES] = got[base + part, h : h + 1, :]
        for h in range(halves):
            slopes[n : n + 1, half(h)] = got[base + r, 2 + h : 3 + h, :]
            shifts[n : n + 1, half(h)] = got[base + r, 4 + h : 5 + h, :]
        row = 6 + n % 2
        lab = got[(n // 2) * n_task, row : row + 1, :]
        for t in range(1, n_task):
            lab = lab + got[(n // 2) * n_task + t, row : row + 1, :]
        labels[n : n + 1, :] = lab
    pooled_all = pooled[...]
    table = ht[...]
    both_last = (((1,), (1,)), ((), ()))
    both_first = (((0,), (0,)), ((), ()))
    logits = lax.dot_general(pooled_all, table, both_last, precision=highest, preferred_element_type=f32) + bias[...]
    count = jnp.sum(valid[...], axis=0, keepdims=True)
    errors = valid[...] * (sigmoid(logits) - labels[:, 0:tasks]) / count
    gram = lax.dot_general(errors, errors, both_first, precision=highest, preferred_element_type=f32) * lax.dot_general(
        table, table, both_last, precision=highest, preferred_element_type=f32
    )
    row_id = lax.broadcasted_iota(jnp.int32, (tasks, tasks), 0)
    col_id = lax.broadcasted_iota(jnp.int32, (tasks, tasks), 1)
    trace = jnp.sum(jnp.sum(jnp.where(row_id == col_id, gram, 0.0), axis=1, keepdims=True), axis=0, keepdims=True)
    normalized = gram / (trace / tasks)
    start_row = avg_row[...] / jnp.sum(avg_row[...], axis=1, keepdims=True)
    start_col = avg_col[...] / jnp.sum(avg_col[...], axis=0, keepdims=True)
    w_row, w_col = start_row, start_col
    for j in range(FW_STEPS):
        rate = 1.0 / (j + 4.0)
        z_col = -tasks * jnp.sum(normalized * w_row, axis=1, keepdims=True)
        z_row = -tasks * jnp.sum(normalized * w_col, axis=0, keepdims=True)
        e_col = jnp.exp(z_col - jnp.max(z_col, axis=0, keepdims=True))
        e_row = jnp.exp(z_row - jnp.max(z_row, axis=1, keepdims=True))
        w_col = (1.0 - rate) * w_col + rate * (e_col / jnp.sum(e_col, axis=0, keepdims=True))
        w_row = (1.0 - rate) * w_row + rate * (e_row / jnp.sum(e_row, axis=1, keepdims=True))
    tw[...] = w_row
    an[...] = 0.9 * start_row + 0.1 * w_row
    logit_grads = errors * ((loss_scale * tasks) * w_row)
    hbg[...] = jnp.sum(logit_grads, axis=0, keepdims=True)
    hwg[...] = lax.dot_general(logit_grads, pooled_all, both_first, precision=highest, preferred_element_type=f32)
    grads[...] = jnp.dot(logit_grads, table, precision=highest, preferred_element_type=f32) / loss_scale
    own = pl.ds(pl.multiple_of(r * width, LANES), width)
    q = grads[:, own]
    mine_all[...] = q
    pooled_part[...] = pooled[:, own]
    gain = jnp.sum(q * slopes[...], axis=0, keepdims=True)
    shift = jnp.sum(q * shifts[...], axis=0, keepdims=True)
    mine = mine_all[pl.ds(2 * meta[0] + meta[1], 1), :]
    coefs[...] = jnp.zeros(coefs.shape, f32)
    for h in range(halves):
        coefs[h : h + 1, :] = gain[:, half(h)]
        coefs[2 + h : 3 + h, :] = shift[:, half(h)]
        coefs[4 + h : 5 + h, :] = mine[:, half(h)]
    for i in range(2):
        pooled_own[i : i + 1, :] = pooled_part[pl.ds(2 * meta[0] + i, 1), :]


def head(meta, got, ht, bias, valid, avg_row, avg_col, n_parts):
    tasks, channels = ht.shape
    images = valid.shape[0]
    width = channels // n_parts
    shapes = [(ROWS, LANES), (1, tasks), (1, tasks), (tasks, channels), (1, tasks), (2, width)]
    return pl.pallas_call(
        functools.partial(head_kernel, n_parts),
        in_specs=[SM] + [VM] * 6,
        out_specs=tuple(VM for _ in shapes),
        out_shape=tuple(jax.ShapeDtypeStruct(s, f32) for s in shapes),
        scratch_shapes=[
            pltpu.VMEM((images, channels), f32),
            pltpu.VMEM((images, width), f32),
            pltpu.VMEM((images, width), f32),
            pltpu.VMEM((images, LANES), f32),
            pltpu.VMEM((images, channels), f32),
            pltpu.VMEM((images, width), f32),
            pltpu.VMEM((images, width), f32),
        ],
        compiler_params=params(60),
        cost_estimate=cost(1 << 20, 1 << 20),
        name="head",
    )(meta, got, ht, bias, valid, avg_row, avg_col)


def grad_two_kernel(meta, c, own, other, coefs, coefs1, heads, pixels, low, summed):
    valid = meta[3].astype(f32)
    first = meta[1] == 0
    for h in range(c.shape[1] // LANES):
        mean, scale = coefs[h : h + 1, :], coefs[2 + h : 3 + h, :]
        gain = coefs1[8 + h : 9 + h, :]
        hat = (c[:, half(h)] - mean) * scale
        x = picked(first, own, other, h, c.shape[1] // 2).astype(f32)
        v = hat * gain + coefs1[10 + h : 11 + h, :] + x
        dn = (valid * heads[4 + h : 5 + h, :]) * silu_slope(v)
        summed[:, half(h)] = dn
        away = (heads[2 + h : 3 + h, :] + hat * heads[h : h + 1, :]) / pixels[0]
        low[:, half(h)] = ((valid * gain * scale) * (dn - away)).astype(bf16)


def grad_two(meta, c, own, other, coefs, coefs1, heads, pixels):
    rows, width = c.shape
    block = 1024
    return pl.pallas_call(
        grad_two_kernel,
        grid=(rows // block,),
        in_specs=[
            SM,
            blocked(block, width),
            blocked(block, width // 2),
            blocked(block, width // 2),
            whole(coefs.shape),
            whole(coefs1.shape),
            whole(heads.shape),
            SM,
        ],
        out_specs=(blocked(block, width), blocked(block, width)),
        out_shape=(
            jax.ShapeDtypeStruct((rows, width), bf16),
            jax.ShapeDtypeStruct((rows, width), f32),
        ),
        compiler_params=params(60),
        cost_estimate=cost(30 * rows * width, 12 * rows * width),
        name="grad_two",
    )(meta, c, own, other, coefs, coefs1, heads, pixels)


def grad_one_kernel(meta, c, dn, got, weight, coefs, pixels, low, sums):
    valid = meta[3].astype(f32)
    halves = c.shape[1] // LANES

    @pl.when(pl.program_id(0) == 0)
    def _():
        sums[...] = jnp.zeros(sums.shape, f32)
        for h in range(halves):
            sums[h : h + 1, :] = weighted(got, weight[...], h)
            sums[2 + h : 3 + h, :] = weighted(got, weight[...], 2 + h)

    for h in range(halves):
        mean, scale = coefs[h : h + 1, :], coefs[2 + h : 3 + h, :]
        hat = (c[:, half(h)] - mean) * scale
        away = (sums[2 + h : 3 + h, :] + hat * sums[h : h + 1, :]) / pixels[0]
        low[:, half(h)] = ((valid * coefs[4 + h : 5 + h, :] * scale) * (dn[:, half(h)] - away)).astype(bf16)


def grad_one(meta, c, dn, got, weight, coefs, pixels):
    rows, width = c.shape
    block = 1024
    return pl.pallas_call(
        grad_one_kernel,
        grid=(rows // block,),
        in_specs=[
            SM,
            blocked(block, width),
            blocked(block, width),
            whole(got.shape),
            whole(weight.shape),
            whole(coefs.shape),
            SM,
        ],
        out_specs=(blocked(block, width), whole((ROWS, LANES))),
        out_shape=(
            jax.ShapeDtypeStruct((rows, width), bf16),
            jax.ShapeDtypeStruct((ROWS, LANES), f32),
        ),
        compiler_params=params(60),
        cost_estimate=cost(10 * rows * width, 10 * rows * width),
        name="grad_one",
    )(meta, c, dn, got, weight, coefs, pixels)


def back_setup(meta, n_parts, pieces, gs, w, scratch, rows, width):
    cs = width // 2
    r = meta[2]
    for i in range(n_parts):
        fill_part(scratch, [gs[i]], None, i * width, rows)

    def place(k, carry):
        for i in range(n_parts):
            spots = weight_rows(meta, cs)
            for piece, to in zip(pieces[3 * i : 3 * i + 3], spots):
                to = pl.ds(pl.multiple_of(to.start + i * width, cs // 2), to.size)
                for s in range(2):
                    w[k, to, s * cs : (s + 1) * cs] = load_slice(piece, k, s * n_parts + r, cs)
        return carry

    lax.fori_loop(0, 9, place, 0)


def back_products(scratch, w, at, chunk):
    acc = None
    for k in range(9):
        dy, dx = k // 3 - 1, k % 3 - 1
        lhs = scratch[1 - dx, pl.ds(pl.multiple_of(at + SIDE * (1 - dy), SIDE), chunk), :]
        term = jnp.dot(lhs, w[k], preferred_element_type=f32)
        acc = term if acc is None else acc + term
    return acc


def back_two_kernel(n_parts, meta, *refs):
    pieces, gs, refs = refs[: 3 * n_parts], refs[3 * n_parts : 4 * n_parts], refs[4 * n_parts :]
    c, coefs, out, stats, scratch, w = refs
    rows, width = out.shape
    halves = width // LANES
    chunk = 1024
    back_setup(meta, n_parts, pieces, gs, w, scratch, rows, width)

    def step(j, carry):
        at = pl.multiple_of(j * chunk, chunk)
        acc = back_products(scratch, w, at, chunk)
        sums = []
        for h in range(halves):
            hat = (c[pl.ds(at, chunk), half(h)] - coefs[h : h + 1, :]) * coefs[2 + h : 3 + h, :]
            dn = acc[:, half(h)] * silu_slope(hat * coefs[4 + h : 5 + h, :] + coefs[6 + h : 7 + h, :])
            out[pl.ds(at, chunk), half(h)] = dn
            sums.append(carry[2 * h] + jnp.sum(dn * hat, axis=0, keepdims=True))
            sums.append(carry[2 * h + 1] + jnp.sum(dn, axis=0, keepdims=True))
        return tuple(sums)

    zero = jnp.zeros((1, LANES), f32)
    sums = lax.fori_loop(0, rows // chunk, step, (zero,) * (2 * halves))
    send_rows(stats, [(2 * i + h, sums[2 * h + i]) for h in range(halves) for i in range(2)])


def back_scratch(rows, width, n):
    return [
        pltpu.VMEM((3, rows + 2 * SIDE, n * width), bf16),
        pltpu.VMEM((9, n * width, width), bf16),
    ]


def back_two(meta, pieces, g_parts, c, coefs, n_devices):
    rows, width = c.shape
    n = len(g_parts)
    return pl.pallas_call(
        functools.partial(back_two_kernel, n),
        in_specs=[SM] + [VM] * (4 * n + 2),
        out_specs=(VM, VM),
        out_shape=(
            jax.ShapeDtypeStruct((rows, width), f32),
            jax.ShapeDtypeStruct((n_devices, ROWS, LANES), f32),
        ),
        scratch_shapes=back_scratch(rows, width, n),
        compiler_params=params(60),
        cost_estimate=cost(2 * 9 * rows * width * width * n, 16 << 20),
        name="back_two",
    )(meta, *pieces, *g_parts, c, coefs)


def back_one_kernel(n_parts, meta, *refs):
    pieces, gs, refs = refs[: 3 * n_parts], refs[3 * n_parts : 4 * n_parts], refs[4 * n_parts :]
    summed, keep, send, scratch, w = refs
    rows, width = summed.shape
    cs = width // 2
    chunk = 1024
    first = meta[1] == 0
    back_setup(meta, n_parts, pieces, gs, w, scratch, rows, width)

    def step(j, carry):
        at = pl.multiple_of(j * chunk, chunk)
        acc = back_products(scratch, w, at, chunk) + summed[pl.ds(at, chunk), :]
        a, b = acc[:, :cs], acc[:, cs:]
        keep[:, pl.ds(at, chunk)] = jnp.where(first, a, b).T
        send[:, pl.ds(at, chunk)] = jnp.where(first, b, a).T.astype(bf16)
        return carry

    lax.fori_loop(0, rows // chunk, step, 0)


def back_one(meta, pieces, g_parts, summed):
    rows, width = summed.shape
    n = len(g_parts)
    return pl.pallas_call(
        functools.partial(back_one_kernel, n),
        in_specs=[SM] + [VM] * (4 * n + 1),
        out_specs=(VM, VM),
        out_shape=(
            jax.ShapeDtypeStruct((width // 2, rows), f32),
            jax.ShapeDtypeStruct((width // 2, rows), bf16),
        ),
        scratch_shapes=back_scratch(rows, width, n),
        compiler_params=params(60),
        cost_estimate=cost(2 * 9 * rows * width * width * n, 16 << 20),
        name="back_one",
    )(meta, *pieces, *g_parts, summed)


def weight_kernel(n_parts, per_part, meta, g, *refs):
    xs, (keep, send, scratch) = refs[: n_parts * per_part], refs[n_parts * per_part :]
    rows, width = g.shape
    cs = width // 2
    first = meta[1] == 0
    fill_part(scratch, [g], None, 0, rows)
    rights = []
    for i in range(n_parts):
        part = xs[i * per_part : (i + 1) * per_part]
        if per_part == 1:
            rights.append(part[0][...])
        else:
            own, other = part[0][...], part[1][...]
            rights.append(jnp.concatenate([jnp.where(first, own, other), jnp.where(first, other, own)], axis=1))
    for k in range(9):
        dy, dx = k // 3 - 1, k % 3 - 1
        lo = SIDE * (1 - dy)
        lhs = scratch[1 - dx, lo : lo + rows, :]
        for i in range(n_parts):
            term = lax.dot_general(lhs, rights[i], (((0,), (0,)), ((), ())), preferred_element_type=f32)
            a, b = term[:cs], term[cs:]
            cols = slice(i * width, (i + 1) * width)
            keep[k, :, cols] = jnp.where(first, a, b)
            send[k, :, cols] = jnp.where(first, b, a).astype(bf16)


def weight_grad(meta, g, parts):
    rows, width = g.shape
    n, per_part = len(parts), len(parts[0])
    shape = (9, width // 2, n * width)
    return pl.pallas_call(
        functools.partial(weight_kernel, n, per_part),
        in_specs=[SM] + [VM] * (n * per_part + 1),
        out_specs=(VM, VM),
        out_shape=(jax.ShapeDtypeStruct(shape, f32), jax.ShapeDtypeStruct(shape, bf16)),
        scratch_shapes=[pltpu.VMEM((3, rows + 2 * SIDE, width), bf16)],
        compiler_params=params(60),
        cost_estimate=cost(2 * 9 * rows * width * width * n, 16 << 20),
        name="weight_grad",
    )(meta, g, *[v for part in parts for v in part])


def swap(values, axis, by):
    n = lax.axis_size(axis)
    return lax.ppermute(values, axis, [(i, i ^ by) for i in range(n)])


def xor_order(values, r):
    bit = 1
    while bit < len(values):
        flip = (r & bit) != 0
        values = [jnp.where(flip, values[i ^ bit], v) for i, v in enumerate(values)]
        bit *= 2
    return values


def gate(values, *others):
    return lax.optimization_barrier((values, *others))[0]


def scatter_stage(total, stage, kind, after=None):
    stride, size = stage
    k = (lax.axis_index("batch") // stride) % size
    split = total.reshape(size, -1, total.shape[1])
    total = lax.dynamic_index_in_dim(split, k, keepdims=False)
    got = [
        swap(lax.dynamic_index_in_dim(split, k ^ j, keepdims=False).astype(kind), "batch", stride * j)
        for j in range(1, size)
    ]
    for v in got:
        total = total + (v if after is None else gate(v, after)).astype(f32)
    return total


def gather_stage(out, stage):
    stride, size = stage
    k = (lax.axis_index("batch") // stride) % size
    pieces = [out] + [swap(out, "batch", stride * j) for j in range(1, size)]
    return jnp.concatenate(xor_order(pieces, k), axis=0)


def on_device(
    images,
    conv1_weight,
    norm1_gain,
    norm1_bias,
    conv2_weight,
    norm2_gain,
    norm2_bias,
    head_weight,
    head_bias,
    labels,
    image_counts,
    average_weights,
):
    n_task, n_batch = lax.axis_size("task"), lax.axis_size("batch")
    t, b = lax.axis_index("task"), lax.axis_index("batch")
    slots, cs, pixels = images.shape
    n_parts = n_task // slots
    g, r = t // n_parts, t % n_parts
    first = g == 0
    width = slots * cs
    channels = n_task * cs
    n_devices = n_task * n_batch
    tasks_here = head_weight.shape[1]
    tasks = tasks_here * n_task

    valid_images = (jnp.arange(slots)[None, :] < image_counts[:, None]).astype(f32)
    image_total = jnp.sum(image_counts).astype(f32)
    pixel_total = (image_total * pixels).reshape(1)
    own_valid = (g < lax.dynamic_index_in_dim(image_counts, b, keepdims=False)).astype(jnp.int32)
    meta = jnp.stack([b, g, r, own_valid, b % 2]).astype(jnp.int32)
    same = (jnp.arange(n_parts) == r).astype(f32)
    weight = (valid_images[:, :, None] * same[None, None, :]).reshape(n_devices, 1)
    weight = jnp.broadcast_to(weight, (n_devices, LANES))

    def weight_pieces(w, after=None):
        halves = w.reshape(9, 2, cs // 2, channels)
        sent = lax.dynamic_index_in_dim(halves, b % 2, axis=1, keepdims=False)
        if after is not None:
            sent = gate(sent, after)
        return [w, swap(sent, "task", n_parts)]

    def all_pieces(pieces):
        return [swap(v, "task", i) if i else v for i in range(n_parts) for v in pieces]

    def all_parts(v):
        return [v] + [swap(v, "task", i) for i in range(1, n_parts)]

    w1 = weight_pieces(conv1_weight)
    w1.append(swap(w1[1], "batch", 1))
    x_own, x_send = turn(meta, images)
    x_other = swap(gate(x_send, w1[1]), "task", n_parts)
    x_parts = list(zip(all_parts(x_own), all_parts(gate(x_other, w1[2]))))
    w2 = weight_pieces(conv2_weight, x_other)

    lines = jnp.pad(head_bias, (0, channels - tasks_here)).reshape(1, channels)
    mine = jnp.concatenate([head_weight.T.astype(f32), lines])
    mine = jnp.pad(mine, ((0, -mine.shape[0] % ROWS), (0, 0)))
    every = xor_order([mine] + [swap(mine, "task", i) for i in range(1, n_task)], t)
    table = jnp.concatenate([v[:tasks_here] for v in every])
    table = table.reshape(tasks, slots, n_parts, cs).swapaxes(1, 2).reshape(tasks, channels)
    bias_row = jnp.concatenate([v[tasks_here, :tasks_here] for v in every]).reshape(1, tasks)
    vecs = jnp.stack([norm1_gain, norm1_bias, norm2_gain, norm2_bias])
    vecs = jnp.pad(vecs, ((4, 0), (0, LANES - cs)))
    label_rows = lax.dynamic_update_slice(
        jnp.zeros((slots, LANES), f32), labels.astype(f32), (0, t * tasks_here)
    )

    def exchange(rows):
        flat_rows = rows.reshape(n_devices * ROWS, LANES)
        return lax.all_to_all(flat_rows, ("batch", "task"), 0, 0, tiled=True).reshape(rows.shape)

    c1, stats = conv_stats(meta, vecs, w1, x_parts, n_devices)
    w2.append(swap(gate(w2[1], stats), "batch", 1))
    a_own, coefs1 = activate(meta, c1, exchange(stats), weight, n_parts)
    a_parts = [[v] for v in all_parts(gate(a_own, w2[2]))]
    c2, stats = conv_stats(meta, vecs, w2, a_parts, n_devices)
    sums, coefs2 = pool(meta, c2, x_own, x_other, exchange(stats), weight, coefs1, label_rows)
    heads, task_weights, average_next, head_grad, bias_grad, pooled_rows = head(
        meta,
        exchange(sums),
        table,
        bias_row,
        valid_images.reshape(-1, 1),
        average_weights.reshape(1, -1),
        average_weights.reshape(-1, 1),
        n_parts,
    )

    def assemble(done):
        parts = [v.reshape(9, cs, -1)[:, :, i * width : (i + 1) * width] for v in done for i in range(v.shape[1] // width)]
        out = [
            v.astype(f32)
            for s in range(slots)
            for v in xor_order([part[:, :, s * cs : (s + 1) * cs] for part in parts], r)
        ]
        return jnp.concatenate(out, axis=2)

    def both_groups(keep, got):
        return (keep + got.astype(f32)).reshape(9 * cs, -1)

    bits = n_batch.bit_length() - 1
    near = 1 << (bits // 2)
    stages = [(1, near), (near, n_batch // near)]
    low2, summed = grad_two(meta, c2, x_own, x_other, coefs2, coefs1, heads, pixel_total)
    low2_parts = all_parts(low2)
    keep2, send2 = weight_grad(meta, low2, a_parts)
    got2 = swap(send2, "task", n_parts)
    dn1, stats = back_two(meta, all_pieces(w2), [gate(low2_parts[0], keep2)] + low2_parts[1:], c1, coefs1, n_devices)
    low1, sums1 = grad_one(meta, c1, dn1, exchange(stats), weight, coefs1, pixel_total)
    sum2 = scatter_stage(both_groups(keep2, gate(got2, dn1)), stages[0], bf16)
    low1_parts = all_parts(low1)
    pairs = []
    for part in x_parts:
        pairs.append(weight_grad(meta, gate(low1, pairs[-1][0]) if pairs else low1, [part]))
    got1 = [swap(send, "task", n_parts) for _, send in pairs]
    low1_parts[0] = gate(low1_parts[0], pairs[-1][0])
    keep, send = back_one(meta, all_pieces(w1), low1_parts, summed)
    sum2 = scatter_stage(gate(sum2, pairs[-1][0]), stages[1], f32, keep)
    sum1 = [scatter_stage(both_groups(pair[0], gate(v, keep)), stages[0], bf16) for pair, v in zip(pairs, got1)]
    sum2 = gather_stage(sum2.astype(bf16), stages[1])
    sum1 = [scatter_stage(v, stages[1], bf16) for v in sum1]
    sum2 = gather_stage(sum2, stages[0])
    sum1 = [gather_stage(v.astype(bf16), stages[1]) for v in sum1]
    sum1 = [gather_stage(v, stages[0]) for v in sum1]
    input_grad = join(meta, keep, swap(send, "task", n_parts))
    conv1_grad = assemble(sum1)
    conv2_grad = assemble([sum2])

    def own_slice(rows, at):
        line = rows[at : at + 2].reshape(-1)
        return lax.dynamic_slice_in_dim(line, g * cs, cs)

    head_weight_grad = lax.dynamic_slice_in_dim(head_grad, t * tasks_here, tasks_here, axis=0)
    head_weight_grad = head_weight_grad.reshape(tasks_here, n_parts, slots, cs).swapaxes(1, 2)
    head_weight_grad = head_weight_grad.reshape(tasks_here, channels).T
    head_bias_grad = lax.dynamic_slice_in_dim(bias_grad[0], t * tasks_here, tasks_here)
    pooled = lax.dynamic_slice_in_dim(pooled_rows, g * cs, cs, axis=1)
    return (
        pooled,
        input_grad,
        conv1_grad,
        own_slice(sums1, 0),
        own_slice(sums1, 2),
        conv2_grad,
        own_slice(heads, 0),
        own_slice(heads, 2),
        head_weight_grad,
        head_bias_grad,
        task_weights[0],
        average_next[0],
    )


def solution(mesh):
    in_specs = (
        P("batch", "task", None),
        P(None, "task", None),
        P("task"),
        P("task"),
        P(None, "task", None),
        P("task"),
        P("task"),
        P(None, "task"),
        P("task"),
        P("batch", "task"),
        P(),
        P(),
    )
    out_specs = (
        P("batch", "task"),
        P("batch", "task", None),
        P(None, "task", None),
        P("task"),
        P("task"),
        P(None, "task", None),
        P("task"),
        P("task"),
        P(None, "task"),
        P("task"),
        P(),
        P(),
    )
    return jax.shard_map(
        on_device, mesh=mesh, in_specs=in_specs, out_specs=out_specs, check_vma=False
    )
```

```python
import functools

import jax
import jax.numpy as jnp
from jax import lax
from jax.experimental import pallas as pl
from jax.experimental.pallas import tpu as pltpu
from jax.sharding import PartitionSpec as P

SIDE = 64
FW_STEPS = 20
LANES = 128
ROWS = 8

eps = 1e-05
loss_scale = 4096.0
highest = lax.Precision.HIGHEST
f32 = jnp.float32
bf16 = jnp.bfloat16


def params(mib, **more):
    return pltpu.CompilerParams(vmem_limit_bytes=mib << 20, **more)


def cost(flops, moved):
    return pl.CostEstimate(flops=flops, bytes_accessed=moved, transcendentals=0)


VM = pl.BlockSpec(memory_space=pltpu.VMEM)
HB = pl.BlockSpec(memory_space=pl.ANY)
SM = pl.BlockSpec(memory_space=pltpu.SMEM)


def sigmoid(v):
    return 1.0 / (1.0 + jnp.exp(-v))


def silu_slope(v):
    s = sigmoid(v)
    return s * (1.0 + v * (1.0 - s))


def half(h):
    return slice(h * LANES, (h + 1) * LANES)


def held(values):
    return pltpu.with_memory_space_constraint(values, pltpu.VMEM)


def away(values):
    return pltpu.with_memory_space_constraint(values, pltpu.HBM)


def vmem_out(shape, kind):
    return pltpu.VMEM(shape, kind)


def hbm_out(shape, kind):
    return pltpu.HBM(shape, kind)


def column_is(rows, width, at):
    return (lax.broadcasted_iota(jnp.int32, (rows, width), 0) & (SIDE - 1)) == at


def moved(v, e):
    rows, width = v.shape
    if e == 0:
        return v
    edge = SIDE - 1 if e == 1 else 0
    return jnp.where(column_is(rows, width, edge), 0.0, pltpu.roll(v, rows - 1 if e == 1 else 1, 0))


def aligned(cs):
    return cs % LANES == 0


def column_plan(meta, parts, n_parts, cs):
    g, r = meta[1], meta[2]
    plan = []
    for i, part in enumerate(parts):
        if not aligned(cs):
            plan.append((part[0], slice(0, 2 * cs), i * 2 * cs))
            continue
        for s in range(2):
            place = s * n_parts + (r ^ i) if len(part) == 1 else (g, 1 - g)[s] * n_parts + (r ^ i)
            ref, cols = (part[0], slice(s * cs, (s + 1) * cs)) if len(part) == 1 else (part[s], slice(0, cs))
            plan.append((ref, cols, pl.multiple_of(place * cs, cs)))
    return plan


def place_columns(dst, plan, first_row):
    rows = plan[0][0].shape[0]
    block = 512

    def step(j, carry):
        at = pl.multiple_of(j * block, block)
        for ref, cols, to in plan:
            width = cols.stop - cols.start
            dst[pl.ds(pl.multiple_of(at + first_row, SIDE), block), pl.ds(to, width)] = ref[pl.ds(at, block), cols]
        return carry

    lax.fori_loop(0, rows // block, step, 0)


def clear_ends(dst, rows):
    zero = jnp.zeros((SIDE, dst.shape[1]), dst.dtype)
    dst[0:SIDE, :] = zero
    dst[SIDE + rows : SIDE + rows + SIDE, :] = zero


def piece_rows(meta, cs, base, n_pieces):
    g, q = meta[1], meta[4]
    qs = cs // (n_pieces - 1)
    return [pl.ds(pl.multiple_of(base + g * cs, cs), cs)] + [
        pl.ds(pl.multiple_of(base + (1 - g) * cs + (q ^ i if n_pieces > 2 else 0) * qs, qs), qs)
        for i in range(n_pieces - 1)
    ]


def forward_copies(meta, pieces, w, cs, sems):
    if not aligned(cs):
        return [pltpu.make_async_copy(pieces[0], w, sems.at[0])]
    spots = piece_rows(meta, cs, 0, len(pieces))
    return [pltpu.make_async_copy(p, w.at[:, to, :], sems.at[i]) for i, (p, to) in enumerate(zip(pieces, spots))]


def backward_copies(meta, pieces, w, cs, n_parts, sems):
    width = 2 * cs
    if not aligned(cs):
        return [
            pltpu.make_async_copy(p, w.at[:, pl.ds(i * width, width), :], sems.at[i]) for i, p in enumerate(pieces)
        ]
    copies = []
    for i in range(n_parts):
        each = len(pieces) // n_parts
        for p, to in zip(pieces[each * i : each * (i + 1)], piece_rows(meta, cs, i * width, each)):
            for s in range(2):
                cols = pl.ds(pl.multiple_of((s * n_parts + meta[2]) * cs, cs), cs)
                copies.append(
                    pltpu.make_async_copy(p.at[:, :, cols], w.at[:, to, pl.ds(s * cs, cs)], sems.at[len(copies)])
                )
    return copies


def part_half(part, first, rows, h):
    if len(part) == 1:
        return part[0][rows, half(h)].astype(f32)
    own, other = part[0][rows, :], part[1][rows, :]
    return (jnp.where(first, own, other) if h == 0 else jnp.where(first, other, own)).astype(f32)


def row_blocks(rows, block, body, start):
    def step(j, carry):
        return body(pl.ds(pl.multiple_of(j * block, block), block), carry)

    return lax.fori_loop(0, rows // block, step, start)


def send_rows(out, rows, base=None):
    n = out.shape[0]
    start = jnp.zeros((ROWS, LANES), f32) if base is None else base
    out[...] = jnp.broadcast_to(start[None], out.shape)
    for at, value in rows:
        out[:, at : at + 1, :] = jnp.broadcast_to(value[None], (n, 1, LANES))


def weighted(got, weight):
    return jnp.sum(got[...] * weight[...], axis=0)


def norm_coefs(got, weight, rows):
    w = weight[...]
    values = got[...]
    count = jnp.sum(w, axis=0)
    total = jnp.sum(values * w, axis=0)
    mean = total / count
    off = values - mean[None]
    apart = jnp.sum(off * off * w, axis=0)
    squares = total[2:4] + rows * apart[0:2]
    return mean[0:2], lax.rsqrt(squares / (count[0:2] * rows) + eps)


def stream_in(source, buffer, sems, block):
    rows = buffer.shape[0]

    def copy(j):
        at = pl.ds(pl.multiple_of(j * block, block), block)
        return pltpu.make_async_copy(source.at[at, :], buffer.at[at, :], sems.at[j])

    for j in range(rows // block):
        copy(j).start()
    return lambda j: copy(j).wait()


def stream_out(buffer, target, sems, block):
    rows = buffer.shape[0]

    def copy(j):
        at = pl.ds(pl.multiple_of(j * block, block), block)
        return pltpu.make_async_copy(buffer.at[at, :], target.at[at, :], sems.at[j])

    def finish():
        for j in range(rows // block):
            copy(j).wait()

    return (lambda j: copy(j).start()), finish


def stream_scratch(rows, width, block):
    return [pltpu.VMEM((rows, width), f32), pltpu.SemaphoreType.DMA((rows // block,))]


BLOCK = 512
CHUNK = 1024


def conv_kernel(parts_of, n_parts, n_pieces, meta, extra, *refs):
    pieces, refs = refs[:n_pieces], refs[n_pieces:]
    n = sum(parts_of)
    xs, (target, stats, scratch, w, sems, out, out_sems) = refs[:n], refs[n:]
    parts, at = [], 0
    for size in parts_of:
        parts.append(xs[at : at + size])
        at += size
    rows, width = out.shape
    cs = width // 2
    chunk = CHUNK
    send, finish = stream_out(out, target, out_sems, chunk)
    copies = forward_copies(meta, pieces, w, cs, sems)
    for c in copies:
        c.start()
    clear_ends(scratch, rows)
    place_columns(scratch, column_plan(meta, parts, n_parts, cs), SIDE)
    for c in copies:
        c.wait()

    def step(j, carry):
        mean, squares = carry
        at = pl.multiple_of(j * chunk, chunk)
        total = None
        for dx in (0, 1, -1):
            acc = None
            for dy in (-1, 0, 1):
                lhs = scratch[pl.ds(pl.multiple_of(at + SIDE * (dy + 1), SIDE), chunk), :]
                tap = w[3 * (dy + 1) + dx + 1]
                term = lax.dot_general(lhs, tap, (((1,), (1,)), ((), ())), preferred_element_type=f32)
                acc = term if acc is None else acc + term
            acc = moved(acc, dx)
            total = acc if total is None else total + acc
        out[pl.ds(at, chunk), :] = total
        send(j)
        here = jnp.sum(total, axis=0, keepdims=True) / chunk
        away = out[pl.ds(at, chunk), :] - here
        spread = jnp.sum(away * away, axis=0, keepdims=True)
        before = jnp.asarray(j, f32)
        gap = here - mean
        share = before / (before + 1.0)
        return mean + gap / (before + 1.0), squares + spread + gap * gap * (share * chunk)

    zero = jnp.zeros((1, width), f32)
    mean, squares = lax.fori_loop(0, rows // chunk, step, (zero, zero))
    send_rows(
        stats,
        [(h, mean[:, half(h)]) for h in range(width // LANES)]
        + [(2 + h, squares[:, half(h)]) for h in range(width // LANES)],
        extra[...],
    )
    finish()


def conv_stats(meta, extra, pieces, parts, cs, n_devices, weight_of):
    rows, width, channels = parts[0][0].shape[0], 2 * cs, pieces[0].shape[2]
    flat = [v for part in parts for v in part]
    return pl.pallas_call(
        functools.partial(conv_kernel, [len(p) for p in parts], len(parts), len(pieces)),
        in_specs=[SM, VM] + [HB] * len(pieces) + [VM] * len(flat),
        out_specs=(HB, VM),
        out_shape=(hbm_out((rows, width), f32), vmem_out((n_devices, ROWS, LANES), f32)),
        scratch_shapes=[
            pltpu.VMEM((rows + 2 * SIDE, channels), bf16),
            pltpu.VMEM((9, width, channels), bf16),
            pltpu.SemaphoreType.DMA((len(pieces),)),
            *stream_scratch(rows, width, CHUNK),
        ],
        compiler_params=params(20),
        cost_estimate=cost(weight_of * rows * width * channels, weight_of << 20),
        name="conv_stats",
    )(meta, extra, *[away(v) for v in pieces], *[held(v) for v in flat])


def act_kernel(n_parts, meta, source, got, weight, out, coefs, c, sems):
    rows, width = c.shape
    halves, cs = width // LANES, width // 2
    wait = stream_in(source, c, sems, BLOCK)
    mean, scale = norm_coefs(got, weight, loss_scale)
    coefs[...] = jnp.zeros(coefs.shape, f32)
    coefs[0:2, :] = mean
    coefs[2:4, :] = scale
    for v in range(4):
        for g in range(2):
            row = got[g * n_parts + meta[2], 4 + v : 5 + v, 0:cs]
            lo = g * cs
            coefs[4 + 2 * v + lo // LANES : 5 + 2 * v + lo // LANES, lo % LANES : lo % LANES + cs] = row

    def body(at, carry):
        wait(at.start // BLOCK)
        for h in range(halves):
            normed = (c[at, half(h)] - coefs[h : h + 1, :]) * coefs[2 + h : 3 + h, :]
            normed = normed * coefs[4 + h : 5 + h, :] + coefs[6 + h : 7 + h, :]
            out[at, half(h)] = (normed * sigmoid(normed)).astype(bf16)
        return carry

    row_blocks(rows, BLOCK, body, 0)


def activate(meta, c, got, weight, n_parts):
    rows, width = c.shape
    return pl.pallas_call(
        functools.partial(act_kernel, n_parts),
        in_specs=[SM, HB, VM, VM],
        out_specs=(VM, VM),
        out_shape=(vmem_out((rows, width), bf16), vmem_out((2 * ROWS, LANES), f32)),
        scratch_shapes=stream_scratch(rows, width, BLOCK),
        compiler_params=params(12),
        cost_estimate=cost(20 * rows * width, 6 * rows * width),
        name="activate",
    )(meta, away(c), held(got), weight)


def turn_kernel(meta, images, own, other, buffer, sems):
    g = meta[1]
    rows = own.shape[0]
    block = 1024
    n = rows // block

    def copy(i, s):
        cols = pl.ds(pl.multiple_of(i * block, block), block)
        which = (1 - g, g)[s]
        return pltpu.make_async_copy(images.at[which, :, cols], buffer.at[s, :, cols], sems.at[s, i])

    for s in range(2):
        for i in range(n):
            copy(i, s).start()
    for s, out in ((0, other), (1, own)):

        def step(i, carry, s=s, out=out):
            copy(i, s).wait()
            cols = pl.ds(pl.multiple_of(i * block, block), block)
            out[cols, :] = buffer[s, :, cols].T
            return carry

        lax.fori_loop(0, n, step, 0)


def turn(meta, images):
    slots, cs, rows = images.shape
    return pl.pallas_call(
        turn_kernel,
        in_specs=[SM, HB],
        out_specs=(VM, VM),
        out_shape=(vmem_out((rows, cs), bf16),) * 2,
        scratch_shapes=[pltpu.VMEM((slots, cs, rows), bf16), pltpu.SemaphoreType.DMA((slots, rows // 1024))],
        compiler_params=params(8),
        cost_estimate=cost(1 << 20, 8 * rows * cs),
        name="turn",
    )(meta, away(images))


def join_kernel(meta, got, half_done, out, buffer, sems):
    cs, rows = got.shape
    block = 1024
    n = rows // block
    del half_done

    def copy(i):
        cols = pl.ds(pl.multiple_of(i * block, block), block)
        return pltpu.make_async_copy(buffer.at[:, cols], out.at[1 - meta[1], :, cols], sems.at[i])

    for i in range(n):
        cols = slice(i * block, (i + 1) * block)
        buffer[:, cols] = got[:, cols].astype(f32)
        copy(i).start()
    for i in range(n):
        copy(i).wait()


def join(meta, got, half_done):
    cs, rows = got.shape
    return pl.pallas_call(
        join_kernel,
        in_specs=[SM, VM, HB],
        out_specs=HB,
        out_shape=hbm_out(half_done.shape, f32),
        scratch_shapes=[pltpu.VMEM((cs, rows), f32), pltpu.SemaphoreType.DMA((rows // 1024,))],
        input_output_aliases={2: 0},
        compiler_params=params(8),
        cost_estimate=cost(1 << 20, 8 * rows * cs),
        name="join",
    )(meta, held(got), away(half_done))


def pool_kernel(n_x, meta, source, *refs):
    x, (got, weight, coefs1, labels, out, coefs, c, sems) = refs[:n_x], refs[n_x:]
    rows, width = c.shape
    halves = width // LANES
    first = meta[1] == 0
    wait = stream_in(source, c, sems, BLOCK)
    mean, scale = norm_coefs(got, weight, loss_scale)
    coefs[...] = jnp.zeros(coefs.shape, f32)
    coefs[0:2, :] = mean
    coefs[2:4, :] = scale

    def body(at, carry):
        wait(at.start // BLOCK)
        sums = list(carry)
        for h in range(halves):
            hat = (c[at, half(h)] - coefs[h : h + 1, :]) * coefs[2 + h : 3 + h, :]
            v = hat * coefs1[8 + h : 9 + h, :] + coefs1[10 + h : 11 + h, :] + part_half(x, first, at, h)
            s = sigmoid(v)
            slope = s * (1.0 + v * (1.0 - s))
            sums[3 * h] += jnp.sum(v * s, axis=0, keepdims=True)
            sums[3 * h + 1] += jnp.sum(slope * hat, axis=0, keepdims=True)
            sums[3 * h + 2] += jnp.sum(slope, axis=0, keepdims=True)
        return tuple(sums)

    sums = row_blocks(rows, BLOCK, body, (jnp.zeros((1, LANES), f32),) * (3 * halves))
    valid = meta[3].astype(f32)
    lines = [(6, labels[0:1, :]), (7, labels[1:2, :])]
    for h in range(halves):
        lines.append((h, sums[3 * h] * (valid / loss_scale)))
        lines.append((2 + h, sums[3 * h + 1]))
        lines.append((4 + h, sums[3 * h + 2]))
    send_rows(out, lines)


def pool(meta, c, x, got, weight, coefs1, labels):
    rows, width = c.shape
    return pl.pallas_call(
        functools.partial(pool_kernel, len(x)),
        in_specs=[SM, HB] + [VM] * (4 + len(x)),
        out_specs=(VM, VM),
        out_shape=(vmem_out(got.shape, f32), vmem_out((ROWS, LANES), f32)),
        scratch_shapes=stream_scratch(rows, width, BLOCK),
        compiler_params=params(12),
        cost_estimate=cost(30 * rows * width, 6 * rows * width),
        name="pool",
    )(meta, away(c), *[held(v) for v in x], held(got), weight, held(coefs1), labels)


def head_kernel(n_parts, meta, got, ht, bias, valid, avg_row, avg_col, coefs, tw, an, hwg, hbg, pooled_own, pooled, slopes, shifts, labels, grads, mine_all, pooled_part):
    tasks, channels = ht.shape
    images = valid.shape[0]
    n_task = 2 * n_parts
    width = channels // n_parts
    halves = width // LANES
    r = meta[2]
    for n in range(images):
        base = (n // 2) * n_task + (n % 2) * n_parts
        for part in range(n_parts):
            for h in range(halves):
                lo = part * width + h * LANES
                pooled[n : n + 1, lo : lo + LANES] = got[base + part, h : h + 1, :]
        for h in range(halves):
            slopes[n : n + 1, half(h)] = got[base + r, 2 + h : 3 + h, :]
            shifts[n : n + 1, half(h)] = got[base + r, 4 + h : 5 + h, :]
        row = 6 + n % 2
        lab = got[(n // 2) * n_task, row : row + 1, :]
        for t in range(1, n_task):
            lab = lab + got[(n // 2) * n_task + t, row : row + 1, :]
        labels[n : n + 1, :] = lab
    pooled_all = pooled[...]
    table = ht[...]
    both_last = (((1,), (1,)), ((), ()))
    both_first = (((0,), (0,)), ((), ()))
    logits = lax.dot_general(pooled_all, table, both_last, precision=highest, preferred_element_type=f32) + bias[...]
    count = jnp.sum(valid[...], axis=0, keepdims=True)
    errors = valid[...] * (sigmoid(logits) - labels[:, 0:tasks]) / count
    gram = lax.dot_general(errors, errors, both_first, precision=highest, preferred_element_type=f32) * lax.dot_general(
        table, table, both_last, precision=highest, preferred_element_type=f32
    )
    row_id = lax.broadcasted_iota(jnp.int32, (tasks, tasks), 0)
    col_id = lax.broadcasted_iota(jnp.int32, (tasks, tasks), 1)
    trace = jnp.sum(jnp.sum(jnp.where(row_id == col_id, gram, 0.0), axis=1, keepdims=True), axis=0, keepdims=True)
    normalized = gram / (trace / tasks)
    start_row = avg_row[...] / jnp.sum(avg_row[...], axis=1, keepdims=True)
    start_col = avg_col[...] / jnp.sum(avg_col[...], axis=0, keepdims=True)
    w_row, w_col = start_row, start_col
    for j in range(FW_STEPS):
        rate = 1.0 / (j + 4.0)
        z_col = -tasks * jnp.sum(normalized * w_row, axis=1, keepdims=True)
        z_row = -tasks * jnp.sum(normalized * w_col, axis=0, keepdims=True)
        e_col = jnp.exp(z_col - jnp.max(z_col, axis=0, keepdims=True))
        e_row = jnp.exp(z_row - jnp.max(z_row, axis=1, keepdims=True))
        w_col = (1.0 - rate) * w_col + rate * (e_col / jnp.sum(e_col, axis=0, keepdims=True))
        w_row = (1.0 - rate) * w_row + rate * (e_row / jnp.sum(e_row, axis=1, keepdims=True))
    tw[...] = w_row
    an[...] = 0.9 * start_row + 0.1 * w_row
    logit_grads = errors * ((loss_scale * tasks) * w_row)
    hbg[...] = jnp.sum(logit_grads, axis=0, keepdims=True)
    hwg[...] = lax.dot_general(logit_grads, pooled_all, both_first, precision=highest, preferred_element_type=f32)
    grads[...] = jnp.dot(logit_grads, table, precision=highest, preferred_element_type=f32) / loss_scale
    own = pl.ds(pl.multiple_of(r * width, LANES), width)
    q = grads[:, own]
    mine_all[...] = q
    pooled_part[...] = pooled[:, own]
    gain = jnp.sum(q * slopes[...], axis=0, keepdims=True)
    shift = jnp.sum(q * shifts[...], axis=0, keepdims=True)
    mine = mine_all[pl.ds(2 * meta[0] + meta[1], 1), :]
    coefs[...] = jnp.zeros(coefs.shape, f32)
    for h in range(halves):
        coefs[h : h + 1, :] = gain[:, half(h)]
        coefs[2 + h : 3 + h, :] = shift[:, half(h)]
        coefs[4 + h : 5 + h, :] = mine[:, half(h)]
    for i in range(2):
        pooled_own[i : i + 1, :] = pooled_part[pl.ds(2 * meta[0] + i, 1), :]


def head(meta, got, ht, bias, valid, avg_row, avg_col, n_parts):
    tasks, channels = ht.shape
    images = valid.shape[0]
    width = channels // n_parts
    shapes = [(ROWS, LANES), (1, tasks), (1, tasks), (tasks, channels), (1, tasks), (2, width)]
    return pl.pallas_call(
        functools.partial(head_kernel, n_parts),
        in_specs=[SM] + [VM] * 6,
        out_specs=tuple(VM for _ in shapes),
        out_shape=tuple(jax.ShapeDtypeStruct(s, f32) for s in shapes),
        scratch_shapes=[
            pltpu.VMEM((images, channels), f32),
            pltpu.VMEM((images, width), f32),
            pltpu.VMEM((images, width), f32),
            pltpu.VMEM((images, LANES), f32),
            pltpu.VMEM((images, channels), f32),
            pltpu.VMEM((images, width), f32),
            pltpu.VMEM((images, width), f32),
        ],
        compiler_params=params(60),
        cost_estimate=cost(1 << 20, 1 << 20),
        name="head",
    )(meta, got, ht, bias, valid, avg_row, avg_col)


def grad_two_kernel(n_x, meta, source, *refs):
    x, (coefs, coefs1, heads, pixels, low, target, c, sems, summed, out_sems) = refs[:n_x], refs[n_x:]
    rows, width = c.shape
    valid = meta[3].astype(f32)
    first = meta[1] == 0
    wait = stream_in(source, c, sems, BLOCK)
    send, finish = stream_out(summed, target, out_sems, BLOCK)

    def body(at, carry):
        wait(at.start // BLOCK)
        for h in range(width // LANES):
            mean, scale = coefs[h : h + 1, :], coefs[2 + h : 3 + h, :]
            gain = coefs1[8 + h : 9 + h, :]
            hat = (c[at, half(h)] - mean) * scale
            v = hat * gain + coefs1[10 + h : 11 + h, :] + part_half(x, first, at, h)
            dn = (valid * heads[4 + h : 5 + h, :]) * silu_slope(v)
            summed[at, half(h)] = dn
            away = (heads[2 + h : 3 + h, :] + hat * heads[h : h + 1, :]) / pixels[0]
            low[at, half(h)] = ((valid * gain * scale) * (dn - away)).astype(bf16)
        send(at.start // BLOCK)
        return carry

    row_blocks(rows, BLOCK, body, 0)
    finish()


def grad_two(meta, c, x, coefs, coefs1, heads, pixels):
    rows, width = c.shape
    return pl.pallas_call(
        functools.partial(grad_two_kernel, len(x)),
        in_specs=[SM, HB] + [VM] * (3 + len(x)) + [SM],
        out_specs=(VM, HB),
        out_shape=(vmem_out((rows, width), bf16), hbm_out((rows, width), f32)),
        scratch_shapes=stream_scratch(rows, width, BLOCK) * 2,
        compiler_params=params(16),
        cost_estimate=cost(30 * rows * width, 12 * rows * width),
        name="grad_two",
    )(meta, away(c), *[held(v) for v in x], held(coefs), held(coefs1), held(heads), pixels)


def grad_one_kernel(meta, c_source, dn_source, got, weight, coefs, pixels, low, sums, c, c_sems, dn, dn_sems):
    rows, width = c.shape
    valid = meta[3].astype(f32)
    wait_c = stream_in(c_source, c, c_sems, BLOCK)
    wait_dn = stream_in(dn_source, dn, dn_sems, BLOCK)
    sums[...] = weighted(got, weight)

    def body(at, carry):
        wait_c(at.start // BLOCK)
        wait_dn(at.start // BLOCK)
        for h in range(width // LANES):
            mean, scale = coefs[h : h + 1, :], coefs[2 + h : 3 + h, :]
            hat = (c[at, half(h)] - mean) * scale
            away = (sums[2 + h : 3 + h, :] + hat * sums[h : h + 1, :]) / pixels[0]
            low[at, half(h)] = ((valid * coefs[4 + h : 5 + h, :] * scale) * (dn[at, half(h)] - away)).astype(bf16)
        return carry

    row_blocks(rows, BLOCK, body, 0)


def grad_one(meta, c, dn, got, weight, coefs, pixels):
    rows, width = c.shape
    return pl.pallas_call(
        grad_one_kernel,
        in_specs=[SM, HB, HB] + [VM] * 3 + [SM],
        out_specs=(VM, VM),
        out_shape=(vmem_out((rows, width), bf16), vmem_out((ROWS, LANES), f32)),
        scratch_shapes=stream_scratch(rows, width, BLOCK) * 2,
        compiler_params=params(16),
        cost_estimate=cost(10 * rows * width, 10 * rows * width),
        name="grad_one",
    )(meta, away(c), away(dn), held(got), weight, held(coefs), pixels)


def back_setup(gs, scratch, copies, rows, width):
    clear_ends(scratch, rows)
    place_columns(scratch, [(g, slice(0, width), i * width) for i, g in enumerate(gs)], SIDE)
    for c in copies:
        c.wait()


def back_products(scratch, w, at, chunk):
    total = None
    for dx in (0, 1, -1):
        acc = None
        for dy in (-1, 0, 1):
            lhs = scratch[pl.ds(pl.multiple_of(at + SIDE * (1 - dy), SIDE), chunk), :]
            term = jnp.dot(lhs, w[3 * (dy + 1) + dx + 1], preferred_element_type=f32)
            acc = term if acc is None else acc + term
        acc = moved(acc, -dx)
        total = acc if total is None else total + acc
    return total


def back_two_kernel(n_parts, n_pieces, meta, *refs):
    pieces, gs, refs = refs[:n_pieces], refs[n_pieces : n_pieces + n_parts], refs[n_pieces + n_parts :]
    source, coefs, target, stats, scratch, w, sems, c, c_sems, out, out_sems = refs
    rows, width = out.shape
    halves = width // LANES
    chunk = CHUNK
    push, finish = stream_out(out, target, out_sems, chunk)
    copies = backward_copies(meta, pieces, w, width // 2, n_parts, sems)
    for copy in copies:
        copy.start()
    wait = stream_in(source, c, c_sems, chunk)
    back_setup(gs, scratch, copies, rows, width)

    def step(j, carry):
        at = pl.multiple_of(j * chunk, chunk)
        acc = back_products(scratch, w, at, chunk)
        wait(j)
        sums = []
        for h in range(halves):
            hat = (c[pl.ds(at, chunk), half(h)] - coefs[h : h + 1, :]) * coefs[2 + h : 3 + h, :]
            dn = acc[:, half(h)] * silu_slope(hat * coefs[4 + h : 5 + h, :] + coefs[6 + h : 7 + h, :])
            out[pl.ds(at, chunk), half(h)] = dn
            sums.append(carry[2 * h] + jnp.sum(dn * hat, axis=0, keepdims=True))
            sums.append(carry[2 * h + 1] + jnp.sum(dn, axis=0, keepdims=True))
        push(j)
        return tuple(sums)

    zero = jnp.zeros((1, LANES), f32)
    sums = lax.fori_loop(0, rows // chunk, step, (zero,) * (2 * halves))
    send_rows(stats, [(2 * i + h, sums[2 * h + i]) for h in range(halves) for i in range(2)])
    finish()


def back_scratch(rows, width, n):
    return [
        pltpu.VMEM((rows + 2 * SIDE, n * width), bf16),
        pltpu.VMEM((9, n * width, width), bf16),
        pltpu.SemaphoreType.DMA((10 * n,)),
    ]


def back_two(meta, pieces, g_parts, c, coefs, n_devices):
    rows, width = c.shape
    n = len(g_parts)
    return pl.pallas_call(
        functools.partial(back_two_kernel, n, len(pieces)),
        in_specs=[SM] + [HB] * len(pieces) + [VM] * n + [HB, VM],
        out_specs=(HB, VM),
        out_shape=(hbm_out((rows, width), f32), vmem_out((n_devices, ROWS, LANES), f32)),
        scratch_shapes=back_scratch(rows, width, n) + stream_scratch(rows, width, CHUNK) * 2,
        compiler_params=params(28),
        cost_estimate=cost(2 * 9 * rows * width * width * n, 16 << 20),
        name="back_two",
    )(meta, *[away(v) for v in pieces], *[held(v) for v in g_parts], away(c), held(coefs))


def back_one_kernel(n_parts, n_pieces, meta, *refs):
    pieces, gs, refs = refs[:n_pieces], refs[n_pieces : n_pieces + n_parts], refs[n_pieces + n_parts :]
    source, out, send, scratch, w, sems, keep, keep_sems, summed, in_sems = refs
    rows, width = summed.shape
    cs = width // 2
    chunk = CHUNK
    g = meta[1]
    copies = backward_copies(meta, pieces, w, cs, n_parts, sems)
    for c in copies:
        c.start()
    wait = stream_in(source, summed, in_sems, chunk)
    first = g == 0
    back_setup(gs, scratch, copies, rows, width)

    def copy(j):
        cols = pl.ds(pl.multiple_of(j * chunk, chunk), chunk)
        return pltpu.make_async_copy(keep.at[:, cols], out.at[g, :, cols], keep_sems.at[j])

    def step(j, carry):
        at = pl.multiple_of(j * chunk, chunk)
        acc = back_products(scratch, w, at, chunk)
        wait(j)
        acc = acc + summed[pl.ds(at, chunk), :]
        a, b = acc[:, :cs], acc[:, cs:]
        keep[:, pl.ds(at, chunk)] = jnp.where(first, a, b).T
        copy(j).start()
        send[:, pl.ds(at, chunk)] = jnp.where(first, b, a).T.astype(bf16)
        return carry

    lax.fori_loop(0, rows // chunk, step, 0)
    for j in range(rows // chunk):
        copy(j).wait()


def back_one(meta, pieces, g_parts, summed):
    rows, width = summed.shape
    n = len(g_parts)
    cs = width // 2
    return pl.pallas_call(
        functools.partial(back_one_kernel, n, len(pieces)),
        in_specs=[SM] + [HB] * len(pieces) + [VM] * n + [HB],
        out_specs=(HB, VM),
        out_shape=(hbm_out((2, cs, rows), f32), vmem_out((cs, rows), bf16)),
        scratch_shapes=back_scratch(rows, width, n)
        + [pltpu.VMEM((cs, rows), f32), pltpu.SemaphoreType.DMA((rows // CHUNK,))]
        + stream_scratch(rows, width, CHUNK),
        compiler_params=params(28),
        cost_estimate=cost(2 * 9 * rows * width * width * n, 16 << 20),
        name="back_one",
    )(meta, *[away(v) for v in pieces], *[held(v) for v in g_parts], away(summed))


def weight_kernel(sizes, n_parts, taps, meta, g, *refs):
    n = sum(sizes)
    xs, (keep_out, send_out, shifted, x, keep, send, sems) = refs[:n], refs[n:]
    rows, width = g.shape
    cs = width // 2
    first = meta[1] == 0
    parts, at = [], 0
    for size in sizes:
        parts.append(xs[at : at + size])
        at += size
    place_columns(x, column_plan(meta, parts, n_parts, cs), 0)
    moves = sorted({1 - k % 3 for k in taps})
    for i in range(len(moves)):
        clear_ends(shifted.at[i], rows)

    def shift(at, carry):
        low = g[at, :]
        value = low.astype(f32)
        to = pl.ds(pl.multiple_of(at.start + SIDE, SIDE), at.size)
        for i, e in enumerate(moves):
            shifted[i, to, :] = moved(value, e).astype(bf16) if e else low
        return carry

    row_blocks(rows, BLOCK, shift, 0)

    def copies(j):
        pairs = ((send, send_out), (keep, keep_out))
        return [pltpu.make_async_copy(v.at[j], to.at[j], sems.at[i, j]) for i, (v, to) in enumerate(pairs)]

    for j, k in enumerate(taps):
        lo = SIDE * (2 - k // 3)
        lhs = shifted[moves.index(1 - k % 3), lo : lo + rows, :]
        term = lax.dot_general(lhs, x[...], (((0,), (0,)), ((), ())), preferred_element_type=f32)
        a, b = term[:cs], term[cs:]
        keep[j] = jnp.where(first, a, b)
        send[j] = jnp.where(first, b, a).astype(bf16)
        for c in copies(j):
            c.start()
    for j in range(len(taps)):
        for c in copies(j):
            c.wait()


def weight_grad(meta, g, parts, n_parts, taps):
    rows, width = g.shape
    flat = [v for p in parts for v in p]
    columns = n_parts * width
    shape = (len(taps), width // 2, columns)
    return pl.pallas_call(
        functools.partial(weight_kernel, [len(p) for p in parts], n_parts, taps),
        in_specs=[SM] + [VM] * (len(flat) + 1),
        out_specs=(HB, HB),
        out_shape=(hbm_out(shape, f32), hbm_out(shape, bf16)),
        scratch_shapes=[
            pltpu.VMEM((len({k % 3 for k in taps}), rows + 2 * SIDE, width), bf16),
            pltpu.VMEM((rows, columns), bf16),
            pltpu.VMEM(shape, f32),
            pltpu.VMEM(shape, bf16),
            pltpu.SemaphoreType.DMA((2, len(taps))),
        ],
        compiler_params=params(28),
        cost_estimate=cost(2 * len(taps) * rows * width * columns, 16 << 20),
        name="weight_grad",
    )(meta, held(g), *[held(v) for v in flat])


def swap(values, axis, by):
    n = lax.axis_size(axis)
    return lax.ppermute(values, axis, [(i, i ^ by) for i in range(n)])


def xor_order(values, r):
    bit = 1
    while bit < len(values):
        flip = (r & bit) != 0
        values = [jnp.where(flip, values[i ^ bit], v) for i, v in enumerate(values)]
        bit *= 2
    return values


def gate(values, *others):
    return lax.optimization_barrier((values, *others))[0]


def scatter_split(total, stage, kind):
    stride, size = stage
    k = (lax.axis_index("batch") // stride) % size
    split = total.reshape(size, -1, total.shape[1])
    mine = lax.dynamic_index_in_dim(split, k, keepdims=False)
    return mine, [lax.dynamic_index_in_dim(split, k ^ j, keepdims=False).astype(kind) for j in range(1, size)]


def scatter_move(sent, stage):
    return [swap(v, "batch", stage[0] * j) for j, v in enumerate(sent, 1)]


def scatter_add(mine, got, *after):
    for v in got:
        mine = mine + gate(v, *after).astype(f32)
    return mine


def gather_move(out, stage):
    return [swap(out, "batch", stage[0] * j) for j in range(1, stage[1])]


def gather_join(out, got, stage, *after):
    k = (lax.axis_index("batch") // stage[0]) % stage[1]
    return jnp.concatenate(xor_order([out] + [gate(v, *after) for v in got], k), axis=0)


def on_device(
    images,
    conv1_weight,
    norm1_gain,
    norm1_bias,
    conv2_weight,
    norm2_gain,
    norm2_bias,
    head_weight,
    head_bias,
    labels,
    image_counts,
    average_weights,
):
    n_task, n_batch = lax.axis_size("task"), lax.axis_size("batch")
    t, b = lax.axis_index("task"), lax.axis_index("batch")
    slots, cs, pixels = images.shape
    n_parts = n_task // slots
    g, r = t // n_parts, t % n_parts
    first = g == 0
    width = slots * cs
    channels = n_task * cs
    n_devices = n_task * n_batch
    tasks_here = head_weight.shape[1]
    tasks = tasks_here * n_task

    valid_images = (jnp.arange(slots)[None, :] < image_counts[:, None]).astype(f32)
    image_total = jnp.sum(image_counts).astype(f32)
    pixel_total = (image_total * pixels).reshape(1)
    own_valid = (g < lax.dynamic_index_in_dim(image_counts, b, keepdims=False)).astype(jnp.int32)
    place = jnp.stack([b, g, r, 0 * b, b % 4]).astype(jnp.int32)
    meta = jnp.stack([b, g, r, own_valid, b % 4]).astype(jnp.int32)
    same = (jnp.arange(n_parts) == r).astype(f32)
    weight = (valid_images[:, :, None] * same[None, None, :]).reshape(n_devices, 1)
    weight = jnp.broadcast_to(weight[:, :, None], (n_devices, ROWS, LANES))

    def relative(w):
        blocks = [w[..., i * cs : (i + 1) * cs] for i in range(n_task)]
        order = [xor_order(blocks[s * n_parts : (s + 1) * n_parts], r) for s in range(slots)]
        return [jnp.concatenate([order[s][i] for s in range(slots)], axis=-1) for i in range(n_parts)]

    def ordered(own, other, axis):
        return jnp.concatenate([jnp.where(first, own, other), jnp.where(first, other, own)], axis=axis)

    def joined(pieces):
        other = jnp.concatenate(xor_order(list(pieces[1:]), b % 4 if len(pieces) > 2 else 0), axis=1)
        return relative(ordered(pieces[0], other, 1))

    def forward_pieces(pieces):
        return pieces if aligned(cs) else [jnp.concatenate(joined(pieces), axis=2)]

    def backward_pieces(pieces):
        if aligned(cs):
            return [swap(v, "task", i) if i else v for i in range(n_parts) for v in pieces]
        return [swap(v, "task", i) if i else v for i, v in enumerate(joined(pieces))]

    def all_parts(v):
        return [v] + [swap(v, "task", i) for i in range(1, n_parts)]

    near_sent = lax.dynamic_index_in_dim(
        conv1_weight.reshape(9, 4, cs // 4, channels), b % 4, axis=1, keepdims=False
    )
    near = swap(near_sent, "task", n_parts)

    head_bias, head_weight = gate(head_bias, near_sent), gate(head_weight, near_sent)
    lines = jnp.pad(head_bias, (0, channels - tasks_here)).reshape(1, channels)
    mine = jnp.concatenate([head_weight.T.astype(f32), lines])
    mine = jnp.pad(mine, ((0, -mine.shape[0] % ROWS), (0, 0)))
    every = xor_order([mine] + [swap(mine, "task", i) for i in range(1, n_task)], t)
    table = jnp.concatenate([v[:tasks_here] for v in every])
    table = table.reshape(tasks, slots, n_parts, cs).swapaxes(1, 2).reshape(tasks, channels)
    bias_row = jnp.concatenate([v[tasks_here, :tasks_here] for v in every]).reshape(1, tasks)
    vecs = jnp.stack([norm1_gain, norm1_bias, norm2_gain, norm2_bias])
    vecs = jnp.pad(vecs, ((4, 0), (0, LANES - cs)))
    label_rows = lax.dynamic_update_slice(
        jnp.zeros((slots, LANES), f32), labels.astype(f32), (0, t * tasks_here)
    )
    columns = [label_rows, vecs, valid_images.reshape(-1, 1), average_weights.reshape(-1, 1)]

    x_own, x_send = turn(place, images)
    near = gate(near, x_send)
    x_other = swap(gate(x_send, near), "task", n_parts)
    side = swap(near, "batch", 1)
    w1 = [conv1_weight, near, side, swap(near, "batch", 2), swap(side, "batch", 2)]
    w2 = [conv2_weight, swap(gate(conv2_weight, near), "task", n_parts)]
    if aligned(cs):
        x_parts = list(zip(all_parts(x_own), all_parts(gate(x_other, *w1, table, bias_row, weight, *columns))))
    else:
        x_parts = [[v] for v in all_parts(ordered(x_own, x_other, 1))]

    def exchange(rows):
        flat_rows = rows.reshape(n_devices * ROWS, LANES)
        return lax.all_to_all(flat_rows, ("batch", "task"), 0, 0, tiled=True).reshape(rows.shape)

    c1, stats = conv_stats(meta, vecs, forward_pieces(w1), x_parts, cs, n_devices, 0)
    a_own, coefs1 = activate(meta, c1, exchange(gate(stats, w2[1])), weight, n_parts)
    a_parts = [[v] for v in all_parts(a_own)]
    c2, stats = conv_stats(meta, vecs, forward_pieces(w2), a_parts, cs, n_devices, 18)
    sums, coefs2 = pool(meta, c2, x_parts[0], exchange(stats), weight, coefs1, label_rows)
    heads, task_weights, average_next, head_grad, bias_grad, pooled_rows = head(
        meta,
        exchange(sums),
        table,
        bias_row,
        columns[2],
        average_weights.reshape(1, -1),
        columns[3],
        n_parts,
    )

    def both_groups(keep, got, *after):
        return (keep + gate(got, *after).astype(f32)).reshape(-1, channels)

    def assemble(done, taps):
        where = {k: (v, j) for v, ks in zip(done, taps) for j, k in enumerate(ks)}
        out = jnp.concatenate([where[k][0][where[k][1] * cs : (where[k][1] + 1) * cs] for k in range(9)])
        out = out.reshape(9, cs, channels)
        if not aligned(cs):
            parts = [out[:, :, i * width : (i + 1) * width] for i in range(n_parts)]
            order = [v for s in range(slots) for v in xor_order([p[:, :, s * cs : (s + 1) * cs] for p in parts], r)]
            out = jnp.concatenate(order, axis=2)
        return out.astype(f32)

    bits = n_batch.bit_length() - 1
    near = 1 << (bits // 2)
    one, two = (1, near), (near, n_batch // near)
    every_tap, taps_a, taps_b = tuple(range(9)), (0, 3, 6, 1), (4, 7, 2, 5, 8)
    low2, summed = grad_two(meta, c2, x_parts[0], coefs2, coefs1, heads, pixel_total)
    low2_parts = all_parts(low2)
    keep2, send2 = weight_grad(meta, low2, a_parts, n_parts, every_tap)
    got2 = swap(send2, "task", n_parts)
    low2_parts[0] = gate(low2_parts[0], keep2)
    dn1, stats = back_two(meta, backward_pieces(w2), low2_parts, c1, coefs1, n_devices)
    low1, sums1 = grad_one(meta, c1, dn1, exchange(stats), weight, coefs1, pixel_total)
    low1_parts = all_parts(low1)

    mine2, sent2 = scatter_split(both_groups(keep2, got2, low1), one, bf16)
    got2 = scatter_move(sent2, one)
    keep_a, send_a = weight_grad(meta, gate(low1, *sent2), x_parts, n_parts, taps_a)
    got_a = swap(send_a, "task", n_parts)
    keep_b, send_b = weight_grad(meta, gate(low1, keep_a), x_parts, n_parts, taps_b)
    got_b = swap(send_b, "task", n_parts)
    mine2, sent2 = scatter_split(scatter_add(mine2, got2, keep_b), two, f32)
    got2 = scatter_move(sent2, two)
    low1_parts[0] = gate(low1_parts[0], *sent2)
    half_done, send = back_one(meta, backward_pieces(w1), low1_parts, summed)
    got = swap(send, "task", n_parts)
    mine_a, sent_a = scatter_split(both_groups(keep_a, got_a, send), one, bf16)
    got_a = scatter_move(sent_a, one)
    mine_b, sent_b = scatter_split(both_groups(keep_b, got_b, *sent_a), one, bf16)
    got_b = scatter_move(sent_b, one)
    sum2 = scatter_add(mine2, got2, *sent_b).astype(bf16)
    got2 = gather_move(sum2, two)
    mine_a, sent_a = scatter_split(scatter_add(mine_a, got_a, sum2), two, bf16)
    got_a = scatter_move(sent_a, two)
    mine_b, sent_b = scatter_split(scatter_add(mine_b, got_b, *sent_a), two, bf16)
    got_b = scatter_move(sent_b, two)
    sum2 = gather_join(sum2, got2, two, *sent_b)
    got2 = gather_move(sum2, one)
    sum_a = scatter_add(mine_a, got_a, sum2).astype(bf16)
    got_a = gather_move(sum_a, two)
    sum_b = scatter_add(mine_b, got_b, sum_a).astype(bf16)
    got_b = gather_move(sum_b, two)
    sum_a = gather_join(sum_a, got_a, two, sum_b, got)
    got_a = gather_move(sum_a, one)
    sum_b = gather_join(sum_b, got_b, two, sum_a)
    got_b = gather_move(sum_b, one)
    input_grad = join(meta, gate(got, sum_b), half_done)
    conv2_grad = assemble([gather_join(sum2, got2, one, input_grad)], [every_tap])
    sum_a = gather_join(sum_a, got_a, one, conv2_grad)
    sum_b = gather_join(sum_b, got_b, one, sum_a)
    conv1_grad = assemble([sum_a, sum_b], [taps_a, taps_b])

    def own_slice(rows, at):
        line = rows[at : at + 2].reshape(-1)
        return lax.dynamic_slice_in_dim(line, g * cs, cs)

    head_weight_grad = lax.dynamic_slice_in_dim(head_grad, t * tasks_here, tasks_here, axis=0)
    head_weight_grad = head_weight_grad.reshape(tasks_here, n_parts, slots, cs).swapaxes(1, 2)
    head_weight_grad = head_weight_grad.reshape(tasks_here, channels).T
    head_bias_grad = lax.dynamic_slice_in_dim(bias_grad[0], t * tasks_here, tasks_here)
    pooled = lax.dynamic_slice_in_dim(pooled_rows, g * cs, cs, axis=1)
    return (
        pooled,
        input_grad,
        conv1_grad,
        own_slice(sums1, 0),
        own_slice(sums1, 2),
        conv2_grad,
        own_slice(heads, 0),
        own_slice(heads, 2),
        head_weight_grad,
        head_bias_grad,
        task_weights[0],
        average_next[0],
    )


def solution(mesh):
    in_specs = (
        P("batch", "task", None),
        P(None, "task", None),
        P("task"),
        P("task"),
        P(None, "task", None),
        P("task"),
        P("task"),
        P(None, "task"),
        P("task"),
        P("batch", "task"),
        P(),
        P(),
    )
    out_specs = (
        P("batch", "task"),
        P("batch", "task", None),
        P(None, "task", None),
        P("task"),
        P("task"),
        P(None, "task", None),
        P("task"),
        P("task"),
        P(None, "task"),
        P("task"),
        P(),
        P(),
    )
    return jax.shard_map(
        on_device, mesh=mesh, in_specs=in_specs, out_specs=out_specs, check_vma=False
    )
```

```python
import functools

import jax
import jax.numpy as jnp
from jax import lax
from jax.experimental import pallas as pl
from jax.experimental.pallas import tpu as pltpu
from jax.sharding import PartitionSpec as P

SIDE = 64
FW_STEPS = 20
LANES = 128
ROWS = 8

eps = 1e-05
loss_scale = 4096.0
highest = lax.Precision.HIGHEST
f32 = jnp.float32
bf16 = jnp.bfloat16


def params(mib, **more):
    return pltpu.CompilerParams(vmem_limit_bytes=mib << 20, **more)


def cost(flops, moved):
    return pl.CostEstimate(flops=flops, bytes_accessed=moved, transcendentals=0)


VM = pl.BlockSpec(memory_space=pltpu.VMEM)
HB = pl.BlockSpec(memory_space=pl.ANY)
SM = pl.BlockSpec(memory_space=pltpu.SMEM)


def sigmoid(v):
    return 0.5 + 0.5 * jnp.tanh(0.5 * v)


def silu_slope(v):
    s = sigmoid(v)
    return s * (1.0 + v * (1.0 - s))


def half(h):
    return slice(h * LANES, (h + 1) * LANES)


def held(values):
    return pltpu.with_memory_space_constraint(values, pltpu.VMEM)


def away(values):
    return pltpu.with_memory_space_constraint(values, pltpu.HBM)


def vmem_out(shape, kind):
    return pltpu.VMEM(shape, kind)


def hbm_out(shape, kind):
    return pltpu.HBM(shape, kind)


def column_is(rows, width, at):
    return (lax.broadcasted_iota(jnp.int32, (rows, width), 0) & (SIDE - 1)) == at


def moved(v, e):
    rows, width = v.shape
    if e == 0:
        return v
    edge = SIDE - 1 if e == 1 else 0
    return jnp.where(column_is(rows, width, edge), 0.0, pltpu.roll(v, rows - 1 if e == 1 else 1, 0))


def aligned(cs):
    return cs % LANES == 0


def column_plan(meta, parts, n_parts, cs):
    g, r = meta[1], meta[2]
    plan = []
    for i, part in enumerate(parts):
        if not aligned(cs):
            plan.append((part[0], slice(0, 2 * cs), i * 2 * cs))
            continue
        for s in range(2):
            place = s * n_parts + (r ^ i) if len(part) == 1 else (g, 1 - g)[s] * n_parts + (r ^ i)
            ref, cols = (part[0], slice(s * cs, (s + 1) * cs)) if len(part) == 1 else (part[s], slice(0, cs))
            plan.append((ref, cols, pl.multiple_of(place * cs, cs)))
    return plan


def place_columns(dst, plan, first_row):
    rows = plan[0][0].shape[0]
    block = 512

    def step(j, carry):
        at = pl.multiple_of(j * block, block)
        for ref, cols, to in plan:
            width = cols.stop - cols.start
            dst[pl.ds(pl.multiple_of(at + first_row, SIDE), block), pl.ds(to, width)] = ref[pl.ds(at, block), cols]
        return carry

    lax.fori_loop(0, rows // block, step, 0)


def clear_ends(dst, rows):
    zero = jnp.zeros((SIDE, dst.shape[1]), dst.dtype)
    dst[0:SIDE, :] = zero
    dst[SIDE + rows : SIDE + rows + SIDE, :] = zero


def piece_rows(meta, cs, base, n_pieces):
    g, q = meta[1], meta[4]
    qs = cs // (n_pieces - 1)
    return [pl.ds(pl.multiple_of(base + g * cs, cs), cs)] + [
        pl.ds(pl.multiple_of(base + (1 - g) * cs + (q ^ i if n_pieces > 2 else 0) * qs, qs), qs)
        for i in range(n_pieces - 1)
    ]


def forward_copies(meta, pieces, w, cs, sems):
    if not aligned(cs):
        return [pltpu.make_async_copy(pieces[0], w, sems.at[0])]
    spots = piece_rows(meta, cs, 0, len(pieces))
    return [pltpu.make_async_copy(p, w.at[:, to, :], sems.at[i]) for i, (p, to) in enumerate(zip(pieces, spots))]


def backward_copies(meta, pieces, w, cs, n_parts, sems):
    width = 2 * cs
    if not aligned(cs):
        return [
            pltpu.make_async_copy(p, w.at[:, pl.ds(i * width, width), :], sems.at[i]) for i, p in enumerate(pieces)
        ]
    copies = []
    for i in range(n_parts):
        each = len(pieces) // n_parts
        for p, to in zip(pieces[each * i : each * (i + 1)], piece_rows(meta, cs, i * width, each)):
            for s in range(2):
                cols = pl.ds(pl.multiple_of((s * n_parts + meta[2]) * cs, cs), cs)
                copies.append(
                    pltpu.make_async_copy(p.at[:, :, cols], w.at[:, to, pl.ds(s * cs, cs)], sems.at[len(copies)])
                )
    return copies


def part_half(part, first, rows, h):
    if len(part) == 1:
        return part[0][rows, half(h)].astype(f32)
    own, other = part[0][rows, :], part[1][rows, :]
    return (jnp.where(first, own, other) if h == 0 else jnp.where(first, other, own)).astype(f32)


def row_blocks(rows, block, body, start):
    def step(j, carry):
        return body(pl.ds(pl.multiple_of(j * block, block), block), carry)

    return lax.fori_loop(0, rows // block, step, start)


def send_rows(out, rows, base=None):
    n = out.shape[0]
    start = jnp.zeros((ROWS, LANES), f32) if base is None else base
    out[...] = jnp.broadcast_to(start[None], out.shape)
    for at, value in rows:
        out[:, at : at + 1, :] = jnp.broadcast_to(value[None], (n, 1, LANES))


def weighted(got, weight):
    return jnp.sum(got[...] * weight[...], axis=0)


def norm_coefs(got, weight, rows):
    w = weight[...]
    values = got[...]
    count = jnp.sum(w, axis=0)
    total = jnp.sum(values * w, axis=0)
    mean = total / count
    off = values - mean[None]
    apart = jnp.sum(off * off * w, axis=0)
    squares = total[2:4] + rows * apart[0:2]
    return mean[0:2], lax.rsqrt(squares / (count[0:2] * rows) + eps)


def stream_in(source, buffer, sems, block):
    rows = buffer.shape[0]

    def copy(j):
        at = pl.ds(pl.multiple_of(j * block, block), block)
        return pltpu.make_async_copy(source.at[at, :], buffer.at[at, :], sems.at[j])

    for j in range(rows // block):
        copy(j).start()
    return lambda j: copy(j).wait()


def stream_out(buffer, target, sems, block):
    rows = buffer.shape[0]

    def copy(j):
        at = pl.ds(pl.multiple_of(j * block, block), block)
        return pltpu.make_async_copy(buffer.at[at, :], target.at[at, :], sems.at[j])

    def finish():
        for j in range(rows // block):
            copy(j).wait()

    return (lambda j: copy(j).start()), finish


def stream_scratch(rows, width, block):
    return [pltpu.VMEM((rows, width), f32), pltpu.SemaphoreType.DMA((rows // block,))]


BLOCK = 512
CHUNK = 1024


def fetch_kernel(n_pieces, cs, meta, *refs):
    pieces, (w, sems) = refs[:n_pieces], refs[n_pieces:]
    copies = forward_copies(meta, pieces, w, cs, sems)
    for c in copies:
        c.start()
    for c in copies:
        c.wait()


def fetch(meta, pieces, cs):
    shape = (9, 2 * cs, pieces[0].shape[2])
    return pl.pallas_call(
        functools.partial(fetch_kernel, len(pieces), cs),
        in_specs=[SM] + [HB] * len(pieces),
        out_specs=VM,
        out_shape=vmem_out(shape, bf16),
        scratch_shapes=[pltpu.SemaphoreType.DMA((len(pieces),))],
        compiler_params=params(2),
        name="fetch",
    )(meta, *[away(v) for v in pieces])


def conv_kernel(parts_of, n_parts, meta, extra, w, *refs):
    n = sum(parts_of)
    xs, (target, stats, scratch, out, out_sems) = refs[:n], refs[n:]
    parts, at = [], 0
    for size in parts_of:
        parts.append(xs[at : at + size])
        at += size
    rows, width = out.shape
    cs = width // 2
    chunk = CHUNK
    send, finish = stream_out(out, target, out_sems, chunk)
    clear_ends(scratch, rows)
    place_columns(scratch, column_plan(meta, parts, n_parts, cs), SIDE)
    mean = squares = jnp.zeros((1, width), f32)
    for j in range(rows // chunk):
        at = slice(j * chunk, (j + 1) * chunk)
        total = None
        for dx in (0, 1, -1):
            acc = None
            for dy in (-1, 0, 1):
                lo = at.start + SIDE * (dy + 1)
                tap = w[3 * (dy + 1) + dx + 1]
                term = lax.dot_general(
                    scratch[lo : lo + chunk, :], tap, (((1,), (1,)), ((), ())), preferred_element_type=f32
                )
                acc = term if acc is None else acc + term
            acc = moved(acc, dx)
            total = acc if total is None else total + acc
        out[at, :] = total
        send(j)
        here = jnp.sum(total, axis=0, keepdims=True) / chunk
        off = out[at, :] - here
        spread = jnp.sum(off * off, axis=0, keepdims=True)
        gap = here - mean
        mean = mean + gap / (j + 1.0)
        squares = squares + spread + gap * gap * (chunk * j / (j + 1.0))
    send_rows(
        stats,
        [(h, mean[:, half(h)]) for h in range(width // LANES)]
        + [(2 + h, squares[:, half(h)]) for h in range(width // LANES)],
        extra[...],
    )
    finish()


def conv_stats(meta, extra, w, parts, cs, n_devices, flops):
    rows, width, channels = parts[0][0].shape[0], 2 * cs, w.shape[2]
    flat = [v for part in parts for v in part]
    return pl.pallas_call(
        functools.partial(conv_kernel, [len(p) for p in parts], len(parts)),
        in_specs=[SM, VM, VM] + [VM] * len(flat),
        out_specs=(HB, VM),
        out_shape=(hbm_out((rows, width), f32), vmem_out((n_devices, ROWS, LANES), f32)),
        scratch_shapes=[pltpu.VMEM((rows + 2 * SIDE, channels), bf16), *stream_scratch(rows, width, CHUNK)],
        compiler_params=params(20),
        cost_estimate=cost(flops, 0),
        name="conv_stats",
    )(meta, extra, held(w), *[held(v) for v in flat])


def act_kernel(n_parts, meta, source, got, weight, out, coefs, c, sems):
    rows, width = c.shape
    halves, cs = width // LANES, width // 2
    wait = stream_in(source, c, sems, BLOCK)
    mean, scale = norm_coefs(got, weight, loss_scale)
    coefs[...] = jnp.zeros(coefs.shape, f32)
    coefs[0:2, :] = mean
    coefs[2:4, :] = scale
    for v in range(4):
        for g in range(2):
            row = got[g * n_parts + meta[2], 4 + v : 5 + v, 0:cs]
            lo = g * cs
            coefs[4 + 2 * v + lo // LANES : 5 + 2 * v + lo // LANES, lo % LANES : lo % LANES + cs] = row

    def body(at, carry):
        wait(at.start // BLOCK)
        for h in range(halves):
            normed = (c[at, half(h)] - coefs[h : h + 1, :]) * coefs[2 + h : 3 + h, :]
            normed = normed * coefs[4 + h : 5 + h, :] + coefs[6 + h : 7 + h, :]
            out[at, half(h)] = (normed * sigmoid(normed)).astype(bf16)
        return carry

    row_blocks(rows, BLOCK, body, 0)


def activate(meta, c, got, weight, n_parts):
    rows, width = c.shape
    return pl.pallas_call(
        functools.partial(act_kernel, n_parts),
        in_specs=[SM, HB, VM, VM],
        out_specs=(VM, VM),
        out_shape=(vmem_out((rows, width), bf16), vmem_out((2 * ROWS, LANES), f32)),
        scratch_shapes=stream_scratch(rows, width, BLOCK),
        compiler_params=params(12),
        cost_estimate=cost(0, 0),
        name="activate",
    )(meta, away(c), held(got), weight)


def turn_kernel(meta, images, own, other, buffer, sems):
    g = meta[1]
    rows = own.shape[0]
    block = 1024
    n = rows // block

    def copy(i, s):
        cols = pl.ds(pl.multiple_of(i * block, block), block)
        which = (1 - g, g)[s]
        return pltpu.make_async_copy(images.at[which, :, cols], buffer.at[s, :, cols], sems.at[s, i])

    for s in range(2):
        for i in range(n):
            copy(i, s).start()
    for s, out in ((0, other), (1, own)):

        def step(i, carry, s=s, out=out):
            copy(i, s).wait()
            cols = pl.ds(pl.multiple_of(i * block, block), block)
            out[cols, :] = buffer[s, :, cols].T
            return carry

        lax.fori_loop(0, n, step, 0)


def turn(meta, images):
    slots, cs, rows = images.shape
    return pl.pallas_call(
        turn_kernel,
        in_specs=[SM, HB],
        out_specs=(VM, VM),
        out_shape=(vmem_out((rows, cs), bf16),) * 2,
        scratch_shapes=[pltpu.VMEM((slots, cs, rows), bf16), pltpu.SemaphoreType.DMA((slots, rows // 1024))],
        compiler_params=params(8),
        cost_estimate=cost(0, 0),
        name="turn",
    )(meta, away(images))


def join_kernel(meta, got, half_done, out, buffer, sems):
    cs, rows = got.shape
    block = 1024
    n = rows // block
    del half_done

    def copy(i):
        cols = pl.ds(pl.multiple_of(i * block, block), block)
        return pltpu.make_async_copy(buffer.at[:, cols], out.at[1 - meta[1], :, cols], sems.at[i])

    for i in range(n):
        cols = slice(i * block, (i + 1) * block)
        buffer[:, cols] = got[:, cols].astype(f32)
        copy(i).start()
    for i in range(n):
        copy(i).wait()


def join(meta, got, half_done):
    cs, rows = got.shape
    return pl.pallas_call(
        join_kernel,
        in_specs=[SM, VM, HB],
        out_specs=HB,
        out_shape=hbm_out(half_done.shape, f32),
        scratch_shapes=[pltpu.VMEM((cs, rows), f32), pltpu.SemaphoreType.DMA((rows // 1024,))],
        input_output_aliases={2: 0},
        compiler_params=params(8),
        cost_estimate=cost(0, 0),
        name="join",
    )(meta, held(got), away(half_done))


def pool_kernel(n_x, meta, source, *refs):
    x, (got, weight, coefs1, labels, out, coefs, c, sems) = refs[:n_x], refs[n_x:]
    rows, width = c.shape
    halves = width // LANES
    first = meta[1] == 0
    wait = stream_in(source, c, sems, BLOCK)
    mean, scale = norm_coefs(got, weight, loss_scale)
    coefs[...] = jnp.zeros(coefs.shape, f32)
    coefs[0:2, :] = mean
    coefs[2:4, :] = scale

    def body(at, carry):
        wait(at.start // BLOCK)
        sums = list(carry)
        for h in range(halves):
            hat = (c[at, half(h)] - coefs[h : h + 1, :]) * coefs[2 + h : 3 + h, :]
            v = hat * coefs1[8 + h : 9 + h, :] + coefs1[10 + h : 11 + h, :] + part_half(x, first, at, h)
            s = sigmoid(v)
            slope = s * (1.0 + v * (1.0 - s))
            sums[3 * h] += jnp.sum(v * s, axis=0, keepdims=True)
            sums[3 * h + 1] += jnp.sum(slope * hat, axis=0, keepdims=True)
            sums[3 * h + 2] += jnp.sum(slope, axis=0, keepdims=True)
        return tuple(sums)

    sums = row_blocks(rows, BLOCK, body, (jnp.zeros((1, LANES), f32),) * (3 * halves))
    valid = meta[3].astype(f32)
    lines = [(6, labels[0:1, :]), (7, labels[1:2, :])]
    for h in range(halves):
        lines.append((h, sums[3 * h] * (valid / loss_scale)))
        lines.append((2 + h, sums[3 * h + 1]))
        lines.append((4 + h, sums[3 * h + 2]))
    send_rows(out, lines)


def pool(meta, c, x, got, weight, coefs1, labels):
    rows, width = c.shape
    return pl.pallas_call(
        functools.partial(pool_kernel, len(x)),
        in_specs=[SM, HB] + [VM] * (4 + len(x)),
        out_specs=(VM, VM),
        out_shape=(vmem_out(got.shape, f32), vmem_out((ROWS, LANES), f32)),
        scratch_shapes=stream_scratch(rows, width, BLOCK),
        compiler_params=params(12),
        cost_estimate=cost(0, 0),
        name="pool",
    )(meta, away(c), *[held(v) for v in x], held(got), weight, held(coefs1), labels)


def own_lanes(first, v, cs):
    return jnp.where(first, v[:, :cs], v[:, cs:])


def head_kernel(n_parts, n_ahead, meta, got, heads, stats, valid, avg_row, avg_col, *refs):
    sources, refs = refs[:n_ahead], refs[n_ahead:]
    (coefs, tw, an, hwg, hbg, pooled_own, gain_own, shift_own), ahead, refs = refs[:8], refs[8 : 8 + n_ahead], refs[8 + n_ahead :]
    pooled, slopes, shifts, labels, grads, mine_all, pooled_part, ht, sems = refs
    early = [pltpu.make_async_copy(v, to, sems.at[i]) for i, (v, to) in enumerate(zip(sources, ahead))]
    for c in early:
        c.start()
    tasks, channels = ht.shape
    images = valid.shape[0]
    n_task = 2 * n_parts
    width = channels // n_parts
    cs = width // 2
    halves = width // LANES
    tasks_here = tasks // n_task
    r = meta[2]
    first = meta[1] == 0
    for part in range(n_parts):
        for s in range(2):
            lo, at = part * width + s * cs, (s * n_parts + part) * cs
            ht[:, lo : lo + cs] = heads[:, at : at + cs]
    bias = stats[0, 4:5, :]
    for t in range(1, n_task):
        bias = bias + stats[t, 4:5, :]
    for n in range(images):
        base = (n // 2) * n_task + (n % 2) * n_parts
        for part in range(n_parts):
            for h in range(halves):
                lo = part * width + h * LANES
                pooled[n : n + 1, lo : lo + LANES] = got[base + part, h : h + 1, :]
        for h in range(halves):
            slopes[n : n + 1, half(h)] = got[base + r, 2 + h : 3 + h, :]
            shifts[n : n + 1, half(h)] = got[base + r, 4 + h : 5 + h, :]
        row = 6 + n % 2
        lab = got[(n // 2) * n_task, row : row + 1, :]
        for t in range(1, n_task):
            lab = lab + got[(n // 2) * n_task + t, row : row + 1, :]
        labels[n : n + 1, :] = lab
    pooled_all = pooled[...]
    table = ht[...]
    both_last = (((1,), (1,)), ((), ()))
    both_first = (((0,), (0,)), ((), ()))
    logits = lax.dot_general(pooled_all, table, both_last, precision=highest, preferred_element_type=f32)
    logits = logits + bias[:, 0:tasks]
    count = jnp.sum(valid[...], axis=0, keepdims=True)
    errors = valid[...] * (1.0 / (1.0 + jnp.exp(-logits)) - labels[:, 0:tasks]) / count
    gram = lax.dot_general(errors, errors, both_first, precision=highest, preferred_element_type=f32) * lax.dot_general(
        table, table, both_last, precision=highest, preferred_element_type=f32
    )
    row_id = lax.broadcasted_iota(jnp.int32, (tasks, tasks), 0)
    col_id = lax.broadcasted_iota(jnp.int32, (tasks, tasks), 1)
    trace = jnp.sum(jnp.sum(jnp.where(row_id == col_id, gram, 0.0), axis=1, keepdims=True), axis=0, keepdims=True)
    normalized = gram / (trace / tasks)
    start_row = avg_row[...] / jnp.sum(avg_row[...], axis=1, keepdims=True)
    start_col = avg_col[...] / jnp.sum(avg_col[...], axis=0, keepdims=True)
    w_row, w_col = start_row, start_col
    for j in range(FW_STEPS):
        rate = 1.0 / (j + 4.0)
        z_col = -tasks * jnp.sum(normalized * w_row, axis=1, keepdims=True)
        z_row = -tasks * jnp.sum(normalized * w_col, axis=0, keepdims=True)
        e_col = jnp.exp(z_col - jnp.max(z_col, axis=0, keepdims=True))
        e_row = jnp.exp(z_row - jnp.max(z_row, axis=1, keepdims=True))
        w_col = (1.0 - rate) * w_col + rate * (e_col / jnp.sum(e_col, axis=0, keepdims=True))
        w_row = (1.0 - rate) * w_row + rate * (e_row / jnp.sum(e_row, axis=1, keepdims=True))
    tw[...] = w_row
    an[...] = 0.9 * start_row + 0.1 * w_row
    logit_grads = errors * ((loss_scale * tasks) * w_row)
    task_id = lax.broadcasted_iota(jnp.int32, (tasks, tasks_here), 0) - (meta[1] * n_parts + r) * tasks_here
    mine = (task_id == lax.broadcasted_iota(jnp.int32, (tasks, tasks_here), 1)).astype(f32)
    own_grads = jnp.dot(logit_grads, mine, precision=highest, preferred_element_type=f32)
    hbg[...] = jnp.sum(own_grads, axis=0, keepdims=True)
    by_part = lax.dot_general(own_grads, pooled_all, both_first, precision=highest, preferred_element_type=f32)
    for part in range(n_parts):
        for s in range(2):
            lo, at = part * width + s * cs, (s * n_parts + part) * cs
            hwg[:, at : at + cs] = by_part[:, lo : lo + cs]
    grads[...] = jnp.dot(logit_grads, table, precision=highest, preferred_element_type=f32) / loss_scale
    own = pl.ds(pl.multiple_of(r * width, LANES), width)
    q = grads[:, own]
    mine_all[...] = q
    pooled_part[...] = pooled[:, own]
    gain = jnp.sum(q * slopes[...], axis=0, keepdims=True)
    shift = jnp.sum(q * shifts[...], axis=0, keepdims=True)
    here = mine_all[pl.ds(2 * meta[0] + meta[1], 1), :]
    coefs[...] = jnp.zeros(coefs.shape, f32)
    for h in range(halves):
        coefs[h : h + 1, :] = gain[:, half(h)]
        coefs[2 + h : 3 + h, :] = shift[:, half(h)]
        coefs[4 + h : 5 + h, :] = here[:, half(h)]
    gain_own[...] = own_lanes(first, gain, cs)
    shift_own[...] = own_lanes(first, shift, cs)
    for i in range(2):
        pooled_own[i : i + 1, :] = own_lanes(first, pooled_part[pl.ds(2 * meta[0] + i, 1), :], cs)
    for c in early:
        c.wait()


def head(meta, got, heads, stats, valid, avg_row, avg_col, n_parts, sources):
    tasks, channels = heads.shape
    images = valid.shape[0]
    width = channels // n_parts
    cs = width // 2
    tasks_here = tasks // (2 * n_parts)
    shapes = [(1, tasks), (1, tasks), (tasks_here, channels), (1, tasks_here), (2, cs), (1, cs), (1, cs)]
    return pl.pallas_call(
        functools.partial(head_kernel, n_parts, len(sources)),
        in_specs=[SM] + [VM] * 6 + [HB] * len(sources),
        out_specs=(VM,) * (8 + len(sources)),
        out_shape=(vmem_out((ROWS, LANES), f32),)
        + tuple(hbm_out(s, f32) for s in shapes)
        + tuple(vmem_out(v.shape, v.dtype) for v in sources),
        scratch_shapes=[
            pltpu.VMEM((images, channels), f32),
            pltpu.VMEM((images, width), f32),
            pltpu.VMEM((images, width), f32),
            pltpu.VMEM((images, LANES), f32),
            pltpu.VMEM((images, channels), f32),
            pltpu.VMEM((images, width), f32),
            pltpu.VMEM((images, width), f32),
            pltpu.VMEM((tasks, channels), f32),
            pltpu.SemaphoreType.DMA((len(sources),)),
        ],
        compiler_params=params(6),
        cost_estimate=cost(1 << 20, 1 << 20),
        name="head",
    )(meta, got, heads, stats, valid, avg_row, avg_col, *[away(v) for v in sources])


def grad_two_kernel(n_x, n_ahead, meta, c, *refs):
    x, (coefs, coefs1, heads, pixels), refs = refs[:n_x], refs[n_x : n_x + 4], refs[n_x + 4 :]
    sources, (low, target), refs = refs[:n_ahead], refs[n_ahead : n_ahead + 2], refs[n_ahead + 2 :]
    ahead, (summed, out_sems, sems) = refs[:n_ahead], refs[n_ahead:]
    early = [pltpu.make_async_copy(v, to, sems.at[i]) for i, (v, to) in enumerate(zip(sources, ahead))]
    for copy in early:
        copy.start()
    rows, width = c.shape
    valid = meta[3].astype(f32)
    first = meta[1] == 0
    send, finish = stream_out(summed, target, out_sems, BLOCK)

    def body(at, carry):
        for h in range(width // LANES):
            mean, scale = coefs[h : h + 1, :], coefs[2 + h : 3 + h, :]
            gain = coefs1[8 + h : 9 + h, :]
            hat = (c[at, half(h)] - mean) * scale
            v = hat * gain + coefs1[10 + h : 11 + h, :] + part_half(x, first, at, h)
            dn = (valid * heads[4 + h : 5 + h, :]) * silu_slope(v)
            summed[at, half(h)] = dn
            away = (heads[2 + h : 3 + h, :] + hat * heads[h : h + 1, :]) / pixels[0]
            low[at, half(h)] = ((valid * gain * scale) * (dn - away)).astype(bf16)
        send(at.start // BLOCK)
        return carry

    row_blocks(rows, BLOCK, body, 0)
    finish()
    for copy in early:
        copy.wait()


def grad_two(meta, c, x, coefs, coefs1, heads, pixels, sources):
    rows, width = c.shape
    return pl.pallas_call(
        functools.partial(grad_two_kernel, len(x), len(sources)),
        in_specs=[SM] + [VM] * (4 + len(x)) + [SM] + [HB] * len(sources),
        out_specs=(VM, HB) + (VM,) * len(sources),
        out_shape=(vmem_out((rows, width), bf16), hbm_out((rows, width), f32))
        + tuple(vmem_out(v.shape, v.dtype) for v in sources),
        scratch_shapes=stream_scratch(rows, width, BLOCK) + [pltpu.SemaphoreType.DMA((len(sources),))],
        compiler_params=params(10),
        cost_estimate=cost(0, 0),
        name="grad_two",
    )(meta, held(c), *[held(v) for v in x], held(coefs), held(coefs1), held(heads), pixels, *[away(v) for v in sources])


def grad_one_kernel(meta, c_source, dn_source, got, weight, coefs, pixels, low, gain_own, bias_own, c, c_sems, dn, dn_sems, sums):
    rows, width = c.shape
    valid = meta[3].astype(f32)
    wait_c = stream_in(c_source, c, c_sems, BLOCK)
    wait_dn = stream_in(dn_source, dn, dn_sems, BLOCK)
    sums[...] = weighted(got, weight)
    first = meta[1] == 0
    for out, at in ((gain_own, 0), (bias_own, 2)):
        line = jnp.concatenate([sums[at + h : at + h + 1, :] for h in range(width // LANES)], axis=1)
        out[...] = own_lanes(first, line, width // 2)

    def body(at, carry):
        wait_c(at.start // BLOCK)
        wait_dn(at.start // BLOCK)
        for h in range(width // LANES):
            mean, scale = coefs[h : h + 1, :], coefs[2 + h : 3 + h, :]
            hat = (c[at, half(h)] - mean) * scale
            away = (sums[2 + h : 3 + h, :] + hat * sums[h : h + 1, :]) / pixels[0]
            low[at, half(h)] = ((valid * coefs[4 + h : 5 + h, :] * scale) * (dn[at, half(h)] - away)).astype(bf16)
        return carry

    row_blocks(rows, BLOCK, body, 0)


def grad_one(meta, c, dn, got, weight, coefs, pixels):
    rows, width = c.shape
    return pl.pallas_call(
        grad_one_kernel,
        in_specs=[SM, HB, HB] + [VM] * 3 + [SM],
        out_specs=(VM, VM, VM),
        out_shape=(vmem_out((rows, width), bf16), hbm_out((1, width // 2), f32), hbm_out((1, width // 2), f32)),
        scratch_shapes=stream_scratch(rows, width, BLOCK) * 2 + [pltpu.VMEM((ROWS, LANES), f32)],
        compiler_params=params(24),
        cost_estimate=cost(0, 0),
        name="grad_one",
    )(meta, away(c), away(dn), held(got), weight, held(coefs), pixels)


def back_setup(gs, scratch):
    rows, width = gs[0].shape
    clear_ends(scratch, rows)
    place_columns(scratch, [(g, slice(0, width), i * width) for i, g in enumerate(gs)], SIDE)


def back_products(scratch, w, at, chunk):
    total = None
    for dx in (0, 1, -1):
        acc = None
        for dy in (-1, 0, 1):
            lo = at + SIDE * (1 - dy)
            term = jnp.dot(scratch[lo : lo + chunk, :], w[3 * (dy + 1) + dx + 1], preferred_element_type=f32)
            acc = term if acc is None else acc + term
        acc = moved(acc, -dx)
        total = acc if total is None else total + acc
    return total


def back_two_kernel(n_parts, meta, w, c, coefs, *refs):
    gs, (target, stats, scratch, out, out_sems) = refs[:n_parts], refs[n_parts:]
    rows, width = out.shape
    halves = width // LANES
    chunk = CHUNK
    n = rows // chunk
    push, finish = stream_out(out, target, out_sems, chunk)
    back_setup(gs, scratch)
    sums = [jnp.zeros((1, LANES), f32)] * (2 * halves)

    def finish_chunk(j):
        at = slice(j * chunk, (j + 1) * chunk)
        for h in range(halves):
            hat = (c[at, half(h)] - coefs[h : h + 1, :]) * coefs[2 + h : 3 + h, :]
            dn = out[at, half(h)] * silu_slope(hat * coefs[4 + h : 5 + h, :] + coefs[6 + h : 7 + h, :])
            out[at, half(h)] = dn
            sums[2 * h] += jnp.sum(dn * hat, axis=0, keepdims=True)
            sums[2 * h + 1] += jnp.sum(dn, axis=0, keepdims=True)
        push(j)

    for j in range(n):
        out[j * chunk : (j + 1) * chunk, :] = back_products(scratch, w, j * chunk, chunk)
        if j:
            finish_chunk(j - 1)
    finish_chunk(n - 1)
    send_rows(stats, [(2 * i + h, sums[2 * h + i]) for h in range(halves) for i in range(2)])
    finish()


def back_two(meta, w, c, coefs, g_parts, n_devices):
    rows, width = c.shape
    n = len(g_parts)
    return pl.pallas_call(
        functools.partial(back_two_kernel, n),
        in_specs=[SM] + [VM] * (n + 3),
        out_specs=(HB, VM),
        out_shape=(hbm_out((rows, width), f32), vmem_out((n_devices, ROWS, LANES), f32)),
        scratch_shapes=[pltpu.VMEM((rows + 2 * SIDE, n * width), bf16), *stream_scratch(rows, width, CHUNK)],
        compiler_params=params(20),
        cost_estimate=cost(2 * 9 * rows * width * width * n, 16 << 20),
        name="back_two",
    )(meta, held(w), held(c), held(coefs), *[held(v) for v in g_parts])


def back_one_kernel(n_parts, meta, w, summed, *refs):
    gs, (out, send, scratch, acc, keep, keep_sems) = refs[:n_parts], refs[n_parts:]
    rows, width = summed.shape
    cs = width // 2
    chunk = CHUNK
    n = rows // chunk
    g = meta[1]
    first = g == 0
    back_setup(gs, scratch)

    def copy(j):
        cols = pl.ds(j * chunk, chunk)
        return pltpu.make_async_copy(keep.at[:, cols], out.at[g, :, cols], keep_sems.at[j])

    def finish_chunk(j):
        at = slice(j * chunk, (j + 1) * chunk)
        total = acc[j % 2] + summed[at, :]
        a, b = total[:, :cs], total[:, cs:]
        keep[:, at] = jnp.where(first, a, b).T
        copy(j).start()
        send[:, at] = jnp.where(first, b, a).T.astype(bf16)

    for j in range(n):
        acc[j % 2] = back_products(scratch, w, j * chunk, chunk)
        if j:
            finish_chunk(j - 1)
    finish_chunk(n - 1)
    for j in range(n):
        copy(j).wait()


def back_one(meta, w, summed, g_parts):
    rows, width = summed.shape
    n = len(g_parts)
    cs = width // 2
    return pl.pallas_call(
        functools.partial(back_one_kernel, n),
        in_specs=[SM] + [VM] * (n + 2),
        out_specs=(HB, VM),
        out_shape=(hbm_out((2, cs, rows), f32), vmem_out((cs, rows), bf16)),
        scratch_shapes=[
            pltpu.VMEM((rows + 2 * SIDE, n * width), bf16),
            pltpu.VMEM((2, CHUNK, width), f32),
            pltpu.VMEM((cs, rows), f32),
            pltpu.SemaphoreType.DMA((rows // CHUNK,)),
        ],
        compiler_params=params(24),
        cost_estimate=cost(2 * 9 * rows * width * width * n, 16 << 20),
        name="back_one",
    )(meta, held(w), held(summed), *[held(v) for v in g_parts])


def weight_kernel(sizes, n_parts, taps, n_pieces, sends, meta, g, *refs):
    n = sum(sizes)
    xs, refs = refs[:n], refs[n:]
    if n_pieces:
        pieces, source, refs = refs[:n_pieces], refs[n_pieces], refs[n_pieces + 1 :]
    keep, send, refs = refs[0], refs[1 : 1 + len(sends)], refs[1 + len(sends) :]
    if n_pieces:
        w, ahead, shifted, x, sems = refs
    else:
        shifted, x = refs
    rows, width = g.shape
    cs = width // 2
    first = meta[1] == 0
    copies = []
    if n_pieces:
        copies = backward_copies(meta, pieces, w, cs, n_parts, sems)
        copies.append(pltpu.make_async_copy(source, ahead, sems.at[len(copies)]))
    for c in copies:
        c.start()
    parts, at = [], 0
    for size in sizes:
        parts.append(xs[at : at + size])
        at += size
    place_columns(x, column_plan(meta, parts, n_parts, cs), 0)
    moves = sorted({1 - k % 3 for k in taps})
    for i in range(len(moves)):
        clear_ends(shifted.at[i], rows)

    def shift(at, carry):
        low = g[at, :]
        value = low.astype(f32)
        to = pl.ds(pl.multiple_of(at.start + SIDE, SIDE), at.size)
        for i, e in enumerate(moves):
            shifted[i, to, :] = moved(value, e).astype(bf16) if e else low
        return carry

    row_blocks(rows, BLOCK, shift, 0)
    for j, k in enumerate(taps):
        lo = SIDE * (2 - k // 3)
        lhs = shifted[moves.index(1 - k % 3), lo : lo + rows, :]
        term = lax.dot_general(lhs, x[...], (((0,), (0,)), ((), ())), preferred_element_type=f32)
        a, b = term[:cs], term[cs:]
        keep[j] = jnp.where(first, a, b)
        which = int(j >= sends[0])
        send[which][j - which * sends[0]] = jnp.where(first, b, a).astype(bf16)
    for c in copies:
        c.wait()


def weight_grad(meta, g, parts, n_parts, taps, pieces=(), source=None, early=None):
    rows, width = g.shape
    flat = [v for p in parts for v in p]
    columns = n_parts * width
    shape = (len(taps), width // 2, columns)
    sends = [len(taps)] if early is None else [early, len(taps) - early]
    extra = [away(v) for v in (*pieces, source)] if pieces else []
    ahead = (vmem_out((9, columns, width), bf16), vmem_out(source.shape, f32)) if pieces else ()
    return pl.pallas_call(
        functools.partial(weight_kernel, [len(p) for p in parts], n_parts, taps, len(pieces), sends),
        in_specs=[SM] + [VM] * (len(flat) + 1) + [HB] * len(extra),
        out_specs=(VM,) * (1 + len(sends) + len(ahead)),
        out_shape=(vmem_out(shape, f32), *[vmem_out((n, *shape[1:]), bf16) for n in sends], *ahead),
        scratch_shapes=[
            pltpu.VMEM((len({k % 3 for k in taps}), rows + 2 * SIDE, width), bf16),
            pltpu.VMEM((rows, columns), bf16),
        ]
        + ([pltpu.SemaphoreType.DMA((10 * n_parts + 1,))] if pieces else []),
        compiler_params=params(24),
        cost_estimate=cost(2 * len(taps) * rows * width * columns, 16 << 20),
        name="weight_grad",
    )(meta, held(g), *[held(v) for v in flat], *extra)


def swap(values, axis, by):
    n = lax.axis_size(axis)
    return lax.ppermute(values, axis, [(i, i ^ by) for i in range(n)])


def xor_order(values, r):
    bit = 1
    while bit < len(values):
        flip = (r & bit) != 0
        values = [jnp.where(flip, values[i ^ bit], v) for i, v in enumerate(values)]
        bit *= 2
    return values


def gate(values, *others):
    return lax.optimization_barrier((values, *others))[0]


class Stage:
    def __init__(self, stride, size):
        self.stride, self.size = stride, size

    def place(self):
        return (lax.axis_index("batch") // self.stride) % self.size

    def split(self, total, kind):
        k = self.place()
        pieces = total.reshape(self.size, -1, total.shape[1])
        mine = lax.dynamic_index_in_dim(pieces, k, keepdims=False)
        others = range(1, self.size)
        return mine, [lax.dynamic_index_in_dim(pieces, k ^ j, keepdims=False).astype(kind) for j in others]

    def send(self, sent):
        return [swap(v, "batch", self.stride * j) for j, v in enumerate(sent, 1)]

    def add(self, mine, got, *after):
        for v in got:
            mine = mine + gate(v, *after).astype(f32)
        return mine

    def spread(self, out):
        return [swap(out, "batch", self.stride * j) for j in range(1, self.size)]

    def join(self, out, got, *after):
        return jnp.concatenate(xor_order([out] + [gate(v, *after) for v in got], self.place()), axis=0)


def on_device(
    images,
    conv1_weight,
    norm1_gain,
    norm1_bias,
    conv2_weight,
    norm2_gain,
    norm2_bias,
    head_weight,
    head_bias,
    labels,
    image_counts,
    average_weights,
):
    n_task, n_batch = lax.axis_size("task"), lax.axis_size("batch")
    t, b = lax.axis_index("task"), lax.axis_index("batch")
    slots, cs, pixels = images.shape
    n_parts = n_task // slots
    g, r = t // n_parts, t % n_parts
    first = g == 0
    width = slots * cs
    channels = n_task * cs
    n_devices = n_task * n_batch
    tasks_here = head_weight.shape[1]
    tasks = tasks_here * n_task

    valid_images = (jnp.arange(slots)[None, :] < image_counts[:, None]).astype(f32)
    image_total = jnp.sum(image_counts).astype(f32)
    pixel_total = (image_total * pixels).reshape(1)
    own_valid = (g < lax.dynamic_index_in_dim(image_counts, b, keepdims=False)).astype(jnp.int32)
    place = jnp.stack([b, g, r, 0 * b, b % 4]).astype(jnp.int32)
    meta = jnp.stack([b, g, r, own_valid, b % 4]).astype(jnp.int32)
    same = (jnp.arange(n_parts) == r).astype(f32)
    weight = (valid_images[:, :, None] * same[None, None, :]).reshape(n_devices, 1)
    weight = jnp.broadcast_to(weight[:, :, None], (n_devices, ROWS, LANES))

    def relative(w):
        blocks = [w[..., i * cs : (i + 1) * cs] for i in range(n_task)]
        order = [xor_order(blocks[s * n_parts : (s + 1) * n_parts], r) for s in range(slots)]
        return [jnp.concatenate([order[s][i] for s in range(slots)], axis=-1) for i in range(n_parts)]

    def ordered(own, other, axis):
        return jnp.concatenate([jnp.where(first, own, other), jnp.where(first, other, own)], axis=axis)

    def joined(pieces):
        other = jnp.concatenate(xor_order(list(pieces[1:]), b % 4 if len(pieces) > 2 else 0), axis=1)
        return relative(ordered(pieces[0], other, 1))

    def forward_pieces(pieces):
        return pieces if aligned(cs) else [jnp.concatenate(joined(pieces), axis=2)]

    def backward_pieces(pieces, done=()):
        if aligned(cs):
            parts = [[swap(v, "task", i) if i else v for v in pieces[len(done) > 0 :]] for i in range(n_parts)]
            return [v for i, part in enumerate(parts) for v in ([done[i]] if done else []) + part]
        return [swap(v, "task", i) if i else v for i, v in enumerate(joined(pieces))]

    def all_parts(v):
        return [v] + [swap(v, "task", i) for i in range(1, n_parts)]

    quarter = lax.dynamic_index_in_dim(
        conv1_weight.reshape(9, 4, cs // 4, channels), b % 4, axis=1, keepdims=False
    ).reshape(-1, channels)
    own_heads = jnp.pad(head_weight.T, ((0, -tasks_here % ROWS), (0, 0)))
    near = swap(quarter, "task", n_parts)
    x_own, x_send = turn(gate(place, quarter), images)
    x_other = swap(x_send, "task", n_parts)

    vecs = jnp.stack([norm1_gain, norm1_bias, norm2_gain, norm2_bias])
    vecs = jnp.pad(vecs, ((4, 0), (0, LANES - cs)))
    bias_rows = lax.dynamic_update_slice(jnp.zeros((ROWS, LANES), f32), head_bias[None], (4, t * tasks_here))
    label_rows = lax.dynamic_update_slice(
        jnp.zeros((slots, LANES), f32), labels.astype(f32), (0, t * tasks_here)
    )
    columns = [bias_rows, label_rows, vecs, valid_images.reshape(-1, 1), average_weights.reshape(-1, 1)]

    near1 = gate(near, x_send).reshape(9, cs // 4, channels)
    side = swap(near1, "batch", 1)
    w1 = [conv1_weight, near1, side, swap(near1, "batch", 2), swap(side, "batch", 2)]
    w2 = [conv2_weight, swap(gate(conv2_weight, near1), "task", n_parts)]
    both_heads = jnp.concatenate([own_heads, swap(gate(own_heads, x_send), "task", n_parts)])
    every = xor_order([both_heads] + [swap(both_heads, "task", i) for i in range(1, n_parts)], r)
    every = jnp.stack(every).reshape(n_parts, slots, -1, channels)[:, :, :tasks_here]
    table = jnp.where(first, every, jnp.flip(every, 1)).swapaxes(0, 1).reshape(tasks, channels).astype(f32)
    forward1 = fetch(place, forward_pieces(w1), cs)
    own2 = [swap(conv2_weight, "task", i) if i else conv2_weight for i in range(n_parts)] if aligned(cs) else ()
    turned1 = backward_pieces(w1)
    if aligned(cs):
        x_parts = list(zip(all_parts(x_own), all_parts(gate(x_other, *w1, weight, vecs, forward1, table, *turned1, *own2, *columns))))
    else:
        x_parts = [[v] for v in all_parts(ordered(x_own, x_other, 1))]

    def exchange(rows):
        flat_rows = rows.reshape(n_devices * ROWS, LANES)
        return lax.all_to_all(flat_rows, ("batch", "task"), 0, 0, tiled=True).reshape(rows.shape)

    c1, stats = conv_stats(place, vecs, forward1, x_parts, cs, n_devices, 0)
    totals = exchange(stats)
    turned2 = backward_pieces([w2[0], gate(w2[1], totals)], own2)
    a_own, coefs1 = activate(meta, c1, totals, gate(weight, w2[1]), n_parts)
    a_parts = [[v] for v in all_parts(a_own)]
    forward2 = fetch(place, [gate(w2[0], a_own), *forward_pieces(w2)[1:]] if aligned(cs) else forward_pieces(w2), cs)
    c2, stats = conv_stats(place, bias_rows, forward2, a_parts, cs, n_devices, 18 * pixels * width * channels)
    stats2 = exchange(stats)
    sums, coefs2 = pool(meta, c2, x_parts[0], stats2, weight, coefs1, gate(label_rows, *turned2))
    heads, task_weights, average_next, head_grad, bias_grad, pooled, gain_two, bias_two, *ahead = head(
        meta,
        exchange(sums),
        table,
        stats2,
        columns[3],
        average_weights.reshape(1, -1),
        columns[4],
        n_parts,
        [c2, *x_parts[0]],
    )

    def both_groups(keep, got, *after):
        return (keep + gate(got, *after).astype(f32)).reshape(-1, channels)

    def assemble(done, taps):
        where = {k: (v, j) for v, ks in zip(done, taps) for j, k in enumerate(ks)}
        out = jnp.concatenate([where[k][0][where[k][1] * cs : (where[k][1] + 1) * cs] for k in range(9)])
        out = out.reshape(9, cs, channels)
        if not aligned(cs):
            parts = [out[:, :, i * width : (i + 1) * width] for i in range(n_parts)]
            order = [v for s in range(slots) for v in xor_order([p[:, :, s * cs : (s + 1) * cs] for p in parts], r)]
            out = jnp.concatenate(order, axis=2)
        return out.astype(f32)

    low_bits = 1 << ((n_batch.bit_length() - 1) // 2)
    one, two = Stage(1, low_bits), Stage(low_bits, n_batch // low_bits)
    taps_a, taps_b = (0, 3, 6, 1), (4, 7, 2, 5, 8)
    every_tap = taps_a + taps_b
    low2, summed, *a_near = grad_two(
        meta, ahead[0], ahead[1:], coefs2, coefs1, heads, pixel_total, [v for p in a_parts for v in p]
    )
    a_near = [[v] for v in a_near]
    low2_parts = all_parts(low2)
    keep2, send2, late2, back2, c1_near = weight_grad(meta, low2, a_near, n_parts, every_tap, turned2, c1, len(taps_a))
    got2 = swap(send2, "task", n_parts)
    low2_parts[0] = gate(low2_parts[0], keep2)
    dn1, stats = back_two(meta, back2, c1_near, coefs1, low2_parts, n_devices)
    totals = exchange(gate(stats, got2))
    got2 = jnp.concatenate([got2, swap(gate(late2, totals), "task", n_parts)])
    low1, gain_one, bias_one = grad_one(meta, c1, dn1, totals, weight, coefs1, pixel_total)
    low1_parts = all_parts(low1)

    keep_a, send_a = weight_grad(meta, low1, x_parts, n_parts, taps_a)
    got_a = swap(send_a, "task", n_parts)
    mine2, sent2 = one.split(both_groups(keep2, got2, keep_a), bf16)
    got2 = one.send(sent2)
    keep_b, send_b, back1, summed = weight_grad(
        meta, gate(low1, keep_a, *sent2), x_parts, n_parts, taps_b, turned1, summed
    )
    got_b = swap(send_b, "task", n_parts)
    mine2, sent2 = two.split(one.add(mine2, got2, keep_b), f32)
    got2 = two.send(sent2)
    mine_a, sent_a = one.split(both_groups(keep_a, got_a, keep_b, *sent2), bf16)
    got_a = one.send(sent_a)
    low1_parts[0] = gate(low1_parts[0], *sent_a)
    half_done, send = back_one(meta, back1, summed, low1_parts)
    got = swap(send, "task", n_parts)
    mine_b, sent_b = one.split(both_groups(keep_b, got_b, send), bf16)
    got_b = one.send(sent_b)
    mine_a, sent_a = two.split(one.add(mine_a, got_a, *sent_b), bf16)
    got_a = two.send(sent_a)
    sum2 = two.add(mine2, got2, *sent_a).astype(bf16)
    got2 = two.spread(sum2)
    mine_b, sent_b = two.split(one.add(mine_b, got_b, sum2), bf16)
    got_b = two.send(sent_b)
    sum_a = two.add(mine_a, got_a, *sent_b).astype(bf16)
    got_a = two.spread(sum_a)
    sum2 = two.join(sum2, got2, sum_a)
    got2 = one.spread(sum2)
    sum_b = two.add(mine_b, got_b, sum2).astype(bf16)
    got_b = two.spread(sum_b)
    sum_a = two.join(sum_a, got_a, sum_b, got)
    got_a = one.spread(sum_a)
    sum_b = two.join(sum_b, got_b, sum_a)
    got_b = one.spread(sum_b)
    input_grad = join(meta, gate(got, sum_b), half_done)
    conv2_grad = assemble([one.join(sum2, got2, input_grad)], [every_tap])
    sum_a = one.join(sum_a, got_a, conv2_grad)
    sum_b = one.join(sum_b, got_b, sum_a)
    conv1_grad = assemble([sum_a, sum_b], [taps_a, taps_b])

    return (
        pooled,
        input_grad,
        conv1_grad,
        gain_one[0],
        bias_one[0],
        conv2_grad,
        gain_two[0],
        bias_two[0],
        head_grad.T,
        bias_grad[0],
        task_weights[0],
        average_next[0],
    )


def solution(mesh):
    in_specs = (
        P("batch", "task", None),
        P(None, "task", None),
        P("task"),
        P("task"),
        P(None, "task", None),
        P("task"),
        P("task"),
        P(None, "task"),
        P("task"),
        P("batch", "task"),
        P(),
        P(),
    )
    out_specs = (
        P("batch", "task"),
        P("batch", "task", None),
        P(None, "task", None),
        P("task"),
        P("task"),
        P(None, "task", None),
        P("task"),
        P("task"),
        P(None, "task"),
        P("task"),
        P(),
        P(),
    )
    return jax.shard_map(
        on_device, mesh=mesh, in_specs=in_specs, out_specs=out_specs, check_vma=False
    )
```

```python
import functools

import jax
import jax.numpy as jnp
from jax import lax
from jax.experimental import pallas as pl
from jax.experimental.pallas import tpu as pltpu
from jax.sharding import PartitionSpec as P

SIDE = 64
FW_STEPS = 20
LANES = 128
ROWS = 8

eps = 1e-05
loss_scale = 4096.0
highest = lax.Precision.HIGHEST
f32 = jnp.float32
bf16 = jnp.bfloat16


def params(mib, **more):
    return pltpu.CompilerParams(vmem_limit_bytes=mib << 20, **more)


def cost(flops, moved):
    return pl.CostEstimate(flops=flops, bytes_accessed=moved, transcendentals=0)


VM = pl.BlockSpec(memory_space=pltpu.VMEM)
HB = pl.BlockSpec(memory_space=pl.ANY)
SM = pl.BlockSpec(memory_space=pltpu.SMEM)


def sigmoid(v):
    return 0.5 + 0.5 * jnp.tanh(0.5 * v)


def silu_slope(v):
    s = sigmoid(v)
    return s * (1.0 + v * (1.0 - s))


def half(h):
    return slice(h * LANES, (h + 1) * LANES)


def held(values):
    return pltpu.with_memory_space_constraint(values, pltpu.VMEM)


def away(values):
    return pltpu.with_memory_space_constraint(values, pltpu.HBM)


def vmem_out(shape, kind):
    return pltpu.VMEM(shape, kind)


def hbm_out(shape, kind):
    return pltpu.HBM(shape, kind)


def column_is(rows, width, at):
    return (lax.broadcasted_iota(jnp.int32, (rows, width), 0) & (SIDE - 1)) == at


def moved(v, e):
    rows, width = v.shape
    if e == 0:
        return v
    edge = SIDE - 1 if e == 1 else 0
    return jnp.where(column_is(rows, width, edge), 0.0, pltpu.roll(v, rows - 1 if e == 1 else 1, 0))


def aligned(cs):
    return cs % LANES == 0


def column_plan(meta, parts, n_parts, cs):
    g, r = meta[1], meta[2]
    plan = []
    for i, part in enumerate(parts):
        if not aligned(cs):
            plan.append((part[0], slice(0, 2 * cs), i * 2 * cs))
            continue
        for s in range(2):
            place = s * n_parts + (r ^ i) if len(part) == 1 else (g, 1 - g)[s] * n_parts + (r ^ i)
            ref, cols = (part[0], slice(s * cs, (s + 1) * cs)) if len(part) == 1 else (part[s], slice(0, cs))
            plan.append((ref, cols, pl.multiple_of(place * cs, cs)))
    return plan


def place_columns(dst, plan, first_row):
    rows = plan[0][0].shape[0]
    block = 512

    def step(j, carry):
        at = pl.multiple_of(j * block, block)
        for ref, cols, to in plan:
            width = cols.stop - cols.start
            dst[pl.ds(pl.multiple_of(at + first_row, SIDE), block), pl.ds(to, width)] = ref[pl.ds(at, block), cols]
        return carry

    lax.fori_loop(0, rows // block, step, 0)


def clear_ends(dst, rows):
    zero = jnp.zeros((SIDE, dst.shape[1]), dst.dtype)
    dst[0:SIDE, :] = zero
    dst[SIDE + rows : SIDE + rows + SIDE, :] = zero


def piece_rows(meta, cs, base, n_pieces):
    g, q = meta[1], meta[4]
    qs = cs // (n_pieces - 1)
    return [pl.ds(pl.multiple_of(base + g * cs, cs), cs)] + [
        pl.ds(pl.multiple_of(base + (1 - g) * cs + (q ^ i if n_pieces > 2 else 0) * qs, qs), qs)
        for i in range(n_pieces - 1)
    ]


def forward_copies(meta, pieces, w, cs, sems):
    if not aligned(cs):
        return [pltpu.make_async_copy(pieces[0], w, sems.at[0])]
    spots = piece_rows(meta, cs, 0, len(pieces))
    return [pltpu.make_async_copy(p, w.at[:, to, :], sems.at[i]) for i, (p, to) in enumerate(zip(pieces, spots))]


def backward_copies(meta, pieces, w, cs, n_parts, sems):
    width = 2 * cs
    if not aligned(cs):
        return [
            pltpu.make_async_copy(p, w.at[:, pl.ds(i * width, width), :], sems.at[i]) for i, p in enumerate(pieces)
        ]
    copies = []
    for i in range(n_parts):
        each = len(pieces) // n_parts
        for p, to in zip(pieces[each * i : each * (i + 1)], piece_rows(meta, cs, i * width, each)):
            for s in range(2):
                cols = pl.ds(pl.multiple_of((s * n_parts + meta[2]) * cs, cs), cs)
                copies.append(
                    pltpu.make_async_copy(p.at[:, :, cols], w.at[:, to, pl.ds(s * cs, cs)], sems.at[len(copies)])
                )
    return copies


def part_half(part, first, rows, h):
    if len(part) == 1:
        return part[0][rows, half(h)].astype(f32)
    own, other = part[0][rows, :], part[1][rows, :]
    return (jnp.where(first, own, other) if h == 0 else jnp.where(first, other, own)).astype(f32)


def row_blocks(rows, block, body, start):
    def step(j, carry):
        return body(pl.ds(pl.multiple_of(j * block, block), block), carry)

    return lax.fori_loop(0, rows // block, step, start)


def send_rows(out, rows, base=None):
    n = out.shape[0]
    start = jnp.zeros((ROWS, LANES), f32) if base is None else base
    out[...] = jnp.broadcast_to(start[None], out.shape)
    for at, value in rows:
        out[:, at : at + 1, :] = jnp.broadcast_to(value[None], (n, 1, LANES))


def weighted(got, weight):
    return jnp.sum(got[...] * weight[...], axis=0)


def norm_coefs(got, weight, rows):
    w = weight[...]
    values = got[...]
    count = jnp.sum(w, axis=0)
    total = jnp.sum(values * w, axis=0)
    mean = total / count
    off = values - mean[None]
    apart = jnp.sum(off * off * w, axis=0)
    squares = total[2:4] + rows * apart[0:2]
    return mean[0:2], lax.rsqrt(squares / (count[0:2] * rows) + eps)


def stream_in(source, buffer, sems, block):
    rows = buffer.shape[0]

    def copy(j):
        at = pl.ds(pl.multiple_of(j * block, block), block)
        return pltpu.make_async_copy(source.at[at, :], buffer.at[at, :], sems.at[j])

    for j in range(rows // block):
        copy(j).start()
    return lambda j: copy(j).wait()


def stream_out(buffer, target, sems, block):
    rows = buffer.shape[0]

    def copy(j):
        at = pl.ds(pl.multiple_of(j * block, block), block)
        return pltpu.make_async_copy(buffer.at[at, :], target.at[at, :], sems.at[j])

    def finish():
        for j in range(rows // block):
            copy(j).wait()

    return (lambda j: copy(j).start()), finish


def stream_scratch(rows, width, block):
    return [pltpu.VMEM((rows, width), f32), pltpu.SemaphoreType.DMA((rows // block,))]


BLOCK = 512
CHUNK = 1024


def fetch_kernel(n_pieces, cs, meta, *refs):
    pieces, (w, sems) = refs[:n_pieces], refs[n_pieces:]
    copies = forward_copies(meta, pieces, w, cs, sems)
    for c in copies:
        c.start()
    for c in copies:
        c.wait()


def fetch(meta, pieces, cs):
    shape = (9, 2 * cs, pieces[0].shape[2])
    return pl.pallas_call(
        functools.partial(fetch_kernel, len(pieces), cs),
        in_specs=[SM] + [HB] * len(pieces),
        out_specs=VM,
        out_shape=vmem_out(shape, bf16),
        scratch_shapes=[pltpu.SemaphoreType.DMA((len(pieces),))],
        compiler_params=params(2),
        name="fetch",
    )(meta, *[away(v) for v in pieces])


def conv_kernel(parts_of, n_parts, meta, extra, w, *refs):
    n = sum(parts_of)
    xs, (target, stats, scratch, out, out_sems) = refs[:n], refs[n:]
    parts, at = [], 0
    for size in parts_of:
        parts.append(xs[at : at + size])
        at += size
    rows, width = out.shape
    cs = width // 2
    chunk = CHUNK
    send, finish = stream_out(out, target, out_sems, chunk)
    clear_ends(scratch, rows)
    place_columns(scratch, column_plan(meta, parts, n_parts, cs), SIDE)
    mean = squares = jnp.zeros((1, width), f32)
    for j in range(rows // chunk):
        at = slice(j * chunk, (j + 1) * chunk)
        total = None
        for dx in (0, 1, -1):
            acc = None
            for dy in (-1, 0, 1):
                lo = at.start + SIDE * (dy + 1)
                tap = w[3 * (dy + 1) + dx + 1]
                term = lax.dot_general(
                    scratch[lo : lo + chunk, :], tap, (((1,), (1,)), ((), ())), preferred_element_type=f32
                )
                acc = term if acc is None else acc + term
            acc = moved(acc, dx)
            total = acc if total is None else total + acc
        out[at, :] = total
        send(j)
        here = jnp.sum(total, axis=0, keepdims=True) / chunk
        off = out[at, :] - here
        spread = jnp.sum(off * off, axis=0, keepdims=True)
        gap = here - mean
        mean = mean + gap / (j + 1.0)
        squares = squares + spread + gap * gap * (chunk * j / (j + 1.0))
    send_rows(
        stats,
        [(h, mean[:, half(h)]) for h in range(width // LANES)]
        + [(2 + h, squares[:, half(h)]) for h in range(width // LANES)],
        extra[...],
    )
    finish()


def conv_stats(meta, extra, w, parts, cs, n_devices, flops):
    rows, width, channels = parts[0][0].shape[0], 2 * cs, w.shape[2]
    flat = [v for part in parts for v in part]
    return pl.pallas_call(
        functools.partial(conv_kernel, [len(p) for p in parts], len(parts)),
        in_specs=[SM, VM, VM] + [VM] * len(flat),
        out_specs=(HB, VM),
        out_shape=(hbm_out((rows, width), f32), vmem_out((n_devices, ROWS, LANES), f32)),
        scratch_shapes=[pltpu.VMEM((rows + 2 * SIDE, channels), bf16), *stream_scratch(rows, width, CHUNK)],
        compiler_params=params(20),
        cost_estimate=cost(flops, 0),
        name="conv_stats",
    )(meta, extra, held(w), *[held(v) for v in flat])


def act_kernel(n_parts, meta, source, got, weight, out, coefs, c, sems):
    rows, width = c.shape
    halves, cs = width // LANES, width // 2
    wait = stream_in(source, c, sems, BLOCK)
    mean, scale = norm_coefs(got, weight, loss_scale)
    coefs[...] = jnp.zeros(coefs.shape, f32)
    coefs[0:2, :] = mean
    coefs[2:4, :] = scale
    for v in range(4):
        for g in range(2):
            row = got[g * n_parts + meta[2], 4 + v : 5 + v, 0:cs]
            lo = g * cs
            coefs[4 + 2 * v + lo // LANES : 5 + 2 * v + lo // LANES, lo % LANES : lo % LANES + cs] = row

    def body(at, carry):
        wait(at.start // BLOCK)
        for h in range(halves):
            normed = (c[at, half(h)] - coefs[h : h + 1, :]) * coefs[2 + h : 3 + h, :]
            normed = normed * coefs[4 + h : 5 + h, :] + coefs[6 + h : 7 + h, :]
            out[at, half(h)] = (normed * sigmoid(normed)).astype(bf16)
        return carry

    row_blocks(rows, BLOCK, body, 0)


def activate(meta, c, got, weight, n_parts):
    rows, width = c.shape
    return pl.pallas_call(
        functools.partial(act_kernel, n_parts),
        in_specs=[SM, HB, VM, VM],
        out_specs=(VM, VM),
        out_shape=(vmem_out((rows, width), bf16), vmem_out((2 * ROWS, LANES), f32)),
        scratch_shapes=stream_scratch(rows, width, BLOCK),
        compiler_params=params(12),
        cost_estimate=cost(0, 0),
        name="activate",
    )(meta, away(c), held(got), weight)


def turn_kernel(meta, images, own, other, buffer, sems):
    g = meta[1]
    rows = own.shape[0]
    block = 1024
    n = rows // block

    def copy(i, s):
        cols = pl.ds(pl.multiple_of(i * block, block), block)
        which = (1 - g, g)[s]
        return pltpu.make_async_copy(images.at[which, :, cols], buffer.at[s, :, cols], sems.at[s, i])

    for s in range(2):
        for i in range(n):
            copy(i, s).start()
    for s, out in ((0, other), (1, own)):

        def step(i, carry, s=s, out=out):
            copy(i, s).wait()
            cols = pl.ds(pl.multiple_of(i * block, block), block)
            out[cols, :] = buffer[s, :, cols].T
            return carry

        lax.fori_loop(0, n, step, 0)


def turn(meta, images):
    slots, cs, rows = images.shape
    return pl.pallas_call(
        turn_kernel,
        in_specs=[SM, HB],
        out_specs=(VM, VM),
        out_shape=(vmem_out((rows, cs), bf16),) * 2,
        scratch_shapes=[pltpu.VMEM((slots, cs, rows), bf16), pltpu.SemaphoreType.DMA((slots, rows // 1024))],
        compiler_params=params(8),
        cost_estimate=cost(0, 0),
        name="turn",
    )(meta, away(images))


def join_kernel(meta, got, half_done, out, buffer, sems):
    cs, rows = got.shape
    block = 1024
    n = rows // block
    del half_done

    def copy(i):
        cols = pl.ds(pl.multiple_of(i * block, block), block)
        return pltpu.make_async_copy(buffer.at[:, cols], out.at[1 - meta[1], :, cols], sems.at[i])

    for i in range(n):
        cols = slice(i * block, (i + 1) * block)
        buffer[:, cols] = got[:, cols].astype(f32)
        copy(i).start()
    for i in range(n):
        copy(i).wait()


def join(meta, got, half_done):
    cs, rows = got.shape
    return pl.pallas_call(
        join_kernel,
        in_specs=[SM, VM, HB],
        out_specs=HB,
        out_shape=hbm_out(half_done.shape, f32),
        scratch_shapes=[pltpu.VMEM((cs, rows), f32), pltpu.SemaphoreType.DMA((rows // 1024,))],
        input_output_aliases={2: 0},
        compiler_params=params(8),
        cost_estimate=cost(0, 0),
        name="join",
    )(meta, held(got), away(half_done))


def pool_kernel(n_x, meta, source, *refs):
    x, (got, weight, coefs1, labels, out, coefs, c, sems) = refs[:n_x], refs[n_x:]
    rows, width = c.shape
    halves = width // LANES
    first = meta[1] == 0
    wait = stream_in(source, c, sems, BLOCK)
    mean, scale = norm_coefs(got, weight, loss_scale)
    coefs[...] = jnp.zeros(coefs.shape, f32)
    coefs[0:2, :] = mean
    coefs[2:4, :] = scale

    def body(at, carry):
        wait(at.start // BLOCK)
        sums = list(carry)
        for h in range(halves):
            hat = (c[at, half(h)] - coefs[h : h + 1, :]) * coefs[2 + h : 3 + h, :]
            v = hat * coefs1[8 + h : 9 + h, :] + coefs1[10 + h : 11 + h, :] + part_half(x, first, at, h)
            s = sigmoid(v)
            slope = s * (1.0 + v * (1.0 - s))
            sums[3 * h] += jnp.sum(v * s, axis=0, keepdims=True)
            sums[3 * h + 1] += jnp.sum(slope * hat, axis=0, keepdims=True)
            sums[3 * h + 2] += jnp.sum(slope, axis=0, keepdims=True)
        return tuple(sums)

    sums = row_blocks(rows, BLOCK, body, (jnp.zeros((1, LANES), f32),) * (3 * halves))
    valid = meta[3].astype(f32)
    lines = [(6, labels[0:1, :]), (7, labels[1:2, :])]
    for h in range(halves):
        lines.append((h, sums[3 * h] * (valid / loss_scale)))
        lines.append((2 + h, sums[3 * h + 1]))
        lines.append((4 + h, sums[3 * h + 2]))
    send_rows(out, lines)


def pool(meta, c, x, got, weight, coefs1, labels):
    rows, width = c.shape
    return pl.pallas_call(
        functools.partial(pool_kernel, len(x)),
        in_specs=[SM, HB] + [VM] * (4 + len(x)),
        out_specs=(VM, VM),
        out_shape=(vmem_out(got.shape, f32), vmem_out((ROWS, LANES), f32)),
        scratch_shapes=stream_scratch(rows, width, BLOCK),
        compiler_params=params(12),
        cost_estimate=cost(0, 0),
        name="pool",
    )(meta, away(c), *[held(v) for v in x], held(got), weight, held(coefs1), labels)


def own_lanes(first, v, cs):
    return jnp.where(first, v[:, :cs], v[:, cs:])


def head_kernel(n_parts, n_ahead, meta, got, heads, stats, valid, avg_row, avg_col, *refs):
    sources, refs = refs[:n_ahead], refs[n_ahead:]
    (coefs, tw, an, hwg, hbg, pooled_own, gain_own, shift_own), ahead, refs = refs[:8], refs[8 : 8 + n_ahead], refs[8 + n_ahead :]
    pooled, slopes, shifts, labels, grads, mine_all, pooled_part, ht, sems = refs
    early = [pltpu.make_async_copy(v, to, sems.at[i]) for i, (v, to) in enumerate(zip(sources, ahead))]
    for c in early:
        c.start()
    tasks, channels = ht.shape
    images = valid.shape[0]
    n_task = 2 * n_parts
    width = channels // n_parts
    cs = width // 2
    halves = width // LANES
    tasks_here = tasks // n_task
    r = meta[2]
    first = meta[1] == 0
    for part in range(n_parts):
        for s in range(2):
            lo, at = part * width + s * cs, (s * n_parts + part) * cs
            ht[:, lo : lo + cs] = heads[:, at : at + cs]
    bias = stats[0, 4:5, :]
    for t in range(1, n_task):
        bias = bias + stats[t, 4:5, :]
    for n in range(images):
        base = (n // 2) * n_task + (n % 2) * n_parts
        for part in range(n_parts):
            for h in range(halves):
                lo = part * width + h * LANES
                pooled[n : n + 1, lo : lo + LANES] = got[base + part, h : h + 1, :]
        for h in range(halves):
            slopes[n : n + 1, half(h)] = got[base + r, 2 + h : 3 + h, :]
            shifts[n : n + 1, half(h)] = got[base + r, 4 + h : 5 + h, :]
        row = 6 + n % 2
        lab = got[(n // 2) * n_task, row : row + 1, :]
        for t in range(1, n_task):
            lab = lab + got[(n // 2) * n_task + t, row : row + 1, :]
        labels[n : n + 1, :] = lab
    pooled_all = pooled[...]
    table = ht[...]
    both_last = (((1,), (1,)), ((), ()))
    both_first = (((0,), (0,)), ((), ()))
    logits = lax.dot_general(pooled_all, table, both_last, precision=highest, preferred_element_type=f32)
    logits = logits + bias[:, 0:tasks]
    count = jnp.sum(valid[...], axis=0, keepdims=True)
    errors = valid[...] * (1.0 / (1.0 + jnp.exp(-logits)) - labels[:, 0:tasks]) / count
    gram = lax.dot_general(errors, errors, both_first, precision=highest, preferred_element_type=f32) * lax.dot_general(
        table, table, both_last, precision=highest, preferred_element_type=f32
    )
    row_id = lax.broadcasted_iota(jnp.int32, (tasks, tasks), 0)
    col_id = lax.broadcasted_iota(jnp.int32, (tasks, tasks), 1)
    trace = jnp.sum(jnp.sum(jnp.where(row_id == col_id, gram, 0.0), axis=1, keepdims=True), axis=0, keepdims=True)
    normalized = gram / (trace / tasks)
    start_row = avg_row[...] / jnp.sum(avg_row[...], axis=1, keepdims=True)
    start_col = avg_col[...] / jnp.sum(avg_col[...], axis=0, keepdims=True)
    w_row, w_col = start_row, start_col
    for j in range(FW_STEPS):
        rate = 1.0 / (j + 4.0)
        z_col = -tasks * jnp.sum(normalized * w_row, axis=1, keepdims=True)
        z_row = -tasks * jnp.sum(normalized * w_col, axis=0, keepdims=True)
        e_col = jnp.exp(z_col - jnp.max(z_col, axis=0, keepdims=True))
        e_row = jnp.exp(z_row - jnp.max(z_row, axis=1, keepdims=True))
        w_col = (1.0 - rate) * w_col + rate * (e_col / jnp.sum(e_col, axis=0, keepdims=True))
        w_row = (1.0 - rate) * w_row + rate * (e_row / jnp.sum(e_row, axis=1, keepdims=True))
    tw[...] = w_row
    an[...] = 0.9 * start_row + 0.1 * w_row
    logit_grads = errors * ((loss_scale * tasks) * w_row)
    task_id = lax.broadcasted_iota(jnp.int32, (tasks, tasks_here), 0) - (meta[1] * n_parts + r) * tasks_here
    mine = (task_id == lax.broadcasted_iota(jnp.int32, (tasks, tasks_here), 1)).astype(f32)
    own_grads = jnp.dot(logit_grads, mine, precision=highest, preferred_element_type=f32)
    hbg[...] = jnp.sum(own_grads, axis=0, keepdims=True)
    by_part = lax.dot_general(own_grads, pooled_all, both_first, precision=highest, preferred_element_type=f32)
    for part in range(n_parts):
        for s in range(2):
            lo, at = part * width + s * cs, (s * n_parts + part) * cs
            hwg[:, at : at + cs] = by_part[:, lo : lo + cs]
    grads[...] = jnp.dot(logit_grads, table, precision=highest, preferred_element_type=f32) / loss_scale
    own = pl.ds(pl.multiple_of(r * width, LANES), width)
    q = grads[:, own]
    mine_all[...] = q
    pooled_part[...] = pooled[:, own]
    gain = jnp.sum(q * slopes[...], axis=0, keepdims=True)
    shift = jnp.sum(q * shifts[...], axis=0, keepdims=True)
    here = mine_all[pl.ds(2 * meta[0] + meta[1], 1), :]
    coefs[...] = jnp.zeros(coefs.shape, f32)
    for h in range(halves):
        coefs[h : h + 1, :] = gain[:, half(h)]
        coefs[2 + h : 3 + h, :] = shift[:, half(h)]
        coefs[4 + h : 5 + h, :] = here[:, half(h)]
    gain_own[...] = own_lanes(first, gain, cs)
    shift_own[...] = own_lanes(first, shift, cs)
    for i in range(2):
        pooled_own[i : i + 1, :] = own_lanes(first, pooled_part[pl.ds(2 * meta[0] + i, 1), :], cs)
    for c in early:
        c.wait()


def head(meta, got, heads, stats, valid, avg_row, avg_col, n_parts, sources):
    tasks, channels = heads.shape
    images = valid.shape[0]
    width = channels // n_parts
    cs = width // 2
    tasks_here = tasks // (2 * n_parts)
    shapes = [(1, tasks), (1, tasks), (tasks_here, channels), (1, tasks_here), (2, cs), (1, cs), (1, cs)]
    return pl.pallas_call(
        functools.partial(head_kernel, n_parts, len(sources)),
        in_specs=[SM] + [VM] * 6 + [HB] * len(sources),
        out_specs=(VM,) * (8 + len(sources)),
        out_shape=(vmem_out((ROWS, LANES), f32),)
        + tuple(hbm_out(s, f32) for s in shapes)
        + tuple(vmem_out(v.shape, v.dtype) for v in sources),
        scratch_shapes=[
            pltpu.VMEM((images, channels), f32),
            pltpu.VMEM((images, width), f32),
            pltpu.VMEM((images, width), f32),
            pltpu.VMEM((images, LANES), f32),
            pltpu.VMEM((images, channels), f32),
            pltpu.VMEM((images, width), f32),
            pltpu.VMEM((images, width), f32),
            pltpu.VMEM((tasks, channels), f32),
            pltpu.SemaphoreType.DMA((len(sources),)),
        ],
        compiler_params=params(6),
        cost_estimate=cost(1 << 20, 1 << 20),
        name="head",
    )(meta, got, heads, stats, valid, avg_row, avg_col, *[away(v) for v in sources])


def grad_two_kernel(n_x, n_ahead, meta, c, *refs):
    x, (coefs, coefs1, heads, pixels), refs = refs[:n_x], refs[n_x : n_x + 4], refs[n_x + 4 :]
    sources, (low, target), refs = refs[:n_ahead], refs[n_ahead : n_ahead + 2], refs[n_ahead + 2 :]
    ahead, (summed, out_sems, sems) = refs[:n_ahead], refs[n_ahead:]
    early = [pltpu.make_async_copy(v, to, sems.at[i]) for i, (v, to) in enumerate(zip(sources, ahead))]
    for copy in early:
        copy.start()
    rows, width = c.shape
    valid = meta[3].astype(f32)
    first = meta[1] == 0
    send, finish = stream_out(summed, target, out_sems, BLOCK)

    def body(at, carry):
        for h in range(width // LANES):
            mean, scale = coefs[h : h + 1, :], coefs[2 + h : 3 + h, :]
            gain = coefs1[8 + h : 9 + h, :]
            hat = (c[at, half(h)] - mean) * scale
            v = hat * gain + coefs1[10 + h : 11 + h, :] + part_half(x, first, at, h)
            dn = (valid * heads[4 + h : 5 + h, :]) * silu_slope(v)
            summed[at, half(h)] = dn
            away = (heads[2 + h : 3 + h, :] + hat * heads[h : h + 1, :]) / pixels[0]
            low[at, half(h)] = ((valid * gain * scale) * (dn - away)).astype(bf16)
        send(at.start // BLOCK)
        return carry

    row_blocks(rows, BLOCK, body, 0)
    finish()
    for copy in early:
        copy.wait()


def grad_two(meta, c, x, coefs, coefs1, heads, pixels, sources):
    rows, width = c.shape
    return pl.pallas_call(
        functools.partial(grad_two_kernel, len(x), len(sources)),
        in_specs=[SM] + [VM] * (4 + len(x)) + [SM] + [HB] * len(sources),
        out_specs=(VM, HB) + (VM,) * len(sources),
        out_shape=(vmem_out((rows, width), bf16), hbm_out((rows, width), f32))
        + tuple(vmem_out(v.shape, v.dtype) for v in sources),
        scratch_shapes=stream_scratch(rows, width, BLOCK) + [pltpu.SemaphoreType.DMA((len(sources),))],
        compiler_params=params(10),
        cost_estimate=cost(0, 0),
        name="grad_two",
    )(meta, held(c), *[held(v) for v in x], held(coefs), held(coefs1), held(heads), pixels, *[away(v) for v in sources])


def grad_one_kernel(meta, c_source, dn_source, got, weight, coefs, pixels, low, gain_own, bias_own, c, c_sems, dn, dn_sems, sums):
    rows, width = c.shape
    valid = meta[3].astype(f32)
    wait_c = stream_in(c_source, c, c_sems, BLOCK)
    wait_dn = stream_in(dn_source, dn, dn_sems, BLOCK)
    sums[...] = weighted(got, weight)
    first = meta[1] == 0
    for out, at in ((gain_own, 0), (bias_own, 2)):
        line = jnp.concatenate([sums[at + h : at + h + 1, :] for h in range(width // LANES)], axis=1)
        out[...] = own_lanes(first, line, width // 2)

    def body(at, carry):
        wait_c(at.start // BLOCK)
        wait_dn(at.start // BLOCK)
        for h in range(width // LANES):
            mean, scale = coefs[h : h + 1, :], coefs[2 + h : 3 + h, :]
            hat = (c[at, half(h)] - mean) * scale
            away = (sums[2 + h : 3 + h, :] + hat * sums[h : h + 1, :]) / pixels[0]
            low[at, half(h)] = ((valid * coefs[4 + h : 5 + h, :] * scale) * (dn[at, half(h)] - away)).astype(bf16)
        return carry

    row_blocks(rows, BLOCK, body, 0)


def grad_one(meta, c, dn, got, weight, coefs, pixels):
    rows, width = c.shape
    return pl.pallas_call(
        grad_one_kernel,
        in_specs=[SM, HB, HB] + [VM] * 3 + [SM],
        out_specs=(VM, VM, VM),
        out_shape=(vmem_out((rows, width), bf16), hbm_out((1, width // 2), f32), hbm_out((1, width // 2), f32)),
        scratch_shapes=stream_scratch(rows, width, BLOCK) * 2 + [pltpu.VMEM((ROWS, LANES), f32)],
        compiler_params=params(24),
        cost_estimate=cost(0, 0),
        name="grad_one",
    )(meta, away(c), away(dn), held(got), weight, held(coefs), pixels)


def back_setup(gs, scratch):
    rows, width = gs[0].shape
    clear_ends(scratch, rows)
    place_columns(scratch, [(g, slice(0, width), i * width) for i, g in enumerate(gs)], SIDE)


def back_products(scratch, w, at, chunk):
    total = None
    for dx in (0, 1, -1):
        acc = None
        for dy in (-1, 0, 1):
            lo = at + SIDE * (1 - dy)
            term = jnp.dot(scratch[lo : lo + chunk, :], w[3 * (dy + 1) + dx + 1], preferred_element_type=f32)
            acc = term if acc is None else acc + term
        acc = moved(acc, -dx)
        total = acc if total is None else total + acc
    return total


def back_two_kernel(n_parts, meta, w, c, coefs, *refs):
    gs, (target, stats, scratch, out, out_sems) = refs[:n_parts], refs[n_parts:]
    rows, width = out.shape
    halves = width // LANES
    chunk = CHUNK
    n = rows // chunk
    push, finish = stream_out(out, target, out_sems, chunk)
    back_setup(gs, scratch)
    sums = [jnp.zeros((1, LANES), f32)] * (2 * halves)

    def finish_chunk(j):
        at = slice(j * chunk, (j + 1) * chunk)
        for h in range(halves):
            hat = (c[at, half(h)] - coefs[h : h + 1, :]) * coefs[2 + h : 3 + h, :]
            dn = out[at, half(h)] * silu_slope(hat * coefs[4 + h : 5 + h, :] + coefs[6 + h : 7 + h, :])
            out[at, half(h)] = dn
            sums[2 * h] += jnp.sum(dn * hat, axis=0, keepdims=True)
            sums[2 * h + 1] += jnp.sum(dn, axis=0, keepdims=True)
        push(j)

    for j in range(n):
        out[j * chunk : (j + 1) * chunk, :] = back_products(scratch, w, j * chunk, chunk)
        if j:
            finish_chunk(j - 1)
    finish_chunk(n - 1)
    send_rows(stats, [(2 * i + h, sums[2 * h + i]) for h in range(halves) for i in range(2)])
    finish()


def back_two(meta, w, c, coefs, g_parts, n_devices):
    rows, width = c.shape
    n = len(g_parts)
    return pl.pallas_call(
        functools.partial(back_two_kernel, n),
        in_specs=[SM] + [VM] * (n + 3),
        out_specs=(HB, VM),
        out_shape=(hbm_out((rows, width), f32), vmem_out((n_devices, ROWS, LANES), f32)),
        scratch_shapes=[pltpu.VMEM((rows + 2 * SIDE, n * width), bf16), *stream_scratch(rows, width, CHUNK)],
        compiler_params=params(20),
        cost_estimate=cost(2 * 9 * rows * width * width * n, 16 << 20),
        name="back_two",
    )(meta, held(w), held(c), held(coefs), *[held(v) for v in g_parts])


def back_one_kernel(n_parts, meta, w, summed, *refs):
    gs, (out, send, scratch, acc, keep, keep_sems) = refs[:n_parts], refs[n_parts:]
    rows, width = summed.shape
    cs = width // 2
    chunk = CHUNK
    n = rows // chunk
    g = meta[1]
    first = g == 0
    back_setup(gs, scratch)

    def copy(j):
        cols = pl.ds(j * chunk, chunk)
        return pltpu.make_async_copy(keep.at[:, cols], out.at[g, :, cols], keep_sems.at[j])

    def finish_chunk(j):
        at = slice(j * chunk, (j + 1) * chunk)
        total = acc[j % 2] + summed[at, :]
        a, b = total[:, :cs], total[:, cs:]
        keep[:, at] = jnp.where(first, a, b).T
        copy(j).start()
        send[:, at] = jnp.where(first, b, a).T.astype(bf16)

    for j in range(n):
        acc[j % 2] = back_products(scratch, w, j * chunk, chunk)
        if j:
            finish_chunk(j - 1)
    finish_chunk(n - 1)
    for j in range(n):
        copy(j).wait()


def back_one(meta, w, summed, g_parts):
    rows, width = summed.shape
    n = len(g_parts)
    cs = width // 2
    return pl.pallas_call(
        functools.partial(back_one_kernel, n),
        in_specs=[SM] + [VM] * (n + 2),
        out_specs=(HB, VM),
        out_shape=(hbm_out((2, cs, rows), f32), vmem_out((cs, rows), bf16)),
        scratch_shapes=[
            pltpu.VMEM((rows + 2 * SIDE, n * width), bf16),
            pltpu.VMEM((2, CHUNK, width), f32),
            pltpu.VMEM((cs, rows), f32),
            pltpu.SemaphoreType.DMA((rows // CHUNK,)),
        ],
        compiler_params=params(24),
        cost_estimate=cost(2 * 9 * rows * width * width * n, 16 << 20),
        name="back_one",
    )(meta, held(w), held(summed), *[held(v) for v in g_parts])


def weight_kernel(sizes, n_parts, taps, n_pieces, sends, meta, g, *refs):
    n = sum(sizes)
    xs, refs = refs[:n], refs[n:]
    if n_pieces:
        pieces, source, refs = refs[:n_pieces], refs[n_pieces], refs[n_pieces + 1 :]
    keep, send, refs = refs[0], refs[1 : 1 + len(sends)], refs[1 + len(sends) :]
    if n_pieces:
        w, ahead, shifted, x, sems = refs
    else:
        shifted, x = refs
    rows, width = g.shape
    cs = width // 2
    first = meta[1] == 0
    copies = []
    if n_pieces:
        copies = backward_copies(meta, pieces, w, cs, n_parts, sems)
        copies.append(pltpu.make_async_copy(source, ahead, sems.at[len(copies)]))
    for c in copies:
        c.start()
    parts, at = [], 0
    for size in sizes:
        parts.append(xs[at : at + size])
        at += size
    place_columns(x, column_plan(meta, parts, n_parts, cs), 0)
    moves = sorted({1 - k % 3 for k in taps})
    for i in range(len(moves)):
        clear_ends(shifted.at[i], rows)

    def shift(at, carry):
        low = g[at, :]
        value = low.astype(f32)
        to = pl.ds(pl.multiple_of(at.start + SIDE, SIDE), at.size)
        for i, e in enumerate(moves):
            shifted[i, to, :] = moved(value, e).astype(bf16) if e else low
        return carry

    row_blocks(rows, BLOCK, shift, 0)
    for j, k in enumerate(taps):
        lo = SIDE * (2 - k // 3)
        lhs = shifted[moves.index(1 - k % 3), lo : lo + rows, :]
        term = lax.dot_general(lhs, x[...], (((0,), (0,)), ((), ())), preferred_element_type=f32)
        a, b = term[:cs], term[cs:]
        keep[j] = jnp.where(first, a, b)
        which = int(j >= sends[0])
        send[which][j - which * sends[0]] = jnp.where(first, b, a).astype(bf16)
    for c in copies:
        c.wait()


def weight_grad(meta, g, parts, n_parts, taps, pieces=(), source=None, early=None):
    rows, width = g.shape
    flat = [v for p in parts for v in p]
    columns = n_parts * width
    shape = (len(taps), width // 2, columns)
    sends = [len(taps)] if early is None else [early, len(taps) - early]
    extra = [away(v) for v in (*pieces, source)] if pieces else []
    ahead = (vmem_out((9, columns, width), bf16), vmem_out(source.shape, f32)) if pieces else ()
    return pl.pallas_call(
        functools.partial(weight_kernel, [len(p) for p in parts], n_parts, taps, len(pieces), sends),
        in_specs=[SM] + [VM] * (len(flat) + 1) + [HB] * len(extra),
        out_specs=(VM,) * (1 + len(sends) + len(ahead)),
        out_shape=(vmem_out(shape, f32), *[vmem_out((n, *shape[1:]), bf16) for n in sends], *ahead),
        scratch_shapes=[
            pltpu.VMEM((len({k % 3 for k in taps}), rows + 2 * SIDE, width), bf16),
            pltpu.VMEM((rows, columns), bf16),
        ]
        + ([pltpu.SemaphoreType.DMA((10 * n_parts + 1,))] if pieces else []),
        compiler_params=params(24),
        cost_estimate=cost(2 * len(taps) * rows * width * columns, 16 << 20),
        name="weight_grad",
    )(meta, held(g), *[held(v) for v in flat], *extra)


def swap(values, axis, by):
    n = lax.axis_size(axis)
    return lax.ppermute(values, axis, [(i, i ^ by) for i in range(n)])


def xor_order(values, r):
    bit = 1
    while bit < len(values):
        flip = (r & bit) != 0
        values = [jnp.where(flip, values[i ^ bit], v) for i, v in enumerate(values)]
        bit *= 2
    return values


def gate(values, *others):
    return lax.optimization_barrier((values, *others))[0]


class Stage:
    def __init__(self, stride, size):
        self.stride, self.size = stride, size
        k = (lax.axis_index("batch").astype(jnp.uint32) >> (stride.bit_length() - 1)) & (size - 1)
        self.order = [k ^ j for j in range(size)]
        self.bits = [(k & (1 << i)) != 0 for i in range(size.bit_length() - 1)]

    def scalars(self):
        return [*self.order, *self.bits]

    def settle(self, scalars):
        self.order, self.bits = list(scalars[: self.size]), list(scalars[self.size :])

    def split(self, total, kind):
        pieces = total.reshape(self.size, -1, total.shape[1])
        mine, *others = [lax.dynamic_index_in_dim(pieces, k, keepdims=False) for k in self.order]
        return mine, [v.astype(kind) for v in others]

    def send(self, sent):
        return [swap(v, "batch", self.stride * j) for j, v in enumerate(sent, 1)]

    def add(self, mine, got, *after):
        for v in got:
            mine = mine + gate(v, *after).astype(f32)
        return mine

    def spread(self, out):
        return [swap(out, "batch", self.stride * j) for j in range(1, self.size)]

    def join(self, out, got, *after):
        pieces = [out] + [gate(v, *after) for v in got]
        for i, flip in enumerate(self.bits):
            pieces = [jnp.where(flip, pieces[j ^ (1 << i)], v) for j, v in enumerate(pieces)]
        return jnp.concatenate(pieces, axis=0)


def on_device(
    images,
    conv1_weight,
    norm1_gain,
    norm1_bias,
    conv2_weight,
    norm2_gain,
    norm2_bias,
    head_weight,
    head_bias,
    labels,
    image_counts,
    average_weights,
):
    n_task, n_batch = lax.axis_size("task"), lax.axis_size("batch")
    t, b = lax.axis_index("task"), lax.axis_index("batch")
    slots, cs, pixels = images.shape
    n_parts = n_task // slots
    g, r = t // n_parts, t % n_parts
    first = g == 0
    width = slots * cs
    channels = n_task * cs
    n_devices = n_task * n_batch
    tasks_here = head_weight.shape[1]
    tasks = tasks_here * n_task

    valid_images = (jnp.arange(slots)[None, :] < image_counts[:, None]).astype(f32)
    image_total = jnp.sum(image_counts).astype(f32)
    pixel_total = (image_total * pixels).reshape(1)
    own_valid = (g < lax.dynamic_index_in_dim(image_counts, b, keepdims=False)).astype(jnp.int32)
    place = jnp.stack([b, g, r, 0 * b, b % 4]).astype(jnp.int32)
    meta = jnp.stack([b, g, r, own_valid, b % 4]).astype(jnp.int32)
    same = (jnp.arange(n_parts) == r).astype(f32)
    weight = (valid_images[:, :, None] * same[None, None, :]).reshape(n_devices, 1)
    weight = jnp.broadcast_to(weight[:, :, None], (n_devices, ROWS, LANES))

    def relative(w):
        blocks = [w[..., i * cs : (i + 1) * cs] for i in range(n_task)]
        order = [xor_order(blocks[s * n_parts : (s + 1) * n_parts], r) for s in range(slots)]
        return [jnp.concatenate([order[s][i] for s in range(slots)], axis=-1) for i in range(n_parts)]

    def ordered(own, other, axis):
        return jnp.concatenate([jnp.where(first, own, other), jnp.where(first, other, own)], axis=axis)

    def joined(pieces):
        other = jnp.concatenate(xor_order(list(pieces[1:]), b % 4 if len(pieces) > 2 else 0), axis=1)
        return relative(ordered(pieces[0], other, 1))

    def forward_pieces(pieces):
        return pieces if aligned(cs) else [jnp.concatenate(joined(pieces), axis=2)]

    def backward_pieces(pieces, done=()):
        if aligned(cs):
            parts = [[swap(v, "task", i) if i else v for v in pieces[len(done) > 0 :]] for i in range(n_parts)]
            return [v for i, part in enumerate(parts) for v in ([done[i]] if done else []) + part]
        return [swap(v, "task", i) if i else v for i, v in enumerate(joined(pieces))]

    def all_parts(v):
        return [v] + [swap(v, "task", i) for i in range(1, n_parts)]

    quarter = lax.dynamic_index_in_dim(
        conv1_weight.reshape(9, 4, cs // 4, channels), b % 4, axis=1, keepdims=False
    ).reshape(-1, channels)
    own_heads = jnp.pad(head_weight.T, ((0, -tasks_here % ROWS), (0, 0)))
    near, near_heads = swap(quarter, "task", n_parts), swap(own_heads, "task", n_parts)
    x_own, x_send = turn(gate(place, quarter), images)
    x_other = swap(gate(x_send, near, near_heads), "task", n_parts)

    vecs = jnp.stack([norm1_gain, norm1_bias, norm2_gain, norm2_bias])
    vecs = jnp.pad(vecs, ((4, 0), (0, LANES - cs)))
    bias_rows = lax.dynamic_update_slice(jnp.zeros((ROWS, LANES), f32), head_bias[None], (4, t * tasks_here))
    label_rows = lax.dynamic_update_slice(
        jnp.zeros((slots, LANES), f32), labels.astype(f32), (0, t * tasks_here)
    )
    columns = [bias_rows, label_rows, vecs, valid_images.reshape(-1, 1), average_weights.reshape(-1, 1)]

    near1 = gate(near, x_send).reshape(9, cs // 4, channels)
    side = swap(near1, "batch", 1)
    w1 = [conv1_weight, near1, side, swap(near1, "batch", 2), swap(side, "batch", 2)]
    w2 = [conv2_weight, swap(gate(conv2_weight, near1), "task", n_parts)]
    both_heads = jnp.concatenate([own_heads, near_heads])
    every = xor_order([both_heads] + [swap(both_heads, "task", i) for i in range(1, n_parts)], r)
    every = jnp.stack(every).reshape(n_parts, slots, -1, channels)[:, :, :tasks_here]
    table = jnp.where(first, every, jnp.flip(every, 1)).swapaxes(0, 1).reshape(tasks, channels).astype(f32)
    forward1 = fetch(place, forward_pieces(w1), cs)
    own2 = [swap(conv2_weight, "task", i) if i else conv2_weight for i in range(n_parts)] if aligned(cs) else ()
    turned1 = backward_pieces(w1)
    low_bits = 1 << ((n_batch.bit_length() - 1) // 2)
    one, two = Stage(1, low_bits), Stage(low_bits, n_batch // low_bits)
    x_other, *scalars = lax.optimization_barrier((x_other, *one.scalars(), *two.scalars()))
    one.settle(scalars[: len(one.scalars())])
    two.settle(scalars[len(one.scalars()) :])
    if aligned(cs):
        x_parts = list(zip(all_parts(x_own), all_parts(gate(x_other, *w1, weight, vecs, forward1, table, *turned1, *own2, *columns))))
    else:
        x_parts = [[v] for v in all_parts(ordered(x_own, x_other, 1))]

    def exchange(rows):
        flat_rows = rows.reshape(n_devices * ROWS, LANES)
        return lax.all_to_all(flat_rows, ("batch", "task"), 0, 0, tiled=True).reshape(rows.shape)

    c1, stats = conv_stats(place, vecs, forward1, x_parts, cs, n_devices, 0)
    totals = exchange(stats)
    turned2 = backward_pieces([w2[0], gate(w2[1], totals)], own2)
    a_own, coefs1 = activate(meta, c1, totals, gate(weight, w2[1]), n_parts)
    a_parts = [[v] for v in all_parts(a_own)]
    forward2 = fetch(place, [gate(w2[0], a_own), *forward_pieces(w2)[1:]] if aligned(cs) else forward_pieces(w2), cs)
    c2, stats = conv_stats(place, bias_rows, forward2, a_parts, cs, n_devices, 18 * pixels * width * channels)
    stats2 = exchange(stats)
    sums, coefs2 = pool(meta, c2, x_parts[0], stats2, weight, coefs1, gate(label_rows, *turned2))
    heads, task_weights, average_next, head_grad, bias_grad, pooled, gain_two, bias_two, *ahead = head(
        meta,
        exchange(sums),
        table,
        stats2,
        columns[3],
        average_weights.reshape(1, -1),
        columns[4],
        n_parts,
        [c2, *x_parts[0]],
    )

    def both_groups(keep, got, *after):
        return (keep + gate(got, *after).astype(f32)).reshape(-1, channels)

    def assemble(done, taps):
        where = {k: (v, j) for v, ks in zip(done, taps) for j, k in enumerate(ks)}
        out = jnp.concatenate([where[k][0][where[k][1] * cs : (where[k][1] + 1) * cs] for k in range(9)])
        out = out.reshape(9, cs, channels)
        if not aligned(cs):
            parts = [out[:, :, i * width : (i + 1) * width] for i in range(n_parts)]
            order = [v for s in range(slots) for v in xor_order([p[:, :, s * cs : (s + 1) * cs] for p in parts], r)]
            out = jnp.concatenate(order, axis=2)
        return out.astype(f32)

    taps_a, taps_b = (0, 3, 6, 1), (4, 7, 2, 5, 8)
    every_tap = taps_b + taps_a
    low2, summed, *a_near = grad_two(
        meta, ahead[0], ahead[1:], coefs2, coefs1, heads, pixel_total, [v for p in a_parts for v in p]
    )
    a_near = [[v] for v in a_near]
    low2_parts = all_parts(low2)
    keep2, send2, late2, back2, c1_near = weight_grad(meta, low2, a_near, n_parts, every_tap, turned2, c1, len(taps_b))
    got2 = swap(send2, "task", n_parts)
    low2_parts[0] = gate(low2_parts[0], keep2)
    dn1, stats = back_two(meta, back2, c1_near, coefs1, low2_parts, n_devices)
    totals = exchange(gate(stats, got2))
    got2 = jnp.concatenate([got2, swap(gate(late2, totals), "task", n_parts)])
    low1, gain_one, bias_one = grad_one(meta, c1, dn1, totals, weight, coefs1, pixel_total)
    low1_parts = all_parts(low1)

    keep_a, send_a = weight_grad(meta, low1, x_parts, n_parts, taps_a)
    got_a = swap(send_a, "task", n_parts)
    mine2, sent2 = one.split(both_groups(keep2, got2, keep_a), bf16)
    got2 = one.send(sent2)
    keep_b, send_b, back1, summed = weight_grad(
        meta, gate(low1, keep_a, *sent2), x_parts, n_parts, taps_b, turned1, summed
    )
    got_b = swap(send_b, "task", n_parts)
    mine2, sent2 = two.split(one.add(mine2, got2, keep_b), f32)
    got2 = two.send(sent2)
    mine_a, sent_a = one.split(both_groups(keep_a, got_a, keep_b, *sent2), bf16)
    got_a = one.send(sent_a)
    low1_parts[0] = gate(low1_parts[0], *sent_a)
    half_done, send = back_one(meta, back1, summed, low1_parts)
    got = swap(send, "task", n_parts)
    mine_b, sent_b = one.split(both_groups(keep_b, got_b, send), bf16)
    got_b = one.send(sent_b)
    mine_a, sent_a = two.split(one.add(mine_a, got_a, *sent_b), bf16)
    got_a = two.send(sent_a)
    sum2 = two.add(mine2, got2, *sent_a).astype(bf16)
    got2 = two.spread(sum2)
    mine_b, sent_b = two.split(one.add(mine_b, got_b, sum2), bf16)
    got_b = two.send(sent_b)
    sum_a = two.add(mine_a, got_a, *sent_b).astype(bf16)
    got_a = two.spread(sum_a)
    sum2 = two.join(sum2, got2, sum_a)
    got2 = one.spread(sum2)
    sum_b = two.add(mine_b, got_b, sum2).astype(bf16)
    got_b = two.spread(sum_b)
    sum_a = two.join(sum_a, got_a, sum_b, got)
    got_a = one.spread(sum_a)
    sum_b = two.join(sum_b, got_b, sum_a)
    got_b = one.spread(sum_b)
    input_grad = join(meta, gate(got, sum_b), half_done)
    conv2_grad = assemble([one.join(sum2, got2, input_grad)], [every_tap])
    sum_a = one.join(sum_a, got_a, conv2_grad)
    sum_b = one.join(sum_b, got_b, sum_a)
    conv1_grad = assemble([sum_a, sum_b], [taps_a, taps_b])

    return (
        pooled,
        input_grad,
        conv1_grad,
        gain_one[0],
        bias_one[0],
        conv2_grad,
        gain_two[0],
        bias_two[0],
        head_grad.T,
        bias_grad[0],
        task_weights[0],
        average_next[0],
    )


def solution(mesh):
    in_specs = (
        P("batch", "task", None),
        P(None, "task", None),
        P("task"),
        P("task"),
        P(None, "task", None),
        P("task"),
        P("task"),
        P(None, "task"),
        P("task"),
        P("batch", "task"),
        P(),
        P(),
    )
    out_specs = (
        P("batch", "task"),
        P("batch", "task", None),
        P(None, "task", None),
        P("task"),
        P("task"),
        P(None, "task", None),
        P("task"),
        P("task"),
        P(None, "task"),
        P("task"),
        P(),
        P(),
    )
    return jax.shard_map(
        on_device, mesh=mesh, in_specs=in_specs, out_specs=out_specs, check_vma=False
    )
```

```python
import functools

import jax
import jax.numpy as jnp
from jax import lax
from jax.experimental import pallas as pl
from jax.experimental.pallas import tpu as pltpu
from jax.sharding import PartitionSpec as P

SIDE = 64
FW_STEPS = 20
LANES = 128
ROWS = 8

eps = 1e-05
loss_scale = 4096.0
highest = lax.Precision.HIGHEST
f32 = jnp.float32
bf16 = jnp.bfloat16


def params(mib, **more):
    return pltpu.CompilerParams(vmem_limit_bytes=mib << 20, **more)


def cost(flops, moved):
    return pl.CostEstimate(flops=flops, bytes_accessed=moved, transcendentals=0)


VM = pl.BlockSpec(memory_space=pltpu.VMEM)
HB = pl.BlockSpec(memory_space=pl.ANY)
SM = pl.BlockSpec(memory_space=pltpu.SMEM)


def sigmoid(v):
    return 0.5 + 0.5 * jnp.tanh(0.5 * v)


def silu_slope(v):
    s = sigmoid(v)
    return s * (1.0 + v * (1.0 - s))


def half(h):
    return slice(h * LANES, (h + 1) * LANES)


def held(values):
    return pltpu.with_memory_space_constraint(values, pltpu.VMEM)


def away(values):
    return pltpu.with_memory_space_constraint(values, pltpu.HBM)


def vmem_out(shape, kind):
    return pltpu.VMEM(shape, kind)


def hbm_out(shape, kind):
    return pltpu.HBM(shape, kind)


def column_is(rows, width, at):
    return (lax.broadcasted_iota(jnp.int32, (rows, width), 0) & (SIDE - 1)) == at


def moved(v, e):
    rows, width = v.shape
    if e == 0:
        return v
    edge = SIDE - 1 if e == 1 else 0
    return jnp.where(column_is(rows, width, edge), 0.0, pltpu.roll(v, rows - 1 if e == 1 else 1, 0))


def aligned(cs):
    return cs % LANES == 0


def column_plan(meta, parts, n_parts, cs):
    g, r = meta[1], meta[2]
    plan = []
    for i, part in enumerate(parts):
        if not aligned(cs):
            plan.append((part[0], slice(0, 2 * cs), i * 2 * cs))
            continue
        for s in range(2):
            place = s * n_parts + (r ^ i) if len(part) == 1 else (g, 1 - g)[s] * n_parts + (r ^ i)
            ref, cols = (part[0], slice(s * cs, (s + 1) * cs)) if len(part) == 1 else (part[s], slice(0, cs))
            plan.append((ref, cols, pl.multiple_of(place * cs, cs)))
    return plan


def place_columns(dst, plan, first_row):
    rows = plan[0][0].shape[0]
    block = 512

    def step(j, carry):
        at = pl.multiple_of(j * block, block)
        for ref, cols, to in plan:
            width = cols.stop - cols.start
            dst[pl.ds(pl.multiple_of(at + first_row, SIDE), block), pl.ds(to, width)] = ref[pl.ds(at, block), cols]
        return carry

    lax.fori_loop(0, rows // block, step, 0)


def clear_ends(dst, rows):
    zero = jnp.zeros((SIDE, dst.shape[1]), dst.dtype)
    dst[0:SIDE, :] = zero
    dst[SIDE + rows : SIDE + rows + SIDE, :] = zero


def piece_rows(meta, cs, base, n_pieces):
    g, q = meta[1], meta[4]
    qs = cs // (n_pieces - 1)
    return [pl.ds(pl.multiple_of(base + g * cs, cs), cs)] + [
        pl.ds(pl.multiple_of(base + (1 - g) * cs + (q ^ i if n_pieces > 2 else 0) * qs, qs), qs)
        for i in range(n_pieces - 1)
    ]


def forward_copies(meta, pieces, w, cs, sems):
    if not aligned(cs):
        return [pltpu.make_async_copy(pieces[0], w, sems.at[0])]
    spots = piece_rows(meta, cs, 0, len(pieces))
    return [pltpu.make_async_copy(p, w.at[:, to, :], sems.at[i]) for i, (p, to) in enumerate(zip(pieces, spots))]


def backward_copies(meta, pieces, w, cs, n_parts, sems):
    width = 2 * cs
    if not aligned(cs):
        return [
            pltpu.make_async_copy(p, w.at[:, pl.ds(i * width, width), :], sems.at[i]) for i, p in enumerate(pieces)
        ]
    copies = []
    for i in range(n_parts):
        each = len(pieces) // n_parts
        for p, to in zip(pieces[each * i : each * (i + 1)], piece_rows(meta, cs, i * width, each)):
            for s in range(2):
                cols = pl.ds(pl.multiple_of((s * n_parts + meta[2]) * cs, cs), cs)
                copies.append(
                    pltpu.make_async_copy(p.at[:, :, cols], w.at[:, to, pl.ds(s * cs, cs)], sems.at[len(copies)])
                )
    return copies


def part_half(part, first, rows, h):
    if len(part) == 1:
        return part[0][rows, half(h)].astype(f32)
    own, other = part[0][rows, :], part[1][rows, :]
    return (jnp.where(first, own, other) if h == 0 else jnp.where(first, other, own)).astype(f32)


def row_blocks(rows, block, body, start):
    def step(j, carry):
        return body(pl.ds(pl.multiple_of(j * block, block), block), carry)

    return lax.fori_loop(0, rows // block, step, start)


def send_rows(out, rows, base=None):
    n = out.shape[0]
    start = jnp.zeros((ROWS, LANES), f32) if base is None else base
    out[...] = jnp.broadcast_to(start[None], out.shape)
    for at, value in rows:
        out[:, at : at + 1, :] = jnp.broadcast_to(value[None], (n, 1, LANES))


def weighted(got, weight):
    return jnp.sum(got[...] * weight[...], axis=0)


def norm_coefs(got, weight, rows):
    w = weight[...]
    values = got[...]
    count = jnp.sum(w, axis=0)
    total = jnp.sum(values * w, axis=0)
    mean = total / count
    off = values - mean[None]
    apart = jnp.sum(off * off * w, axis=0)
    squares = total[2:4] + rows * apart[0:2]
    return mean[0:2], lax.rsqrt(squares / (count[0:2] * rows) + eps)


def stream_in(source, buffer, sems, block):
    rows = buffer.shape[0]

    def copy(j):
        at = pl.ds(pl.multiple_of(j * block, block), block)
        return pltpu.make_async_copy(source.at[at, :], buffer.at[at, :], sems.at[j])

    for j in range(rows // block):
        copy(j).start()
    return lambda j: copy(j).wait()


def stream_out(buffer, target, sems, block):
    rows = buffer.shape[0]

    def copy(j):
        at = pl.ds(pl.multiple_of(j * block, block), block)
        return pltpu.make_async_copy(buffer.at[at, :], target.at[at, :], sems.at[j])

    def finish():
        for j in range(rows // block):
            copy(j).wait()

    return (lambda j: copy(j).start()), finish


def stream_scratch(rows, width, block):
    return [pltpu.VMEM((rows, width), f32), pltpu.SemaphoreType.DMA((rows // block,))]


BLOCK = 512
CHUNK = 1024


def fetch_kernel(n_pieces, cs, meta, *refs):
    pieces, (w, sems) = refs[:n_pieces], refs[n_pieces:]
    copies = forward_copies(meta, pieces, w, cs, sems)
    for c in copies:
        c.start()
    for c in copies:
        c.wait()


def fetch(meta, pieces, cs):
    shape = (9, 2 * cs, pieces[0].shape[2])
    return pl.pallas_call(
        functools.partial(fetch_kernel, len(pieces), cs),
        in_specs=[SM] + [HB] * len(pieces),
        out_specs=VM,
        out_shape=vmem_out(shape, bf16),
        scratch_shapes=[pltpu.SemaphoreType.DMA((len(pieces),))],
        compiler_params=params(2),
        name="fetch",
    )(meta, *[away(v) for v in pieces])


def conv_kernel(parts_of, n_parts, meta, extra, w, *refs):
    n = sum(parts_of)
    xs, (target, stats, scratch, out, out_sems) = refs[:n], refs[n:]
    parts, at = [], 0
    for size in parts_of:
        parts.append(xs[at : at + size])
        at += size
    rows, width = out.shape
    cs = width // 2
    chunk = CHUNK
    send, finish = stream_out(out, target, out_sems, chunk)
    clear_ends(scratch, rows)
    place_columns(scratch, column_plan(meta, parts, n_parts, cs), SIDE)
    mean = squares = jnp.zeros((1, width), f32)
    for j in range(rows // chunk):
        at = slice(j * chunk, (j + 1) * chunk)
        total = None
        for dx in (0, 1, -1):
            acc = None
            for dy in (-1, 0, 1):
                lo = at.start + SIDE * (dy + 1)
                tap = w[3 * (dy + 1) + dx + 1]
                term = lax.dot_general(
                    scratch[lo : lo + chunk, :], tap, (((1,), (1,)), ((), ())), preferred_element_type=f32
                )
                acc = term if acc is None else acc + term
            acc = moved(acc, dx)
            total = acc if total is None else total + acc
        out[at, :] = total
        send(j)
        here = jnp.sum(total, axis=0, keepdims=True) / chunk
        off = out[at, :] - here
        spread = jnp.sum(off * off, axis=0, keepdims=True)
        gap = here - mean
        mean = mean + gap / (j + 1.0)
        squares = squares + spread + gap * gap * (chunk * j / (j + 1.0))
    send_rows(
        stats,
        [(h, mean[:, half(h)]) for h in range(width // LANES)]
        + [(2 + h, squares[:, half(h)]) for h in range(width // LANES)],
        extra[...],
    )
    finish()


def conv_stats(meta, extra, w, parts, cs, n_devices, flops):
    rows, width, channels = parts[0][0].shape[0], 2 * cs, w.shape[2]
    flat = [v for part in parts for v in part]
    return pl.pallas_call(
        functools.partial(conv_kernel, [len(p) for p in parts], len(parts)),
        in_specs=[SM, VM, VM] + [VM] * len(flat),
        out_specs=(HB, VM),
        out_shape=(hbm_out((rows, width), f32), vmem_out((n_devices, ROWS, LANES), f32)),
        scratch_shapes=[pltpu.VMEM((rows + 2 * SIDE, channels), bf16), *stream_scratch(rows, width, CHUNK)],
        compiler_params=params(20),
        cost_estimate=cost(flops, 0),
        name="conv_stats",
    )(meta, extra, held(w), *[held(v) for v in flat])


def act_kernel(n_parts, meta, source, got, weight, out, coefs, c, sems):
    rows, width = c.shape
    halves, cs = width // LANES, width // 2
    wait = stream_in(source, c, sems, BLOCK)
    mean, scale = norm_coefs(got, weight, loss_scale)
    coefs[...] = jnp.zeros(coefs.shape, f32)
    coefs[0:2, :] = mean
    coefs[2:4, :] = scale
    for v in range(4):
        for g in range(2):
            row = got[g * n_parts + meta[2], 4 + v : 5 + v, 0:cs]
            lo = g * cs
            coefs[4 + 2 * v + lo // LANES : 5 + 2 * v + lo // LANES, lo % LANES : lo % LANES + cs] = row

    def body(at, carry):
        wait(at.start // BLOCK)
        for h in range(halves):
            normed = (c[at, half(h)] - coefs[h : h + 1, :]) * coefs[2 + h : 3 + h, :]
            normed = normed * coefs[4 + h : 5 + h, :] + coefs[6 + h : 7 + h, :]
            out[at, half(h)] = (normed * sigmoid(normed)).astype(bf16)
        return carry

    row_blocks(rows, BLOCK, body, 0)


def activate(meta, c, got, weight, n_parts):
    rows, width = c.shape
    return pl.pallas_call(
        functools.partial(act_kernel, n_parts),
        in_specs=[SM, HB, VM, VM],
        out_specs=(VM, VM),
        out_shape=(vmem_out((rows, width), bf16), vmem_out((2 * ROWS, LANES), f32)),
        scratch_shapes=stream_scratch(rows, width, BLOCK),
        compiler_params=params(12),
        cost_estimate=cost(0, 0),
        name="activate",
    )(meta, away(c), held(got), weight)


def turn_kernel(meta, images, own, other, buffer, sems):
    g = meta[1]
    rows = own.shape[0]
    block = 1024
    n = rows // block

    def copy(i, s):
        cols = pl.ds(pl.multiple_of(i * block, block), block)
        which = (1 - g, g)[s]
        return pltpu.make_async_copy(images.at[which, :, cols], buffer.at[s, :, cols], sems.at[s, i])

    for s in range(2):
        for i in range(n):
            copy(i, s).start()
    for s, out in ((0, other), (1, own)):

        def step(i, carry, s=s, out=out):
            copy(i, s).wait()
            cols = pl.ds(pl.multiple_of(i * block, block), block)
            out[cols, :] = buffer[s, :, cols].T
            return carry

        lax.fori_loop(0, n, step, 0)


def turn(meta, images):
    slots, cs, rows = images.shape
    return pl.pallas_call(
        turn_kernel,
        in_specs=[SM, HB],
        out_specs=(VM, VM),
        out_shape=(vmem_out((rows, cs), bf16),) * 2,
        scratch_shapes=[pltpu.VMEM((slots, cs, rows), bf16), pltpu.SemaphoreType.DMA((slots, rows // 1024))],
        compiler_params=params(8),
        cost_estimate=cost(0, 0),
        name="turn",
    )(meta, away(images))


def join_kernel(meta, got, half_done, out, buffer, sems):
    cs, rows = got.shape
    block = 1024
    n = rows // block
    del half_done

    def copy(i):
        cols = pl.ds(pl.multiple_of(i * block, block), block)
        return pltpu.make_async_copy(buffer.at[:, cols], out.at[1 - meta[1], :, cols], sems.at[i])

    for i in range(n):
        cols = slice(i * block, (i + 1) * block)
        buffer[:, cols] = got[:, cols].astype(f32)
        copy(i).start()
    for i in range(n):
        copy(i).wait()


def join(meta, got, half_done):
    cs, rows = got.shape
    return pl.pallas_call(
        join_kernel,
        in_specs=[SM, VM, HB],
        out_specs=HB,
        out_shape=hbm_out(half_done.shape, f32),
        scratch_shapes=[pltpu.VMEM((cs, rows), f32), pltpu.SemaphoreType.DMA((rows // 1024,))],
        input_output_aliases={2: 0},
        compiler_params=params(8),
        cost_estimate=cost(0, 0),
        name="join",
    )(meta, held(got), away(half_done))


def pool_kernel(n_x, meta, source, *refs):
    x, (got, weight, coefs1, labels, out, coefs, c, sems) = refs[:n_x], refs[n_x:]
    rows, width = c.shape
    halves = width // LANES
    first = meta[1] == 0
    wait = stream_in(source, c, sems, BLOCK)
    mean, scale = norm_coefs(got, weight, loss_scale)
    coefs[...] = jnp.zeros(coefs.shape, f32)
    coefs[0:2, :] = mean
    coefs[2:4, :] = scale

    def body(at, carry):
        wait(at.start // BLOCK)
        sums = list(carry)
        for h in range(halves):
            hat = (c[at, half(h)] - coefs[h : h + 1, :]) * coefs[2 + h : 3 + h, :]
            v = hat * coefs1[8 + h : 9 + h, :] + coefs1[10 + h : 11 + h, :] + part_half(x, first, at, h)
            s = sigmoid(v)
            slope = s * (1.0 + v * (1.0 - s))
            sums[3 * h] += jnp.sum(v * s, axis=0, keepdims=True)
            sums[3 * h + 1] += jnp.sum(slope * hat, axis=0, keepdims=True)
            sums[3 * h + 2] += jnp.sum(slope, axis=0, keepdims=True)
        return tuple(sums)

    sums = row_blocks(rows, BLOCK, body, (jnp.zeros((1, LANES), f32),) * (3 * halves))
    valid = meta[3].astype(f32)
    lines = [(6, labels[0:1, :]), (7, labels[1:2, :])]
    for h in range(halves):
        lines.append((h, sums[3 * h] * (valid / loss_scale)))
        lines.append((2 + h, sums[3 * h + 1]))
        lines.append((4 + h, sums[3 * h + 2]))
    send_rows(out, lines)


def pool(meta, c, x, got, weight, coefs1, labels):
    rows, width = c.shape
    return pl.pallas_call(
        functools.partial(pool_kernel, len(x)),
        in_specs=[SM, HB] + [VM] * (4 + len(x)),
        out_specs=(VM, VM),
        out_shape=(vmem_out(got.shape, f32), vmem_out((ROWS, LANES), f32)),
        scratch_shapes=stream_scratch(rows, width, BLOCK),
        compiler_params=params(12),
        cost_estimate=cost(0, 0),
        name="pool",
    )(meta, away(c), *[held(v) for v in x], held(got), weight, held(coefs1), labels)


def own_lanes(first, v, cs):
    return jnp.where(first, v[:, :cs], v[:, cs:])


def head_kernel(n_parts, n_ahead, meta, got, heads, stats, valid, avg_row, avg_col, *refs):
    sources, refs = refs[:n_ahead], refs[n_ahead:]
    (coefs, tw, an, hwg, hbg, pooled_own, gain_own, shift_own), ahead, refs = refs[:8], refs[8 : 8 + n_ahead], refs[8 + n_ahead :]
    pooled, slopes, shifts, labels, grads, mine_all, pooled_part, ht, sems = refs
    early = [pltpu.make_async_copy(v, to, sems.at[i]) for i, (v, to) in enumerate(zip(sources, ahead))]
    for c in early:
        c.start()
    tasks, channels = ht.shape
    images = valid.shape[0]
    n_task = 2 * n_parts
    width = channels // n_parts
    cs = width // 2
    halves = width // LANES
    tasks_here = tasks // n_task
    r = meta[2]
    first = meta[1] == 0
    for part in range(n_parts):
        for s in range(2):
            lo, at = part * width + s * cs, (s * n_parts + part) * cs
            ht[:, lo : lo + cs] = heads[:, at : at + cs]
    bias = stats[0, 4:5, :]
    for t in range(1, n_task):
        bias = bias + stats[t, 4:5, :]
    for n in range(images):
        base = (n // 2) * n_task + (n % 2) * n_parts
        for part in range(n_parts):
            for h in range(halves):
                lo = part * width + h * LANES
                pooled[n : n + 1, lo : lo + LANES] = got[base + part, h : h + 1, :]
        for h in range(halves):
            slopes[n : n + 1, half(h)] = got[base + r, 2 + h : 3 + h, :]
            shifts[n : n + 1, half(h)] = got[base + r, 4 + h : 5 + h, :]
        row = 6 + n % 2
        lab = got[(n // 2) * n_task, row : row + 1, :]
        for t in range(1, n_task):
            lab = lab + got[(n // 2) * n_task + t, row : row + 1, :]
        labels[n : n + 1, :] = lab
    pooled_all = pooled[...]
    table = ht[...]
    both_last = (((1,), (1,)), ((), ()))
    both_first = (((0,), (0,)), ((), ()))
    logits = lax.dot_general(pooled_all, table, both_last, precision=highest, preferred_element_type=f32)
    logits = logits + bias[:, 0:tasks]
    count = jnp.sum(valid[...], axis=0, keepdims=True)
    errors = valid[...] * (1.0 / (1.0 + jnp.exp(-logits)) - labels[:, 0:tasks]) / count
    gram = lax.dot_general(errors, errors, both_first, precision=highest, preferred_element_type=f32) * lax.dot_general(
        table, table, both_last, precision=highest, preferred_element_type=f32
    )
    row_id = lax.broadcasted_iota(jnp.int32, (tasks, tasks), 0)
    col_id = lax.broadcasted_iota(jnp.int32, (tasks, tasks), 1)
    trace = jnp.sum(jnp.sum(jnp.where(row_id == col_id, gram, 0.0), axis=1, keepdims=True), axis=0, keepdims=True)
    normalized = gram / (trace / tasks)
    start_row = avg_row[...] / jnp.sum(avg_row[...], axis=1, keepdims=True)
    start_col = avg_col[...] / jnp.sum(avg_col[...], axis=0, keepdims=True)
    w_row, w_col = start_row, start_col
    for j in range(FW_STEPS):
        rate = 1.0 / (j + 4.0)
        z_col = -tasks * jnp.sum(normalized * w_row, axis=1, keepdims=True)
        z_row = -tasks * jnp.sum(normalized * w_col, axis=0, keepdims=True)
        e_col = jnp.exp(z_col - jnp.max(z_col, axis=0, keepdims=True))
        e_row = jnp.exp(z_row - jnp.max(z_row, axis=1, keepdims=True))
        w_col = (1.0 - rate) * w_col + rate * (e_col / jnp.sum(e_col, axis=0, keepdims=True))
        w_row = (1.0 - rate) * w_row + rate * (e_row / jnp.sum(e_row, axis=1, keepdims=True))
    tw[...] = w_row
    an[...] = 0.9 * start_row + 0.1 * w_row
    logit_grads = errors * ((loss_scale * tasks) * w_row)
    task_id = lax.broadcasted_iota(jnp.int32, (tasks, tasks_here), 0) - (meta[1] * n_parts + r) * tasks_here
    mine = (task_id == lax.broadcasted_iota(jnp.int32, (tasks, tasks_here), 1)).astype(f32)
    own_grads = jnp.dot(logit_grads, mine, precision=highest, preferred_element_type=f32)
    hbg[...] = jnp.sum(own_grads, axis=0, keepdims=True)
    by_part = lax.dot_general(own_grads, pooled_all, both_first, precision=highest, preferred_element_type=f32)
    for part in range(n_parts):
        for s in range(2):
            lo, at = part * width + s * cs, (s * n_parts + part) * cs
            hwg[:, at : at + cs] = by_part[:, lo : lo + cs]
    grads[...] = jnp.dot(logit_grads, table, precision=highest, preferred_element_type=f32) / loss_scale
    own = pl.ds(pl.multiple_of(r * width, LANES), width)
    q = grads[:, own]
    mine_all[...] = q
    pooled_part[...] = pooled[:, own]
    gain = jnp.sum(q * slopes[...], axis=0, keepdims=True)
    shift = jnp.sum(q * shifts[...], axis=0, keepdims=True)
    here = mine_all[pl.ds(2 * meta[0] + meta[1], 1), :]
    coefs[...] = jnp.zeros(coefs.shape, f32)
    for h in range(halves):
        coefs[h : h + 1, :] = gain[:, half(h)]
        coefs[2 + h : 3 + h, :] = shift[:, half(h)]
        coefs[4 + h : 5 + h, :] = here[:, half(h)]
    gain_own[...] = own_lanes(first, gain, cs)
    shift_own[...] = own_lanes(first, shift, cs)
    for i in range(2):
        pooled_own[i : i + 1, :] = own_lanes(first, pooled_part[pl.ds(2 * meta[0] + i, 1), :], cs)
    for c in early:
        c.wait()


def head(meta, got, heads, stats, valid, avg_row, avg_col, n_parts, sources):
    tasks, channels = heads.shape
    images = valid.shape[0]
    width = channels // n_parts
    cs = width // 2
    tasks_here = tasks // (2 * n_parts)
    shapes = [(1, tasks), (1, tasks), (tasks_here, channels), (1, tasks_here), (2, cs), (1, cs), (1, cs)]
    return pl.pallas_call(
        functools.partial(head_kernel, n_parts, len(sources)),
        in_specs=[SM] + [VM] * 6 + [HB] * len(sources),
        out_specs=(VM,) * (8 + len(sources)),
        out_shape=(vmem_out((ROWS, LANES), f32),)
        + tuple(hbm_out(s, f32) for s in shapes)
        + tuple(vmem_out(v.shape, v.dtype) for v in sources),
        scratch_shapes=[
            pltpu.VMEM((images, channels), f32),
            pltpu.VMEM((images, width), f32),
            pltpu.VMEM((images, width), f32),
            pltpu.VMEM((images, LANES), f32),
            pltpu.VMEM((images, channels), f32),
            pltpu.VMEM((images, width), f32),
            pltpu.VMEM((images, width), f32),
            pltpu.VMEM((tasks, channels), f32),
            pltpu.SemaphoreType.DMA((len(sources),)),
        ],
        compiler_params=params(6),
        cost_estimate=cost(1 << 20, 1 << 20),
        name="head",
    )(meta, got, heads, stats, valid, avg_row, avg_col, *[away(v) for v in sources])


def grad_two_kernel(n_x, n_ahead, meta, c, *refs):
    x, (coefs, coefs1, heads, pixels), refs = refs[:n_x], refs[n_x : n_x + 4], refs[n_x + 4 :]
    sources, (low, target), refs = refs[:n_ahead], refs[n_ahead : n_ahead + 2], refs[n_ahead + 2 :]
    ahead, (summed, out_sems, sems) = refs[:n_ahead], refs[n_ahead:]
    early = [pltpu.make_async_copy(v, to, sems.at[i]) for i, (v, to) in enumerate(zip(sources, ahead))]
    for copy in early:
        copy.start()
    rows, width = c.shape
    valid = meta[3].astype(f32)
    first = meta[1] == 0
    send, finish = stream_out(summed, target, out_sems, BLOCK)

    def body(at, carry):
        for h in range(width // LANES):
            mean, scale = coefs[h : h + 1, :], coefs[2 + h : 3 + h, :]
            gain = coefs1[8 + h : 9 + h, :]
            hat = (c[at, half(h)] - mean) * scale
            v = hat * gain + coefs1[10 + h : 11 + h, :] + part_half(x, first, at, h)
            dn = (valid * heads[4 + h : 5 + h, :]) * silu_slope(v)
            summed[at, half(h)] = dn
            away = (heads[2 + h : 3 + h, :] + hat * heads[h : h + 1, :]) / pixels[0]
            low[at, half(h)] = ((valid * gain * scale) * (dn - away)).astype(bf16)
        send(at.start // BLOCK)
        return carry

    row_blocks(rows, BLOCK, body, 0)
    finish()
    for copy in early:
        copy.wait()


def grad_two(meta, c, x, coefs, coefs1, heads, pixels, sources):
    rows, width = c.shape
    return pl.pallas_call(
        functools.partial(grad_two_kernel, len(x), len(sources)),
        in_specs=[SM] + [VM] * (4 + len(x)) + [SM] + [HB] * len(sources),
        out_specs=(VM, HB) + (VM,) * len(sources),
        out_shape=(vmem_out((rows, width), bf16), hbm_out((rows, width), f32))
        + tuple(vmem_out(v.shape, v.dtype) for v in sources),
        scratch_shapes=stream_scratch(rows, width, BLOCK) + [pltpu.SemaphoreType.DMA((len(sources),))],
        compiler_params=params(10),
        cost_estimate=cost(0, 0),
        name="grad_two",
    )(meta, held(c), *[held(v) for v in x], held(coefs), held(coefs1), held(heads), pixels, *[away(v) for v in sources])


def grad_one_kernel(meta, c_source, dn_source, got, weight, coefs, pixels, low, gain_own, bias_own, c, c_sems, dn, dn_sems, sums):
    rows, width = c.shape
    valid = meta[3].astype(f32)
    wait_c = stream_in(c_source, c, c_sems, BLOCK)
    wait_dn = stream_in(dn_source, dn, dn_sems, BLOCK)
    sums[...] = weighted(got, weight)
    first = meta[1] == 0
    for out, at in ((gain_own, 0), (bias_own, 2)):
        line = jnp.concatenate([sums[at + h : at + h + 1, :] for h in range(width // LANES)], axis=1)
        out[...] = own_lanes(first, line, width // 2)

    def body(at, carry):
        wait_c(at.start // BLOCK)
        wait_dn(at.start // BLOCK)
        for h in range(width // LANES):
            mean, scale = coefs[h : h + 1, :], coefs[2 + h : 3 + h, :]
            hat = (c[at, half(h)] - mean) * scale
            away = (sums[2 + h : 3 + h, :] + hat * sums[h : h + 1, :]) / pixels[0]
            low[at, half(h)] = ((valid * coefs[4 + h : 5 + h, :] * scale) * (dn[at, half(h)] - away)).astype(bf16)
        return carry

    row_blocks(rows, BLOCK, body, 0)


def grad_one(meta, c, dn, got, weight, coefs, pixels):
    rows, width = c.shape
    return pl.pallas_call(
        grad_one_kernel,
        in_specs=[SM, HB, HB] + [VM] * 3 + [SM],
        out_specs=(VM, VM, VM),
        out_shape=(vmem_out((rows, width), bf16), hbm_out((1, width // 2), f32), hbm_out((1, width // 2), f32)),
        scratch_shapes=stream_scratch(rows, width, BLOCK) * 2 + [pltpu.VMEM((ROWS, LANES), f32)],
        compiler_params=params(24),
        cost_estimate=cost(0, 0),
        name="grad_one",
    )(meta, away(c), away(dn), held(got), weight, held(coefs), pixels)


def back_setup(gs, scratch):
    rows, width = gs[0].shape
    clear_ends(scratch, rows)
    place_columns(scratch, [(g, slice(0, width), i * width) for i, g in enumerate(gs)], SIDE)


def back_products(scratch, w, at, chunk):
    total = None
    for dx in (0, 1, -1):
        acc = None
        for dy in (-1, 0, 1):
            lo = at + SIDE * (1 - dy)
            term = jnp.dot(scratch[lo : lo + chunk, :], w[3 * (dy + 1) + dx + 1], preferred_element_type=f32)
            acc = term if acc is None else acc + term
        acc = moved(acc, -dx)
        total = acc if total is None else total + acc
    return total


def back_two_kernel(n_parts, meta, w, c, coefs, *refs):
    gs, (target, stats, scratch, out, out_sems) = refs[:n_parts], refs[n_parts:]
    rows, width = out.shape
    halves = width // LANES
    chunk = CHUNK
    n = rows // chunk
    push, finish = stream_out(out, target, out_sems, chunk)
    back_setup(gs, scratch)
    sums = [jnp.zeros((1, LANES), f32)] * (2 * halves)

    def finish_chunk(j):
        at = slice(j * chunk, (j + 1) * chunk)
        for h in range(halves):
            hat = (c[at, half(h)] - coefs[h : h + 1, :]) * coefs[2 + h : 3 + h, :]
            dn = out[at, half(h)] * silu_slope(hat * coefs[4 + h : 5 + h, :] + coefs[6 + h : 7 + h, :])
            out[at, half(h)] = dn
            sums[2 * h] += jnp.sum(dn * hat, axis=0, keepdims=True)
            sums[2 * h + 1] += jnp.sum(dn, axis=0, keepdims=True)
        push(j)

    for j in range(n):
        out[j * chunk : (j + 1) * chunk, :] = back_products(scratch, w, j * chunk, chunk)
        if j:
            finish_chunk(j - 1)
    finish_chunk(n - 1)
    send_rows(stats, [(2 * i + h, sums[2 * h + i]) for h in range(halves) for i in range(2)])
    finish()


def back_two(meta, w, c, coefs, g_parts, n_devices):
    rows, width = c.shape
    n = len(g_parts)
    return pl.pallas_call(
        functools.partial(back_two_kernel, n),
        in_specs=[SM] + [VM] * (n + 3),
        out_specs=(HB, VM),
        out_shape=(hbm_out((rows, width), f32), vmem_out((n_devices, ROWS, LANES), f32)),
        scratch_shapes=[pltpu.VMEM((rows + 2 * SIDE, n * width), bf16), *stream_scratch(rows, width, CHUNK)],
        compiler_params=params(20),
        cost_estimate=cost(2 * 9 * rows * width * width * n, 16 << 20),
        name="back_two",
    )(meta, held(w), held(c), held(coefs), *[held(v) for v in g_parts])


def back_one_kernel(n_parts, meta, w, summed, *refs):
    gs, (out, send, scratch, acc, keep, keep_sems) = refs[:n_parts], refs[n_parts:]
    rows, width = summed.shape
    cs = width // 2
    chunk = CHUNK
    n = rows // chunk
    g = meta[1]
    first = g == 0
    back_setup(gs, scratch)

    def copy(j):
        cols = pl.ds(j * chunk, chunk)
        return pltpu.make_async_copy(keep.at[:, cols], out.at[g, :, cols], keep_sems.at[j])

    def finish_chunk(j):
        at = slice(j * chunk, (j + 1) * chunk)
        total = acc[j % 2] + summed[at, :]
        a, b = total[:, :cs], total[:, cs:]
        keep[:, at] = jnp.where(first, a, b).T
        copy(j).start()
        send[:, at] = jnp.where(first, b, a).T.astype(bf16)

    for j in range(n):
        acc[j % 2] = back_products(scratch, w, j * chunk, chunk)
        if j:
            finish_chunk(j - 1)
    finish_chunk(n - 1)
    for j in range(n):
        copy(j).wait()


def back_one(meta, w, summed, g_parts):
    rows, width = summed.shape
    n = len(g_parts)
    cs = width // 2
    return pl.pallas_call(
        functools.partial(back_one_kernel, n),
        in_specs=[SM] + [VM] * (n + 2),
        out_specs=(HB, VM),
        out_shape=(hbm_out((2, cs, rows), f32), vmem_out((cs, rows), bf16)),
        scratch_shapes=[
            pltpu.VMEM((rows + 2 * SIDE, n * width), bf16),
            pltpu.VMEM((2, CHUNK, width), f32),
            pltpu.VMEM((cs, rows), f32),
            pltpu.SemaphoreType.DMA((rows // CHUNK,)),
        ],
        compiler_params=params(24),
        cost_estimate=cost(2 * 9 * rows * width * width * n, 16 << 20),
        name="back_one",
    )(meta, held(w), held(summed), *[held(v) for v in g_parts])


def weight_kernel(sizes, n_parts, taps, n_pieces, sends, meta, g, *refs):
    n = sum(sizes)
    xs, refs = refs[:n], refs[n:]
    if n_pieces:
        pieces, source, refs = refs[:n_pieces], refs[n_pieces], refs[n_pieces + 1 :]
    keep, send, refs = refs[0], refs[1 : 1 + len(sends)], refs[1 + len(sends) :]
    if n_pieces:
        w, ahead, shifted, x, sems = refs
    else:
        shifted, x = refs
    rows, width = g.shape
    cs = width // 2
    first = meta[1] == 0
    copies = []
    if n_pieces:
        copies = backward_copies(meta, pieces, w, cs, n_parts, sems)
        copies.append(pltpu.make_async_copy(source, ahead, sems.at[len(copies)]))
    for c in copies:
        c.start()
    parts, at = [], 0
    for size in sizes:
        parts.append(xs[at : at + size])
        at += size
    place_columns(x, column_plan(meta, parts, n_parts, cs), 0)
    moves = sorted({1 - k % 3 for k in taps})
    for i in range(len(moves)):
        clear_ends(shifted.at[i], rows)

    def shift(at, carry):
        low = g[at, :]
        value = low.astype(f32)
        to = pl.ds(pl.multiple_of(at.start + SIDE, SIDE), at.size)
        for i, e in enumerate(moves):
            shifted[i, to, :] = moved(value, e).astype(bf16) if e else low
        return carry

    row_blocks(rows, BLOCK, shift, 0)
    for j, k in enumerate(taps):
        lo = SIDE * (2 - k // 3)
        lhs = shifted[moves.index(1 - k % 3), lo : lo + rows, :]
        term = lax.dot_general(lhs, x[...], (((0,), (0,)), ((), ())), preferred_element_type=f32)
        a, b = term[:cs], term[cs:]
        keep[j] = jnp.where(first, a, b)
        which = int(j >= sends[0])
        send[which][j - which * sends[0]] = jnp.where(first, b, a).astype(bf16)
    for c in copies:
        c.wait()


def weight_grad(meta, g, parts, n_parts, taps, pieces=(), source=None, early=None):
    rows, width = g.shape
    flat = [v for p in parts for v in p]
    columns = n_parts * width
    shape = (len(taps), width // 2, columns)
    sends = [len(taps)] if early is None else [early, len(taps) - early]
    extra = [away(v) for v in (*pieces, source)] if pieces else []
    ahead = (vmem_out((9, columns, width), bf16), vmem_out(source.shape, f32)) if pieces else ()
    return pl.pallas_call(
        functools.partial(weight_kernel, [len(p) for p in parts], n_parts, taps, len(pieces), sends),
        in_specs=[SM] + [VM] * (len(flat) + 1) + [HB] * len(extra),
        out_specs=(VM,) * (1 + len(sends) + len(ahead)),
        out_shape=(vmem_out(shape, f32), *[vmem_out((n, *shape[1:]), bf16) for n in sends], *ahead),
        scratch_shapes=[
            pltpu.VMEM((len({k % 3 for k in taps}), rows + 2 * SIDE, width), bf16),
            pltpu.VMEM((rows, columns), bf16),
        ]
        + ([pltpu.SemaphoreType.DMA((10 * n_parts + 1,))] if pieces else []),
        compiler_params=params(24),
        cost_estimate=cost(2 * len(taps) * rows * width * columns, 16 << 20),
        name="weight_grad",
    )(meta, held(g), *[held(v) for v in flat], *extra)


def swap(values, axis, by):
    n = lax.axis_size(axis)
    return lax.ppermute(values, axis, [(i, i ^ by) for i in range(n)])


def xor_order(values, r):
    bit = 1
    while bit < len(values):
        flip = (r & bit) != 0
        values = [jnp.where(flip, values[i ^ bit], v) for i, v in enumerate(values)]
        bit *= 2
    return values


def gate(values, *others):
    return lax.optimization_barrier((values, *others))[0]


class Stage:
    def __init__(self, stride, size):
        self.stride, self.size = stride, size
        k = (lax.axis_index("batch").astype(jnp.uint32) >> (stride.bit_length() - 1)) & (size - 1)
        self.order = [k ^ j for j in range(size)]
        self.bits = [(k & (1 << i)) != 0 for i in range(size.bit_length() - 1)]

    def scalars(self):
        return [*self.order, *self.bits]

    def settle(self, scalars):
        self.order, self.bits = list(scalars[: self.size]), list(scalars[self.size :])

    def split(self, total, kind):
        pieces = total.reshape(self.size, -1, total.shape[1])
        mine, *others = [lax.dynamic_index_in_dim(pieces, k, keepdims=False) for k in self.order]
        return mine, [v.astype(kind) for v in others]

    def send(self, sent):
        return [swap(v, "batch", self.stride * j) for j, v in enumerate(sent, 1)]

    def add(self, mine, got, *after):
        for v in got:
            mine = mine + gate(v, *after).astype(f32)
        return mine

    def spread(self, out):
        return [swap(out, "batch", self.stride * j) for j in range(1, self.size)]

    def join(self, out, got, *after):
        pieces = [out] + [gate(v, *after) for v in got]
        for i, flip in enumerate(self.bits):
            pieces = [jnp.where(flip, pieces[j ^ (1 << i)], v) for j, v in enumerate(pieces)]
        return jnp.concatenate(pieces, axis=0)


def on_device(
    images,
    conv1_weight,
    norm1_gain,
    norm1_bias,
    conv2_weight,
    norm2_gain,
    norm2_bias,
    head_weight,
    head_bias,
    labels,
    image_counts,
    average_weights,
):
    n_task, n_batch = lax.axis_size("task"), lax.axis_size("batch")
    t, b = lax.axis_index("task"), lax.axis_index("batch")
    slots, cs, pixels = images.shape
    n_parts = n_task // slots
    g, r = t // n_parts, t % n_parts
    first = g == 0
    width = slots * cs
    channels = n_task * cs
    n_devices = n_task * n_batch
    tasks_here = head_weight.shape[1]
    tasks = tasks_here * n_task

    valid_images = (jnp.arange(slots)[None, :] < image_counts[:, None]).astype(f32)
    image_total = jnp.sum(image_counts).astype(f32)
    pixel_total = (image_total * pixels).reshape(1)
    own_valid = (g < lax.dynamic_index_in_dim(image_counts, b, keepdims=False)).astype(jnp.int32)
    place = jnp.stack([b, g, r, 0 * b, b % 4]).astype(jnp.int32)
    meta = jnp.stack([b, g, r, own_valid, b % 4]).astype(jnp.int32)
    same = (jnp.arange(n_parts) == r).astype(f32)
    weight = (valid_images[:, :, None] * same[None, None, :]).reshape(n_devices, 1)
    weight = jnp.broadcast_to(weight[:, :, None], (n_devices, ROWS, LANES))

    def relative(w):
        blocks = [w[..., i * cs : (i + 1) * cs] for i in range(n_task)]
        order = [xor_order(blocks[s * n_parts : (s + 1) * n_parts], r) for s in range(slots)]
        return [jnp.concatenate([order[s][i] for s in range(slots)], axis=-1) for i in range(n_parts)]

    def ordered(own, other, axis):
        return jnp.concatenate([jnp.where(first, own, other), jnp.where(first, other, own)], axis=axis)

    def joined(pieces):
        other = jnp.concatenate(xor_order(list(pieces[1:]), b % 4 if len(pieces) > 2 else 0), axis=1)
        return relative(ordered(pieces[0], other, 1))

    def forward_pieces(pieces):
        return pieces if aligned(cs) else [jnp.concatenate(joined(pieces), axis=2)]

    def backward_pieces(pieces, done=()):
        if aligned(cs):
            parts = [[swap(v, "task", i) if i else v for v in pieces[len(done) > 0 :]] for i in range(n_parts)]
            return [v for i, part in enumerate(parts) for v in ([done[i]] if done else []) + part]
        return [swap(v, "task", i) if i else v for i, v in enumerate(joined(pieces))]

    def all_parts(v):
        return [v] + [swap(v, "task", i) for i in range(1, n_parts)]

    quarter = lax.dynamic_index_in_dim(
        conv1_weight.reshape(9, 4, cs // 4, channels), b % 4, axis=1, keepdims=False
    ).reshape(-1, channels)
    own_heads = jnp.pad(head_weight.T, ((0, -tasks_here % ROWS), (0, 0)))
    near, near_heads = swap(quarter, "task", n_parts), swap(own_heads, "task", n_parts)
    x_own, x_send = turn(gate(place, quarter), images)
    x_other = swap(gate(x_send, near, near_heads), "task", n_parts)

    vecs = jnp.stack([norm1_gain, norm1_bias, norm2_gain, norm2_bias])
    vecs = jnp.pad(vecs, ((4, 0), (0, LANES - cs)))
    bias_rows = lax.dynamic_update_slice(jnp.zeros((ROWS, LANES), f32), head_bias[None], (4, t * tasks_here))
    label_rows = lax.dynamic_update_slice(
        jnp.zeros((slots, LANES), f32), labels.astype(f32), (0, t * tasks_here)
    )
    columns = [bias_rows, label_rows, vecs, valid_images.reshape(-1, 1), average_weights.reshape(-1, 1)]

    near1 = gate(near, x_send).reshape(9, cs // 4, channels)
    side = swap(near1, "batch", 1)
    w1 = [conv1_weight, near1, side, swap(near1, "batch", 2), swap(side, "batch", 2)]
    w2 = [conv2_weight, swap(gate(conv2_weight, near1), "task", n_parts)]
    both_heads = jnp.concatenate([own_heads, near_heads])
    every = xor_order([both_heads] + [swap(both_heads, "task", i) for i in range(1, n_parts)], r)
    every = jnp.stack(every).reshape(n_parts, slots, -1, channels)[:, :, :tasks_here]
    table = jnp.where(first, every, jnp.flip(every, 1)).swapaxes(0, 1).reshape(tasks, channels).astype(f32)
    forward1 = fetch(place, forward_pieces(w1), cs)
    own2 = [swap(conv2_weight, "task", i) if i else conv2_weight for i in range(n_parts)] if aligned(cs) else ()
    turned1 = backward_pieces(w1)
    low_bits = 1 << ((n_batch.bit_length() - 1) // 2)
    one, two = Stage(1, low_bits), Stage(low_bits, n_batch // low_bits)
    x_other, *scalars = lax.optimization_barrier((x_other, *one.scalars(), *two.scalars()))
    one.settle(scalars[: len(one.scalars())])
    two.settle(scalars[len(one.scalars()) :])
    if aligned(cs):
        x_parts = list(zip(all_parts(x_own), all_parts(gate(x_other, *w1, weight, vecs, forward1, table, *turned1, *own2, *columns))))
    else:
        x_parts = [[v] for v in all_parts(ordered(x_own, x_other, 1))]

    def exchange(rows):
        flat_rows = rows.reshape(n_devices * ROWS, LANES)
        return lax.all_to_all(flat_rows, ("batch", "task"), 0, 0, tiled=True).reshape(rows.shape)

    c1, stats = conv_stats(place, vecs, forward1, x_parts, cs, n_devices, 0)
    totals = exchange(stats)
    a_own, coefs1 = activate(meta, c1, totals, gate(weight, w2[1]), n_parts)
    a_parts = [[v] for v in all_parts(a_own)]
    forward2 = fetch(place, [gate(w2[0], a_own), *forward_pieces(w2)[1:]] if aligned(cs) else forward_pieces(w2), cs)
    c2, stats = conv_stats(place, bias_rows, forward2, a_parts, cs, n_devices, 18 * pixels * width * channels)
    stats2 = exchange(stats)
    sums, coefs2 = pool(meta, c2, x_parts[0], stats2, weight, coefs1, label_rows)
    turned2 = backward_pieces([w2[0], gate(w2[1], sums)], own2)
    heads, task_weights, average_next, head_grad, bias_grad, pooled, gain_two, bias_two, *ahead = head(
        meta,
        exchange(sums),
        table,
        stats2,
        gate(columns[3], *turned2),
        average_weights.reshape(1, -1),
        columns[4],
        n_parts,
        [c2, *x_parts[0]],
    )

    def both_groups(keep, got, *after):
        return (keep + gate(got, *after).astype(f32)).reshape(-1, channels)

    def assemble(done, taps):
        where = {k: (v, j) for v, ks in zip(done, taps) for j, k in enumerate(ks)}
        out = jnp.concatenate([where[k][0][where[k][1] * cs : (where[k][1] + 1) * cs] for k in range(9)])
        out = out.reshape(9, cs, channels)
        if not aligned(cs):
            parts = [out[:, :, i * width : (i + 1) * width] for i in range(n_parts)]
            order = [v for s in range(slots) for v in xor_order([p[:, :, s * cs : (s + 1) * cs] for p in parts], r)]
            out = jnp.concatenate(order, axis=2)
        return out.astype(f32)

    taps_a, taps_b = (0, 3, 6, 1), (4, 7, 2, 5, 8)
    every_tap = taps_b + taps_a
    low2, summed, *a_near = grad_two(
        meta, ahead[0], ahead[1:], coefs2, coefs1, heads, pixel_total, [v for p in a_parts for v in p]
    )
    a_near = [[v] for v in a_near]
    low2_parts = all_parts(low2)
    keep2, send2, late2, back2, c1_near = weight_grad(meta, low2, a_near, n_parts, every_tap, turned2, c1, 6)
    got2 = swap(send2, "task", n_parts)
    low2_parts[0] = gate(low2_parts[0], keep2)
    dn1, stats = back_two(meta, back2, c1_near, coefs1, low2_parts, n_devices)
    totals = exchange(stats)
    got2 = jnp.concatenate([got2, swap(gate(late2, totals), "task", n_parts)])
    low1, gain_one, bias_one = grad_one(meta, c1, dn1, totals, weight, coefs1, pixel_total)
    low1_parts = all_parts(low1)

    keep_a, send_a = weight_grad(meta, low1, x_parts, n_parts, taps_a)
    got_a = swap(send_a, "task", n_parts)
    mine2, sent2 = one.split(both_groups(keep2, got2, keep_a), bf16)
    got2 = one.send(sent2)
    keep_b, send_b, back1, summed = weight_grad(
        meta, gate(low1, keep_a, *sent2), x_parts, n_parts, taps_b, turned1, summed
    )
    got_b = swap(send_b, "task", n_parts)
    mine2, sent2 = two.split(one.add(mine2, got2, keep_b), f32)
    got2 = two.send(sent2)
    mine_a, sent_a = one.split(both_groups(keep_a, got_a, keep_b, *sent2), bf16)
    got_a = one.send(sent_a)
    low1_parts[0] = gate(low1_parts[0], *sent_a)
    half_done, send = back_one(meta, back1, summed, low1_parts)
    got = swap(send, "task", n_parts)
    mine_b, sent_b = one.split(both_groups(keep_b, got_b, send), bf16)
    got_b = one.send(sent_b)
    mine_a, sent_a = two.split(one.add(mine_a, got_a, *sent_b), bf16)
    got_a = two.send(sent_a)
    sum2 = two.add(mine2, got2, *sent_a).astype(bf16)
    got2 = two.spread(sum2)
    mine_b, sent_b = two.split(one.add(mine_b, got_b, sum2), bf16)
    got_b = two.send(sent_b)
    sum_a = two.add(mine_a, got_a, *sent_b).astype(bf16)
    got_a = two.spread(sum_a)
    sum2 = two.join(sum2, got2, sum_a)
    got2 = one.spread(sum2)
    sum_b = two.add(mine_b, got_b, sum2).astype(bf16)
    got_b = two.spread(sum_b)
    sum_a = two.join(sum_a, got_a, sum_b, got)
    got_a = one.spread(sum_a)
    sum_b = two.join(sum_b, got_b, sum_a)
    got_b = one.spread(sum_b)
    input_grad = join(meta, gate(got, sum_b), half_done)
    conv2_grad = assemble([one.join(sum2, got2, input_grad)], [every_tap])
    sum_a = one.join(sum_a, got_a, conv2_grad)
    sum_b = one.join(sum_b, got_b, sum_a)
    conv1_grad = assemble([sum_a, sum_b], [taps_a, taps_b])

    return (
        pooled,
        input_grad,
        conv1_grad,
        gain_one[0],
        bias_one[0],
        conv2_grad,
        gain_two[0],
        bias_two[0],
        head_grad.T,
        bias_grad[0],
        task_weights[0],
        average_next[0],
    )


def solution(mesh):
    in_specs = (
        P("batch", "task", None),
        P(None, "task", None),
        P("task"),
        P("task"),
        P(None, "task", None),
        P("task"),
        P("task"),
        P(None, "task"),
        P("task"),
        P("batch", "task"),
        P(),
        P(),
    )
    out_specs = (
        P("batch", "task"),
        P("batch", "task", None),
        P(None, "task", None),
        P("task"),
        P("task"),
        P(None, "task", None),
        P("task"),
        P("task"),
        P(None, "task"),
        P("task"),
        P(),
        P(),
    )
    return jax.shard_map(
        on_device, mesh=mesh, in_specs=in_specs, out_specs=out_specs, check_vma=False
    )
```
